128 devices in a mesh: rows: 8 (over x, core), cols: 16 (over y, z).
Axes of the slice: x: 4, y: 4, z: 4, core: 2. Of those that a mesh axis runs over, the one named last changes fastest.
Arguments:
- masks: bfloat16 [768, 384, 384], P(('rows', 'cols'))
- owned_counts: int32 [8, 16], replicated, may hold values from 1 to 6, 32 in all within a row
- cell_ids: int32 [16, 64], P(None, 'cols'), may hold values from 0 to 255, as said below
- kernels: float32 [2, 16, 32, 32], replicated, may hold values from -6 to 6
- kernel_weights: float32 [16], replicated, may hold values from 0.02 to 0.2
- dose: float32 [16, 64], P('rows', 'cols'), may hold values from 0.5 to 1.5
- threshold: float32 [1], replicated, may hold values from 0.3 to 0.6
Outputs:
- resist: bfloat16 [6144, 24576], P('rows', 'cols')
The draws below stay inside these ranges and needn't reach their ends.
Inputs may be any that keep to these rules, and one draw needn't show every extreme that they name: `owned_counts`: each row sums to 32, and some entry of each row equals 6. `cell_ids`: in the block of 2 x 4 instances of one device, at most 2 name cells of one mesh row (cells r * 32 to (r + 1) * 32 - 1), and every device reaches 2 for some row.
All inputs are finite; a program needn't handle non-finite values.
Results may differ from the reference program's by a relative error of at most 0.0034.
Values may be sent and summed in bfloat16 or wider, within the bound.
No kernel may reach another device: no remote copies, remote signals or barrier semaphores. Data moves between devices by JAX's collectives and lax.ppermute only.
A program may use at most 128 MiB of HBM per device.

```python
import math
import jax
import jax.numpy as jnp
import numpy as np
from jax import lax

TILE = 384
NF = 32
NK = 16
Q = 64
REACH = 8
TR = 2
TC = 4
CAPO = 6
ROWCELLS = 32
UNIQ = 256
LINK = 2
GR = 16
GC = 64
N_ROWS = 8
N_COLS = 16


def draw_masks(key, part):
    key = jax.random.fold_in(key, 11)
    slots = N_ROWS * N_COLS * CAPO
    rect_count = 192
    side_span = TILE // 8 + 1
    key_list = jax.random.split(key, 4)
    top_edge = jax.random.randint(key_list[0], (slots, rect_count), 0, TILE, dtype=jnp.int32)
    left_edge = jax.random.randint(key_list[1], (slots, rect_count), 0, TILE, dtype=jnp.int32)
    bottom_edge = jnp.minimum(top_edge + jax.random.randint(key_list[2], (slots, rect_count), 1, side_span, dtype=jnp.int32), TILE)
    right_edge = jnp.minimum(left_edge + jax.random.randint(key_list[3], (slots, rect_count), 1, side_span, dtype=jnp.int32), TILE)
    padded_side = TILE + 1
    slot_base = (jnp.arange(slots, dtype=jnp.int32) * (padded_side * padded_side))[:, None]
    corner_marks = jnp.zeros((slots * padded_side * padded_side,), jnp.int32)
    corner_marks = corner_marks.at[(slot_base + top_edge * padded_side + left_edge).reshape(-1)].add(1)
    corner_marks = corner_marks.at[(slot_base + top_edge * padded_side + right_edge).reshape(-1)].add(-1)
    corner_marks = corner_marks.at[(slot_base + bottom_edge * padded_side + left_edge).reshape(-1)].add(-1)
    corner_marks = corner_marks.at[(slot_base + bottom_edge * padded_side + right_edge).reshape(-1)].add(1)
    corner_grid = corner_marks.reshape(slots, padded_side, padded_side)
    coverage = jnp.cumsum(jnp.cumsum(corner_grid, axis=1), axis=2)[:, :TILE, :TILE]
    return (coverage > 0).astype(jnp.float32).astype(jnp.bfloat16)


def draw_cell_ids(key, part):
    key = jax.random.fold_in(key, 23)
    device_count = N_ROWS * N_COLS
    per_inst = TR * TC
    item_count = N_ROWS * LINK
    key_list = jax.random.split(key, 5)
    forced = jax.random.randint(key_list[0], (device_count, 1), 0, N_ROWS)
    item_iota = jnp.arange(item_count, dtype=jnp.int32)
    item_row = item_iota // LINK
    noise = jax.random.randint(key_list[1], (device_count, item_count), 0, 1 << 20)
    scores = noise * item_count + item_iota[None, :]
    scores = jnp.where(item_row[None, :] == forced, scores - (1 << 28), scores)
    order = jnp.argsort(scores, axis=1, stable=True)[:, :per_inst]
    rows_pick = order // LINK

    def shuffle_one(sub_key):
        return jax.random.permutation(sub_key, per_inst)
    shuffle = jax.vmap(shuffle_one)(jax.random.split(key_list[2], device_count))
    rows_pick = jnp.take_along_axis(rows_pick, shuffle, axis=1)
    first = jax.random.randint(key_list[3], (device_count, per_inst), 0, ROWCELLS)
    second = jax.random.randint(key_list[4], (device_count, per_inst), 0, ROWCELLS)
    cells = rows_pick * ROWCELLS + jnp.minimum(first, second)
    cells = cells.reshape(N_ROWS, N_COLS, TR, TC).transpose(0, 2, 1, 3).reshape(TR * N_ROWS, TC * N_COLS)
    return cells.astype(jnp.int32)


def length_profile(count, total, limit, slope):
    loads = [(1 << 20) // math.isqrt(rank ** slope) + 1 for rank in range(2, count + 1)]
    rest, holding = total - limit - (count - 1), [1] * (count - 1)
    while rest > 0:
        candidates = [i for i in range(count - 1) if holding[i] < limit]
        mass, budget = sum([loads[i] for i in candidates]), rest
        for i in candidates:
            addition = min(limit - holding[i], max(1, budget * loads[i] // mass), rest)
            holding[i] = holding[i] + addition
            rest = rest - addition
    return np.array([limit] + holding)


def uneven(rng, amount, total, most, skew):
    if amount == 2:
        one = jax.random.randint(rng, (), max(1, total - most), min(most, total - 1) + 1)
        return jnp.stack([one, total - one])
    tallies = jnp.asarray(length_profile(amount, total, most, skew), jnp.int32)
    pairs = (amount - 1) // 2
    source_of, sink = tallies[1:1 + 2 * pairs:2], tallies[2:2 + 2 * pairs:2]
    margin = jnp.minimum(source_of - 1, most - sink)
    shifted = jax.random.randint(jax.random.fold_in(rng, 1), (pairs,), 0, 1 << 20) % (margin + 1)
    tallies = tallies.at[1:1 + 2 * pairs:2].set(source_of - shifted).at[2:2 + 2 * pairs:2].set(sink + shifted)
    return tallies[jax.random.permutation(jax.random.fold_in(rng, 2), amount)]


def centred(own_key, shape, width, most, kind=jnp.bfloat16):
    values = width * jax.random.normal(own_key, shape, jnp.float32)
    return jnp.clip(values, min=-most, max=most).astype(kind)


def setup_inputs(seed: int = 0) -> dict:
    key_of = jax.random.split(jax.random.key(seed), 8)
    return {
        "masks": draw_masks(jax.random.fold_in(key_of[7], 71), 0),
        "owned_counts": jax.vmap(lambda own: uneven(own, N_COLS, ROWCELLS, CAPO, 2))(jax.random.split(key_of[1], N_ROWS)).reshape((N_ROWS, N_COLS)).astype(jnp.int32),
        "cell_ids": draw_cell_ids(jax.random.fold_in(key_of[7], 71), 0),
        "kernels": centred(key_of[3], (2, NK, NF, NF), 1.0, 6.0, jnp.float32),
        "kernel_weights": jnp.clip(jnp.exp(jax.random.uniform(key_of[4], (NK,), jnp.float32, math.log(0.02), math.log(0.2))), 0.02, 0.2),
        "dose": jnp.clip(1.0 + 0.1 * jax.random.normal(key_of[5], (GR, GC), jnp.float32), 0.5, 1.5),
        "threshold": jnp.clip(jax.random.uniform(key_of[6], (1,), jnp.float32, 0.3, 0.6), 0.3, 0.6),
    }


exact_mode = lax.Precision.HIGH
table_mode = lax.Precision.HIGHEST
steepness = 8.0


def tables(tile_px, nfreq, coarse_px):
    frequency = jnp.arange(nfreq, dtype=jnp.int32) - nfreq // 2
    pixels = jnp.arange(tile_px, dtype=jnp.int32)
    forward_turn = jnp.mod(frequency[:, None] * pixels[None, :], tile_px).astype(jnp.float32) * (2.0 * jnp.pi / tile_px)
    fwd_cos = jnp.cos(forward_turn) / tile_px
    fwd_sin = jnp.sin(forward_turn) / tile_px
    points = jnp.arange(coarse_px, dtype=jnp.int32)
    back_turn = jnp.mod(points[:, None] * frequency[None, :], coarse_px).astype(jnp.float32) * (2.0 * jnp.pi / coarse_px)
    inv_cos = jnp.cos(back_turn)
    inv_sin = jnp.sin(back_turn)
    harmonic = jnp.arange(coarse_px, dtype=jnp.int32) - coarse_px // 2
    fine_turn = jnp.mod(pixels[:, None] * harmonic[None, :], tile_px).astype(jnp.float32) * (2.0 * jnp.pi / tile_px)
    grid_turn = jnp.mod(points[:, None] * harmonic[None, :], coarse_px).astype(jnp.float32) * (2.0 * jnp.pi / coarse_px)
    interp = jnp.dot(jnp.cos(fine_turn), jnp.cos(grid_turn).T, precision=table_mode)
    interp = interp + jnp.dot(jnp.sin(fine_turn), jnp.sin(grid_turn).T, precision=table_mode)
    interp = (interp / coarse_px).astype(jnp.bfloat16)
    return fwd_cos, fwd_sin, inv_cos, inv_sin, interp


def slot_position(counts, local_cells, slot_count):
    ends = jnp.cumsum(counts, axis=-1)
    starts = ends - counts
    owner_col = jnp.sum((ends <= local_cells[..., None]).astype(jnp.int32), axis=-1)
    column_iota = jnp.arange(counts.shape[-1], dtype=jnp.int32)
    start_sel = jnp.sum(jnp.where(column_iota == owner_col[..., None], starts, 0), axis=-1)
    return owner_col * slot_count + (local_cells - start_sel)


def spectra(masks, fwd_cos, fwd_sin):
    field = masks.astype(jnp.float32)
    part_cos = jnp.einsum('at,sty->say', fwd_cos, field, precision=exact_mode)
    part_sin = -jnp.einsum('at,sty->say', fwd_sin, field, precision=exact_mode)
    spec_real = jnp.einsum('say,by->sab', part_cos, fwd_cos, precision=exact_mode) + jnp.einsum('say,by->sab', part_sin, fwd_sin, precision=exact_mode)
    spec_imag = jnp.einsum('say,by->sab', part_sin, fwd_cos, precision=exact_mode) - jnp.einsum('say,by->sab', part_cos, fwd_sin, precision=exact_mode)
    return spec_real, spec_imag


def coherent_power(spec_real, spec_imag, kernels, kernel_weights, inv_cos, inv_sin):
    ker_real = kernels[0][None]
    ker_imag = kernels[1][None]
    prod_real = ker_real * spec_real[:, None] - ker_imag * spec_imag[:, None]
    prod_imag = ker_real * spec_imag[:, None] + ker_imag * spec_real[:, None]
    half_real = jnp.einsum('pa,skab->skpb', inv_cos, prod_real, precision=exact_mode) - jnp.einsum('pa,skab->skpb', inv_sin, prod_imag, precision=exact_mode)
    half_imag = jnp.einsum('pa,skab->skpb', inv_cos, prod_imag, precision=exact_mode) + jnp.einsum('pa,skab->skpb', inv_sin, prod_real, precision=exact_mode)
    field_real = jnp.einsum('skpb,qb->skpq', half_real, inv_cos, precision=exact_mode) - jnp.einsum('skpb,qb->skpq', half_imag, inv_sin, precision=exact_mode)
    field_imag = jnp.einsum('skpb,qb->skpq', half_real, inv_sin, precision=exact_mode) + jnp.einsum('skpb,qb->skpq', half_imag, inv_cos, precision=exact_mode)
    intensity = field_real * field_real + field_imag * field_imag
    return jnp.einsum('k,skpq->spq', kernel_weights, intensity, precision=table_mode)


def blur_taps(reach):
    offsets = (jnp.arange(2 * reach + 1, dtype=jnp.int32) - reach).astype(jnp.float32)
    weights = jnp.exp(-offsets * offsets / 32.0)
    return weights / jnp.sum(weights)


def smooth(field, weights, axis):
    span = weights.shape[0]
    length = field.shape[axis] - span + 1
    total = weights[0] * lax.slice_in_dim(field, 0, length, axis=axis)
    for offset in range(1, span):
        total = total + weights[offset] * lax.slice_in_dim(field, offset, offset + length, axis=axis)
    return total


def reference(masks, owned_counts, cell_ids, kernels, kernel_weights, dose, threshold):
    fwd_cos, fwd_sin, inv_cos, inv_sin, interp = tables(TILE, NF, Q)
    cells = jnp.arange(UNIQ, dtype=jnp.int32)
    owner_row = cells // ROWCELLS
    local_cells = cells - owner_row * ROWCELLS
    row_counts = jnp.take(owned_counts, owner_row, axis=0)
    mask_index = owner_row * (N_COLS * CAPO) + slot_position(row_counts, local_cells, CAPO)
    cell_mask = jnp.take(masks, mask_index.astype(jnp.int32), axis=0)
    spec_real, spec_imag = spectra(cell_mask, fwd_cos, fwd_sin)
    coarse = coherent_power(spec_real, spec_imag, kernels, kernel_weights, inv_cos, inv_sin).astype(jnp.bfloat16)
    interp_wide = interp.astype(jnp.float32)

    def strip(inputs):
        row_ids, row_dose = inputs
        tiles = jnp.take(coarse, row_ids, axis=0).astype(jnp.float32)
        half = jnp.einsum('ipq,xq->ipx', tiles, interp_wide)
        half = lax.optimization_barrier(half.astype(jnp.bfloat16)).astype(jnp.float32)
        aerial = jnp.einsum('yp,ipx->iyx', interp_wide, half) * row_dose[:, None, None]
        return aerial.transpose(1, 0, 2).reshape(TILE, GC * TILE)

    strips = lax.map(strip, (cell_ids, dose))
    plane = strips.reshape(GR * TILE, GC * TILE)
    weights = blur_taps(REACH)
    padded = jnp.pad(plane, ((REACH, REACH), (0, 0)))
    along_rows = smooth(padded, weights, 0)
    padded = jnp.pad(along_rows, ((0, 0), (REACH, REACH)))
    blurred = smooth(padded, weights, 1)
    return jax.nn.sigmoid(steepness * (blurred - threshold[0])).astype(jnp.bfloat16)
```

```python
import functools

import jax
import jax.numpy as jnp
import ml_dtypes
import numpy as np
from jax import lax
from jax.experimental import pallas as pl
from jax.experimental.pallas import tpu as pltpu
from jax.sharding import PartitionSpec as P

REACH = 8
TILE = 384
NF = 32
NK = 16
Q = 64
SLOTS = 6
ROWS = 8
COLS = 16
CELLS = 32
LANES = 128
INFO = 3 * Q
PACKET = INFO + 16
OUTGOING = 2 * Q + 16
GROUPS = NK // 4
BF16 = jnp.bfloat16
F32 = jnp.float32


def split(table):
    high = table.astype(ml_dtypes.bfloat16)
    low = (table - high.astype(np.float64)).astype(ml_dtypes.bfloat16)
    return high, low


@functools.lru_cache(maxsize=None)
def tables():
    freq = np.arange(NF) - NF // 2
    pixels = np.arange(TILE)
    points = np.arange(Q)
    turn = np.mod(freq[:, None] * pixels[None, :], TILE) * (2.0 * np.pi / TILE)
    forward = np.concatenate([np.cos(turn), np.sin(turn)]) / TILE
    high, low = split(forward)
    forward_rows = np.concatenate([high, low])
    forward_cols = np.ascontiguousarray(forward_rows.T)

    turn = np.mod(points[:, None] * freq[None, :], Q) * (2.0 * np.pi / Q)
    cos, sin = np.cos(turn), np.sin(turn)
    left = np.block([[cos, -sin], [sin, cos]])
    high, low = split(left)
    inverse_left = np.concatenate([high, high, low], axis=1)
    right = np.zeros((2 * LANES, 4 * LANES))
    for k in range(4):
        re = slice(k * NF, (k + 1) * NF)
        im = slice(LANES + k * NF, LANES + (k + 1) * NF)
        out_re = slice(k * LANES, k * LANES + Q)
        out_im = slice(k * LANES + Q, (k + 1) * LANES)
        right[re, out_re], right[re, out_im] = cos.T, sin.T
        right[im, out_re], right[im, out_im] = -sin.T, cos.T
    inverse_right = np.stack(split(right))

    harmonic = np.arange(Q) - Q // 2
    fine = np.mod(pixels[:, None] * harmonic[None, :], TILE) * (2.0 * np.pi / TILE)
    grid = np.mod(points[:, None] * harmonic[None, :], Q) * (2.0 * np.pi / Q)
    interp = (np.cos(fine) @ np.cos(grid).T + np.sin(fine) @ np.sin(grid).T) / Q
    interp16 = interp.astype(ml_dtypes.bfloat16)
    interp = interp16.astype(np.float64)

    offsets = np.arange(2 * REACH + 1) - REACH
    taps = np.exp(-offsets * offsets / 32.0)
    taps = taps / taps.sum()

    def blur(out_pixels, in_pixels):
        gap = out_pixels[:, None] - in_pixels[None, :]
        inside = np.abs(gap) <= REACH
        return np.where(inside, taps[np.clip(gap + REACH, 0, 2 * REACH)], 0.0)

    edge = np.concatenate([interp16[TILE - REACH :], interp16[:REACH]])
    edge_pad = np.zeros((2, 16, LANES), ml_dtypes.bfloat16)
    edge_pad[0, :, :Q] = edge
    edge_pad[1, :, Q:] = edge

    reach_cols = np.concatenate(
        [np.arange(TILE), np.arange(-LANES, 0), np.arange(TILE, TILE + LANES)]
    )
    spread = (blur(reach_cols, pixels) @ interp).T
    across = np.zeros((2, LANES, 5 * LANES))
    across[0, :Q] = spread
    across[1, Q:] = spread
    across = across.astype(ml_dtypes.bfloat16)

    out_rows = np.arange(2 * TILE)
    down = np.concatenate(
        [
            blur(out_rows, pixels) @ interp,
            blur(out_rows, pixels + TILE) @ interp,
            blur(out_rows, np.arange(-REACH, 0)),
            blur(out_rows, np.arange(2 * TILE, 2 * TILE + REACH)),
        ],
        axis=1,
    )
    down = np.stack(split(4.0 * down))

    lane = np.arange(LANES)
    side = np.concatenate(
        [
            blur(lane, np.arange(-REACH, 0)).T,
            blur(lane, np.arange(LANES, LANES + REACH)).T,
        ]
    ).astype(ml_dtypes.bfloat16)
    return dict(
        forward_rows=forward_rows,
        forward_cols=forward_cols,
        inverse_left=inverse_left,
        inverse_right=inverse_right,
        edge=edge,
        edge_pad=edge_pad,
        across=across,
        down=down,
        side=side,
    )


def dot(a, b):
    return jnp.dot(a, b, preferred_element_type=F32)


def halves(x):
    high = x.astype(BF16)
    return high, (x - high.astype(F32)).astype(BF16)


def lanes_of(shape):
    return lax.broadcasted_iota(jnp.int32, shape, 1)


def imaging_kernel(
    mask, kernels, weights, ids, dose, fwd_cols, fwd_rows, inv_left, inv_right, out, ker, info
):
    step = pl.program_id(0)

    @pl.when(step == 0)
    def _():
        for part in range(2):
            for group in range(GROUPS):
                four = [
                    kernels[part, 4 * group + i]
                    * jnp.sqrt(jnp.full((NF, NF), weights[4 * group + i], F32))
                    for i in range(4)
                ]
                ker[part, group] = jnp.concatenate(four, axis=1)
        info[...] = jnp.zeros_like(info)
        info[:, 0:4] = ids[...].astype(F32)
        first = dose[...].astype(BF16).astype(F32)
        second = (dose[...] - first).astype(BF16).astype(F32)
        info[0:2, 4:8] = first
        info[0:2, 8:12] = second
        info[0:2, 12:16] = dose[...] - first - second
        packed = info[...].astype(BF16)
        for c in range(COLS):
            out[c, INFO : INFO + 16, :] = packed

    lane = lanes_of((NF, LANES))
    even = (lane // NF) % 2 == 0
    images = []
    for slot in range(2):
        cols = dot(mask[slot], fwd_cols[...])
        cols = cols + pltpu.roll(cols, Q, 1)
        high, low = halves(cols)
        pair = jnp.where(lanes_of((TILE, LANES)) < Q, high.astype(F32), low.astype(F32))
        both = dot(fwd_rows[...], pair.astype(BF16))
        both = both[:Q] + both[Q:]
        both = both + pltpu.roll(both, Q, 1)
        top, bottom = both[:NF], both[NF:]
        real = top - pltpu.roll(bottom, NF, 1)
        imag = -(bottom + pltpu.roll(top, NF, 1))
        real = jnp.where(even, real, pltpu.roll(real, NF, 1))
        imag = jnp.where(even, imag, pltpu.roll(imag, NF, 1))
        highs, lows = [], []
        for group in range(GROUPS):
            kr, ki = ker[0, group], ker[1, group]
            prod = jnp.concatenate([kr * real - ki * imag, kr * imag + ki * real], axis=0)
            high, low = halves(prod)
            highs.append(high)
            lows.append(low)
        high = jnp.concatenate(highs, axis=1)
        low = jnp.concatenate(lows, axis=1)
        half = dot(inv_left[...], jnp.concatenate([high, low, high], axis=0))
        blocks = []
        for group in range(GROUPS):
            g = slice(group * LANES, (group + 1) * LANES)
            blocks.append(jnp.concatenate([half[:Q, g], half[Q:, g]], axis=1))
        high, low = halves(jnp.concatenate(blocks, axis=0))
        field = dot(high, inv_right[0]) + (dot(high, inv_right[1]) + dot(low, inv_right[0]))
        power = field * field
        total = None
        for group in range(GROUPS):
            for k in range(4):
                part = power[group * Q : (group + 1) * Q, k * LANES : (k + 1) * LANES]
                total = part if total is None else total + part
        images.append(total + pltpu.roll(total, Q, 1))
    tile = jnp.where(lanes_of((Q, LANES)) < Q, images[0], images[1]).astype(BF16)
    at = pl.multiple_of(step * Q, Q)
    for c in range(COLS):
        out[c, pl.ds(at, Q), :] = tile


def routing_kernel(
    packets, counts, edge, edge_pad, out, strips, where_v, where_s, cell_slot, sem
):
    row, col = lax.axis_index("rows"), lax.axis_index("cols")
    before = packets[jnp.maximum(col - 1, 0), INFO : INFO + 16, :].astype(F32)
    here = packets[col, INFO : INFO + 16, :].astype(F32)
    after = packets[jnp.minimum(col + 1, COLS - 1), INFO : INFO + 16, :].astype(F32)
    lane = lanes_of((16, LANES))

    window = jnp.where(
        lane == 0,
        pltpu.roll(before, LANES - 3, 1),
        jnp.where(lane < 5, pltpu.roll(here, 1, 1), pltpu.roll(after, 5, 1)),
    ).astype(jnp.int32)
    cell = window - row * CELLS
    exists = ((lane > 0) | (col > 0)) & ((lane < 5) | (col < COLS - 1)) & (lane < 6)
    mine = (cell >= 0) & (cell < CELLS) & exists
    where_v[...] = jnp.where(mine, cell, -1)
    copy = pltpu.make_async_copy(where_v, where_s, sem)
    copy.start()

    start = jnp.int32(0)
    for c in range(COLS):
        for s in range(SLOTS):
            cell_slot[start + s] = jnp.int32(c * 8 + s)
        start = start + counts[row, c]

    left = lane < Q
    for cell_index in range(CELLS):
        place = cell_slot[cell_index]
        odd = place & 1
        at = pl.multiple_of(((place >> 1) & 3) * Q, Q)
        pair = packets[place >> 3, pl.ds(at, Q), :]
        along = dot(edge[...], pair)
        strips[cell_index, 0:16, :] = jnp.where(left == (odd == 0), along, pltpu.roll(along, Q, 1))
        strips[cell_index, 16:32, :] = lax.dot_general(
            edge_pad[odd],
            jnp.concatenate([pair, pair], axis=0),
            (((1,), (1,)), ((), ())),
            preferred_element_type=F32,
        )
    copy.wait()

    left8 = lanes_of((REACH, LANES)) < Q

    def strip(index, kind):
        value = strips[jnp.maximum(index, 0), kind * REACH : (kind + 1) * REACH, :]
        return jnp.where(index >= 0, value, 0.0)

    def two(first, second, kind):
        return jnp.where(left8, strip(first, kind), strip(second, kind))

    none = jnp.int32(-1)
    info = jnp.where(
        lane < 16,
        before,
        jnp.where(lane < 32, pltpu.roll(here, 16, 1), pltpu.roll(after, 32, 1)),
    ).astype(BF16)
    left64 = lanes_of((Q, LANES)) < Q
    for dest in range(ROWS):
        first, second = none, none
        for i in range(2):
            for j in range(4):
                here_cell = where_s[2 * dest + i, 1 + j]
                held = here_cell >= 0
                second = jnp.where(held & (first >= 0) & (second < 0), here_cell, second)
                first = jnp.where(held & (first < 0), here_cell, first)
        tiles = []
        for index in (first, second):
            place = cell_slot[jnp.maximum(index, 0)]
            at = pl.multiple_of(((place >> 1) & 3) * Q, Q)
            pair = packets[place >> 3, pl.ds(at, Q), :].astype(F32)
            pair = jnp.where(left64 == ((place & 1) == 0), pair, pltpu.roll(pair, Q, 1))
            tiles.append(jnp.where(index >= 0, pair, 0.0))
        out[dest, 0:Q, :] = jnp.where(left64, tiles[0], tiles[1]).astype(BF16)

        def index(i, j):
            inside = 0 <= i < 2 * ROWS
            return where_s[i, j] if inside else none

        up, low = 2 * dest - 1, 2 * dest + 2
        blocks = [two(index(up, j), index(up, j + 1), 0) for j in (0, 2, 4)]
        blocks += [two(index(low, j), index(low, j + 1), 1) for j in (0, 2, 4)]
        blocks.append(two(index(2 * dest, 0), index(2 * dest + 1, 0), 2))
        blocks.append(two(index(2 * dest, 5), index(2 * dest + 1, 5), 3))
        for i in range(4):
            both = jnp.concatenate([blocks[2 * i], blocks[2 * i + 1]], axis=0)
            out[dest, Q + 16 * i : Q + 16 * (i + 1), :] = both.astype(BF16)
        out[dest, 2 * Q : 2 * Q + 16, :] = info


def develop_kernel(tiles, ids, dose, threshold, across, side, down, out, wide, narrow):
    step = pl.program_id(0)
    row = lax.axis_index("rows")

    @pl.when(step == 0)
    def _():
        wide[...] = jnp.zeros_like(wide)

        def add(rows, value, j):
            if 0 <= j < 4:
                wide[rows, j * TILE : (j + 1) * TILE] += value[:, :TILE]
            if j >= 1:
                wide[rows, j * TILE - LANES : j * TILE] += value[:, TILE : TILE + LANES]
            if j <= 2:
                wide[rows, (j + 1) * TILE : (j + 1) * TILE + LANES] += value[:, TILE + LANES :]

        sources = [[ids[2 * row + i, j] // CELLS for j in range(4)] for i in range(2)]
        flat = sources[0] + sources[1]
        for i in range(2):
            for j in range(4):
                n = 4 * i + j
                rank = jnp.int32(0)
                for m in range(n):
                    rank = rank + (flat[m] == flat[n]).astype(jnp.int32)
                rank = jnp.minimum(rank, 1)
                value = dot(tiles[flat[n], 0:Q, :], across[rank]) * dose[i, j]
                add(slice(i * Q, (i + 1) * Q), value, j)

        strips = tiles[0, Q : 2 * Q, :].astype(F32)
        for source in range(1, ROWS):
            strips = strips + tiles[source, Q : 2 * Q, :].astype(F32)

        def doses(source):
            info = tiles[source, 2 * Q : 2 * Q + 16, :].astype(F32)
            return info + pltpu.roll(info, LANES - 4, 1) + pltpu.roll(info, LANES - 8, 1)

        own = doses(row)
        above = doses(jnp.maximum(row - 1, 0))
        below = doses(jnp.minimum(row + 1, ROWS - 1))
        lane_of = [7] + [20 + j for j in range(4)] + [36]
        for j in range(-1, 5):
            block, half = (j + 1) // 2, (j + 1) % 2
            upper = strips[block * 8 : (block + 1) * 8]
            lower = strips[24 + block * 8 : 24 + (block + 1) * 8]
            both = jnp.concatenate([upper, lower], axis=0).astype(BF16)
            value = dot(both, across[half])
            at = lane_of[j + 1]
            top = jnp.broadcast_to(above[1:2, at : at + 1], (REACH, 5 * LANES))
            bottom = jnp.broadcast_to(below[0:1, at : at + 1], (REACH, 5 * LANES))
            add(slice(2 * Q, 2 * Q + 16), value * jnp.concatenate([top, bottom], axis=0), j)

        sides = strips[48:64]
        for end in range(2):
            pixels = jnp.transpose(sides[8 * end : 8 * end + 8]).astype(BF16)
            at = lane_of[0] if end == 0 else lane_of[5]
            value = dot(pixels, side[8 * end : 8 * end + 8, :])
            scale = jnp.concatenate(
                [jnp.broadcast_to(own[i : i + 1, at : at + 1], (Q, LANES)) for i in range(2)],
                axis=0,
            )
            cols = slice(0, LANES) if end == 0 else slice(4 * TILE - LANES, 4 * TILE)
            wide[0 : 2 * Q, cols] += value * scale
        narrow[...] = wide[...].astype(BF16)

    columns = narrow[:, pl.ds(pl.multiple_of(step * TILE, TILE), TILE)]
    level = dot(down[0], columns) + dot(down[1], columns)
    out[...] = (0.5 * jnp.tanh(level - 4.0 * threshold[0]) + 0.5).astype(BF16)


def whole(array):
    return pl.BlockSpec(array.shape, lambda *_: (0,) * array.ndim)


def scalars():
    return pl.BlockSpec(memory_space=pltpu.SMEM)


PARAMS = pltpu.CompilerParams(vmem_limit_bytes=48 * 1024 * 1024)


def local(masks, owned_counts, cell_ids, kernels, kernel_weights, dose, threshold):
    table = {name: jnp.asarray(value) for name, value in tables().items()}

    constants = [
        table[n] for n in ("forward_cols", "forward_rows", "inverse_left", "inverse_right")
    ]
    packet = pl.pallas_call(
        imaging_kernel,
        grid=(SLOTS // 2,),
        out_shape=jax.ShapeDtypeStruct((COLS, PACKET, LANES), BF16),
        in_specs=[
            pl.BlockSpec((2, TILE, TILE), lambda s: (s, 0, 0)),
            whole(kernels),
            scalars(),
            whole(cell_ids),
            whole(dose),
            *[whole(t) for t in constants],
        ],
        out_specs=pl.BlockSpec((COLS, PACKET, LANES), lambda s: (0, 0, 0)),
        scratch_shapes=[
            pltpu.VMEM((2, GROUPS, NF, LANES), F32),
            pltpu.VMEM((16, LANES), F32),
        ],
        compiler_params=PARAMS,
    )(masks, kernels, kernel_weights, cell_ids, dose, *constants)

    packets = lax.all_to_all(packet, "cols", split_axis=0, concat_axis=0, tiled=True)

    outgoing = pl.pallas_call(
        routing_kernel,
        out_shape=jax.ShapeDtypeStruct((ROWS, OUTGOING, LANES), BF16),
        in_specs=[
            pl.BlockSpec(memory_space=pltpu.VMEM),
            scalars(),
            pl.BlockSpec(memory_space=pltpu.VMEM),
            pl.BlockSpec(memory_space=pltpu.VMEM),
        ],
        out_specs=pl.BlockSpec(memory_space=pltpu.VMEM),
        scratch_shapes=[
            pltpu.VMEM((CELLS, 32, LANES), F32),
            pltpu.VMEM((16, LANES), jnp.int32),
            pltpu.SMEM((16, LANES), jnp.int32),
            pltpu.SMEM((CELLS + SLOTS,), jnp.int32),
            pltpu.SemaphoreType.DMA,
        ],
        compiler_params=PARAMS,
    )(packets, owned_counts, table["edge"], table["edge_pad"])

    incoming = lax.all_to_all(outgoing, "rows", split_axis=0, concat_axis=0, tiled=True)

    constants = [table[n] for n in ("across", "side", "down")]
    return pl.pallas_call(
        develop_kernel,
        grid=(4,),
        out_shape=jax.ShapeDtypeStruct((2 * TILE, 4 * TILE), BF16),
        in_specs=[
            whole(incoming),
            scalars(),
            scalars(),
            scalars(),
            *[whole(t) for t in constants],
        ],
        out_specs=pl.BlockSpec((2 * TILE, TILE), lambda s: (0, s)),
        scratch_shapes=[
            pltpu.VMEM((OUTGOING, 4 * TILE), F32),
            pltpu.VMEM((OUTGOING, 4 * TILE), BF16),
        ],
        compiler_params=PARAMS,
    )(incoming, cell_ids, dose, threshold, *constants)


def solution(mesh):
    return jax.shard_map(
        local,
        mesh=mesh,
        in_specs=(
            P(("rows", "cols"), None, None),
            P(),
            P(None, "cols"),
            P(),
            P(),
            P("rows", "cols"),
            P(),
        ),
        out_specs=P("rows", "cols"),
        check_vma=False,
    )
```

```python
import functools

import jax
import jax.numpy as jnp
import ml_dtypes
import numpy as np
from jax import lax
from jax.experimental import pallas as pl
from jax.experimental.pallas import tpu as pltpu
from jax.sharding import PartitionSpec as P

REACH = 8
TILE = 384
NF = 32
NK = 16
Q = 64
SLOTS = 6
ROWS = 8
COLS = 16
CELLS = 32
LANES = 128
INFO = 3 * Q
PACKET = INFO + 16
OUTGOING = 2 * Q + 16
BF16 = jnp.bfloat16
F32 = jnp.float32


def split(table):
    high = table.astype(ml_dtypes.bfloat16)
    low = (table - high.astype(np.float64)).astype(ml_dtypes.bfloat16)
    return high, low


@functools.lru_cache(maxsize=None)
def tables():
    freq = np.arange(NF) - NF // 2
    pixels = np.arange(TILE)
    points = np.arange(Q)
    turn = np.mod(freq[:, None] * pixels[None, :], TILE) * (2.0 * np.pi / TILE)
    forward = np.concatenate([np.cos(turn), np.sin(turn)]) / TILE
    high, low = split(forward)
    forward_rows = np.concatenate([high, low])
    forward_cols = np.ascontiguousarray(forward_rows.T)

    turn = np.mod(points[:, None] * freq[None, :], Q) * (2.0 * np.pi / Q)
    cos, sin = np.cos(turn), np.sin(turn)
    high, low = split(np.concatenate([cos, -sin], axis=1))
    inverse_left = np.concatenate([high, high, low], axis=1)
    right = np.zeros((LANES, 2 * LANES))
    for k in range(2):
        re = slice(2 * k * NF, (2 * k + 1) * NF)
        im = slice((2 * k + 1) * NF, (2 * k + 2) * NF)
        out_re = slice(k * LANES, k * LANES + Q)
        out_im = slice(k * LANES + Q, (k + 1) * LANES)
        right[re, out_re], right[re, out_im] = cos.T, sin.T
        right[im, out_re], right[im, out_im] = -sin.T, cos.T
    high, low = split(right)
    inverse_right = np.concatenate([high, high, low])

    harmonic = np.arange(Q) - Q // 2
    fine = np.mod(pixels[:, None] * harmonic[None, :], TILE) * (2.0 * np.pi / TILE)
    grid = np.mod(points[:, None] * harmonic[None, :], Q) * (2.0 * np.pi / Q)
    interp = (np.cos(fine) @ np.cos(grid).T + np.sin(fine) @ np.sin(grid).T) / Q
    interp16 = interp.astype(ml_dtypes.bfloat16)
    interp = interp16.astype(np.float64)

    offsets = np.arange(2 * REACH + 1) - REACH
    taps = np.exp(-offsets * offsets / 32.0)
    taps = taps / taps.sum()

    def blur(out_pixels, in_pixels):
        gap = out_pixels[:, None] - in_pixels[None, :]
        inside = np.abs(gap) <= REACH
        return np.where(inside, taps[np.clip(gap + REACH, 0, 2 * REACH)], 0.0)

    edge = np.concatenate([interp16[TILE - REACH :], interp16[:REACH]])
    edge_pad = np.zeros((2, 16, LANES), ml_dtypes.bfloat16)
    edge_pad[0, :, :Q] = edge
    edge_pad[1, :, Q:] = edge

    reach_cols = np.concatenate(
        [np.arange(TILE), np.arange(-LANES, 0), np.arange(TILE, TILE + LANES)]
    )
    spread = (blur(reach_cols, pixels) @ interp).T
    across = np.zeros((2, LANES, 5 * LANES))
    across[0, :Q] = spread
    across[1, Q:] = spread
    across = across.astype(ml_dtypes.bfloat16)

    out_rows = np.arange(2 * TILE)
    down = np.concatenate(
        [
            blur(out_rows, pixels) @ interp,
            blur(out_rows, pixels + TILE) @ interp,
            blur(out_rows, np.arange(-REACH, 0)),
            blur(out_rows, np.arange(2 * TILE, 2 * TILE + REACH)),
        ],
        axis=1,
    )
    down = np.stack(split(4.0 * down))

    lane = np.arange(LANES)
    side = np.concatenate(
        [
            blur(lane, np.arange(-REACH, 0)).T,
            blur(lane, np.arange(LANES, LANES + REACH)).T,
        ]
    ).astype(ml_dtypes.bfloat16)
    return dict(
        forward_rows=forward_rows,
        forward_cols=forward_cols,
        inverse_left=inverse_left,
        inverse_right=inverse_right,
        edge=edge,
        edge_pad=edge_pad,
        across=across,
        down=down,
        side=side,
    )


def dot(a, b):
    return jnp.dot(a, b, preferred_element_type=F32)


def halves(x):
    high = x.astype(BF16)
    return high, (x - high.astype(F32)).astype(BF16)


def lanes_of(shape):
    return lax.broadcasted_iota(jnp.int32, shape, 1)


def imaging_kernel(
    mask, kernels, weights, ids, dose, fwd_cols, fwd_rows, inv_left, inv_right,
    out,
    mask_v, kernels_v, weights_s, ids_v, dose_v, cols_v, rows_v, left_v, right_v,
    ker, info, sems,
):
    moves = [(kernels, kernels_v), (weights, weights_s), (fwd_cols, cols_v)]
    moves += [(mask.at[s], mask_v.at[s]) for s in range(SLOTS)]
    moves += [(fwd_rows, rows_v), (inv_left, left_v), (inv_right, right_v)]
    moves += [(ids, ids_v), (dose, dose_v)]
    copies = [
        pltpu.make_async_copy(src, dst, sems.at[i]) for i, (src, dst) in enumerate(moves)
    ]
    for copy in copies:
        copy.start()
    copies[0].wait()
    copies[1].wait()
    for two in range(NK // 2):
        re, im = [], []
        for k in (2 * two, 2 * two + 1):
            scale = jnp.sqrt(jnp.full((NF, NF), weights_s[k], F32))
            re.append(kernels_v[0, k] * scale)
            im.append(kernels_v[1, k] * scale)
        ker[0, two] = jnp.concatenate([re[0], im[0], re[1], im[1]], axis=1)
        ker[1, two] = jnp.concatenate([-im[0], re[0], -im[1], re[1]], axis=1)
    for copy in copies[2:]:
        copy.wait()

    info[...] = jnp.zeros_like(info)
    info[0:4, 0:16] = ids_v[...].astype(F32)
    first = dose_v[...].astype(BF16).astype(F32)
    second = (dose_v[...] - first).astype(BF16).astype(F32)
    info[8:10, 4:8] = first
    info[8:10, 8:12] = second
    info[8:10, 12:16] = dose_v[...] - first - second
    packed = info[...].astype(BF16)
    for c in range(COLS):
        out[c, INFO : INFO + 16, :] = packed

    even = (lanes_of((NF, LANES)) // NF) % 2 == 0
    left = lanes_of((TILE, LANES)) < Q
    images = []
    for slot in range(SLOTS):
        cols = dot(mask_v[slot], cols_v[...])
        cols = cols + pltpu.roll(cols, Q, 1)
        high = cols.astype(BF16).astype(F32)
        pair = jnp.where(left, high, cols - high).astype(BF16)
        both = dot(rows_v[...], pair)
        both = both[:Q] + both[Q:]
        both = both + pltpu.roll(both, Q, 1)
        top, bottom = both[:NF], both[NF:]
        real = top - pltpu.roll(bottom, NF, 1)
        imag = -(bottom + pltpu.roll(top, NF, 1))
        real = jnp.where(even, real, pltpu.roll(real, NF, 1))
        imag = jnp.where(even, imag, pltpu.roll(imag, NF, 1))
        highs, lows = [], []
        for two in range(NK // 2):
            ka, kb = ker[0, two], ker[1, two]
            prod = jnp.concatenate([ka * real + kb * imag, ka * imag - kb * real], axis=0)
            high, low = halves(prod)
            highs.append(high)
            lows.append(low)
        high = jnp.concatenate(highs, axis=1)
        low = jnp.concatenate(lows, axis=1)
        half = dot(left_v[...], jnp.concatenate([high, low, high], axis=0))
        rows = jnp.concatenate(
            [half[:, i * LANES : (i + 1) * LANES] for i in range(NK // 2)], axis=0
        )
        high, low = halves(rows)
        field = dot(jnp.concatenate([high, low, high], axis=1), right_v[...])
        power = field * field
        power = power[:, :LANES] + power[:, LANES:]
        total = power[:Q]
        for i in range(1, NK // 2):
            total = total + power[i * Q : (i + 1) * Q]
        images.append(total + pltpu.roll(total, Q, 1))
    left = lanes_of((Q, LANES)) < Q
    for i in range(SLOTS // 2):
        tile = jnp.where(left, images[2 * i], images[2 * i + 1]).astype(BF16)
        for c in range(COLS):
            out[c, i * Q : (i + 1) * Q, :] = tile


def routing_kernel(
    packets, counts, edge, edge_pad, out, strips, where_v, where_s, cell_slot, sem
):
    row, col = lax.axis_index("rows"), lax.axis_index("cols")
    before = packets[jnp.maximum(col - 1, 0), INFO : INFO + 16, :].astype(F32)
    here = packets[col, INFO : INFO + 16, :].astype(F32)
    after = packets[jnp.minimum(col + 1, COLS - 1), INFO : INFO + 16, :].astype(F32)
    lane = lanes_of((16, LANES))

    line = lax.broadcasted_iota(jnp.int32, (16, LANES), 0)
    window = jnp.where(
        line == 0,
        pltpu.roll(before, 13, 0),
        jnp.where(line < 5, pltpu.roll(here, 1, 0), pltpu.roll(after, 5, 0)),
    ).astype(jnp.int32)
    cell = window - row * CELLS
    exists = ((line > 0) | (col > 0)) & ((line < 5) | (col < COLS - 1)) & (line < 6)
    mine = (cell >= 0) & (cell < CELLS) & exists
    where_v[...] = jnp.where(mine, cell, -1)
    copy = pltpu.make_async_copy(where_v, where_s, sem)
    copy.start()

    start = jnp.int32(0)
    for c in range(COLS):
        for s in range(SLOTS):
            cell_slot[start + s] = jnp.int32(c * 8 + s)
        start = start + counts[row, c]

    left = lane < Q
    for cell_index in range(CELLS):
        place = cell_slot[cell_index]
        odd = place & 1
        at = pl.multiple_of(((place >> 1) & 3) * Q, Q)
        pair = packets[place >> 3, pl.ds(at, Q), :]
        along = dot(edge[...], pair)
        strips[cell_index, 0:16, :] = jnp.where(left == (odd == 0), along, pltpu.roll(along, Q, 1))
        strips[cell_index, 16:32, :] = lax.dot_general(
            edge_pad[odd],
            jnp.concatenate([pair, pair], axis=0),
            (((1,), (1,)), ((), ())),
            preferred_element_type=F32,
        )
    copy.wait()

    left8 = lanes_of((REACH, LANES)) < Q

    def strip(index, kind):
        value = strips[jnp.maximum(index, 0), kind * REACH : (kind + 1) * REACH, :]
        return jnp.where(index >= 0, value, 0.0)

    def two(first, second, kind):
        return jnp.where(left8, strip(first, kind), strip(second, kind))

    none = jnp.int32(-1)
    info = jnp.where(
        lane < 16,
        before,
        jnp.where(lane < 32, pltpu.roll(here, 16, 1), pltpu.roll(after, 32, 1)),
    ).astype(BF16)
    left64 = lanes_of((Q, LANES)) < Q
    for dest in range(ROWS):
        first, second = none, none
        for i in range(2):
            for j in range(4):
                here_cell = where_s[1 + j, 2 * dest + i]
                held = here_cell >= 0
                second = jnp.where(held & (first >= 0) & (second < 0), here_cell, second)
                first = jnp.where(held & (first < 0), here_cell, first)
        tiles = []
        for index in (first, second):
            place = cell_slot[jnp.maximum(index, 0)]
            at = pl.multiple_of(((place >> 1) & 3) * Q, Q)
            pair = packets[place >> 3, pl.ds(at, Q), :].astype(F32)
            pair = jnp.where(left64 == ((place & 1) == 0), pair, pltpu.roll(pair, Q, 1))
            tiles.append(jnp.where(index >= 0, pair, 0.0))
        out[dest, 0:Q, :] = jnp.where(left64, tiles[0], tiles[1]).astype(BF16)

        def index(i, j):
            inside = 0 <= i < 2 * ROWS
            return where_s[j, i] if inside else none

        up, low = 2 * dest - 1, 2 * dest + 2
        blocks = [two(index(up, j), index(up, j + 1), 0) for j in (0, 2, 4)]
        blocks += [two(index(low, j), index(low, j + 1), 1) for j in (0, 2, 4)]
        blocks.append(two(index(2 * dest, 0), index(2 * dest + 1, 0), 2))
        blocks.append(two(index(2 * dest, 5), index(2 * dest + 1, 5), 3))
        for i in range(4):
            both = jnp.concatenate([blocks[2 * i], blocks[2 * i + 1]], axis=0)
            out[dest, Q + 16 * i : Q + 16 * (i + 1), :] = both.astype(BF16)
        out[dest, 2 * Q : 2 * Q + 16, :] = info


def develop_kernel(tiles, ids, dose, threshold, across, side, down, out, wide, narrow):
    step = pl.program_id(0)
    row = lax.axis_index("rows")

    @pl.when(step == 0)
    def _():
        wide[...] = jnp.zeros_like(wide)

        def add(rows, value, j):
            if 0 <= j < 4:
                wide[rows, j * TILE : (j + 1) * TILE] += value[:, :TILE]
            if j >= 1:
                wide[rows, j * TILE - LANES : j * TILE] += value[:, TILE : TILE + LANES]
            if j <= 2:
                wide[rows, (j + 1) * TILE : (j + 1) * TILE + LANES] += value[:, TILE + LANES :]

        sources = [[ids[j, 2 * row + i] // CELLS for j in range(4)] for i in range(2)]
        flat = sources[0] + sources[1]
        for i in range(2):
            for j in range(4):
                n = 4 * i + j
                rank = jnp.int32(0)
                for m in range(n):
                    rank = rank + (flat[m] == flat[n]).astype(jnp.int32)
                rank = jnp.minimum(rank, 1)
                value = dot(tiles[flat[n], 0:Q, :], across[rank]) * dose[i, j]
                add(slice(i * Q, (i + 1) * Q), value, j)

        strips = tiles[0, Q : 2 * Q, :].astype(F32)
        for source in range(1, ROWS):
            strips = strips + tiles[source, Q : 2 * Q, :].astype(F32)

        def doses(source):
            info = tiles[source, 2 * Q : 2 * Q + 16, :].astype(F32)[8:]
            return info + pltpu.roll(info, LANES - 4, 1) + pltpu.roll(info, LANES - 8, 1)

        own = doses(row)
        above = doses(jnp.maximum(row - 1, 0))
        below = doses(jnp.minimum(row + 1, ROWS - 1))
        lane_of = [7] + [20 + j for j in range(4)] + [36]
        for j in range(-1, 5):
            block, half = (j + 1) // 2, (j + 1) % 2
            upper = strips[block * 8 : (block + 1) * 8]
            lower = strips[24 + block * 8 : 24 + (block + 1) * 8]
            both = jnp.concatenate([upper, lower], axis=0).astype(BF16)
            value = dot(both, across[half])
            at = lane_of[j + 1]
            top = jnp.broadcast_to(above[1:2, at : at + 1], (REACH, 5 * LANES))
            bottom = jnp.broadcast_to(below[0:1, at : at + 1], (REACH, 5 * LANES))
            add(slice(2 * Q, 2 * Q + 16), value * jnp.concatenate([top, bottom], axis=0), j)

        sides = strips[48:64]
        for end in range(2):
            pixels = jnp.transpose(sides[8 * end : 8 * end + 8]).astype(BF16)
            at = lane_of[0] if end == 0 else lane_of[5]
            value = dot(pixels, side[8 * end : 8 * end + 8, :])
            scale = jnp.concatenate(
                [jnp.broadcast_to(own[i : i + 1, at : at + 1], (Q, LANES)) for i in range(2)],
                axis=0,
            )
            cols = slice(0, LANES) if end == 0 else slice(4 * TILE - LANES, 4 * TILE)
            wide[0 : 2 * Q, cols] += value * scale
        narrow[...] = wide[...].astype(BF16)

    columns = narrow[:, pl.ds(pl.multiple_of(step * TILE, TILE), TILE)]
    level = dot(down[0], columns) + dot(down[1], columns)
    out[...] = (0.5 * jnp.tanh(level - 4.0 * threshold[0]) + 0.5).astype(BF16)


def whole(array):
    return pl.BlockSpec(array.shape, lambda *_: (0,) * array.ndim)


def scalars():
    return pl.BlockSpec(memory_space=pltpu.SMEM)


PARAMS = pltpu.CompilerParams(vmem_limit_bytes=48 * 1024 * 1024)


def local(masks, owned_counts, cell_ids, kernels, kernel_weights, dose, threshold):
    table = {name: jnp.asarray(value) for name, value in tables().items()}

    ids = cell_ids.T
    constants = [
        table[n] for n in ("forward_cols", "forward_rows", "inverse_left", "inverse_right")
    ]
    operands = [masks, kernels, kernel_weights, ids, dose, *constants]
    placed = [pltpu.with_memory_space_constraint(op, pltpu.HBM) for op in operands]
    packet = pl.pallas_call(
        imaging_kernel,
        out_shape=jax.ShapeDtypeStruct((COLS, PACKET, LANES), BF16),
        in_specs=[pl.BlockSpec(memory_space=pltpu.HBM)] * len(operands),
        out_specs=pl.BlockSpec(memory_space=pltpu.VMEM),
        scratch_shapes=[
            *[
                (pltpu.SMEM if op is kernel_weights else pltpu.VMEM)(op.shape, op.dtype)
                for op in operands
            ],
            pltpu.VMEM((2, NK // 2, NF, LANES), F32),
            pltpu.VMEM((16, LANES), F32),
            pltpu.SemaphoreType.DMA((len(operands) + SLOTS - 1,)),
        ],
        compiler_params=PARAMS,
    )(*placed)

    packets = lax.all_to_all(packet, "cols", split_axis=0, concat_axis=0, tiled=True)

    outgoing = pl.pallas_call(
        routing_kernel,
        out_shape=jax.ShapeDtypeStruct((ROWS, OUTGOING, LANES), BF16),
        in_specs=[
            pl.BlockSpec(memory_space=pltpu.VMEM),
            scalars(),
            pl.BlockSpec(memory_space=pltpu.VMEM),
            pl.BlockSpec(memory_space=pltpu.VMEM),
        ],
        out_specs=pl.BlockSpec(memory_space=pltpu.VMEM),
        scratch_shapes=[
            pltpu.VMEM((CELLS, 32, LANES), F32),
            pltpu.VMEM((16, LANES), jnp.int32),
            pltpu.SMEM((16, LANES), jnp.int32),
            pltpu.SMEM((CELLS + SLOTS,), jnp.int32),
            pltpu.SemaphoreType.DMA,
        ],
        compiler_params=PARAMS,
    )(packets, owned_counts, table["edge"], table["edge_pad"])

    incoming = lax.all_to_all(outgoing, "rows", split_axis=0, concat_axis=0, tiled=True)

    constants = [table[n] for n in ("across", "side", "down")]
    return pl.pallas_call(
        develop_kernel,
        grid=(4,),
        out_shape=jax.ShapeDtypeStruct((2 * TILE, 4 * TILE), BF16),
        in_specs=[
            whole(incoming),
            scalars(),
            scalars(),
            scalars(),
            *[whole(t) for t in constants],
        ],
        out_specs=pl.BlockSpec((2 * TILE, TILE), lambda s: (0, s)),
        scratch_shapes=[
            pltpu.VMEM((OUTGOING, 4 * TILE), F32),
            pltpu.VMEM((OUTGOING, 4 * TILE), BF16),
        ],
        compiler_params=PARAMS,
    )(incoming, ids, dose, threshold, *constants)


def solution(mesh):
    return jax.shard_map(
        local,
        mesh=mesh,
        in_specs=(
            P(("rows", "cols"), None, None),
            P(),
            P(None, "cols"),
            P(),
            P(),
            P("rows", "cols"),
            P(),
        ),
        out_specs=P("rows", "cols"),
        check_vma=False,
    )
```

```python
import functools

import jax
import jax.numpy as jnp
import ml_dtypes
import numpy as np
from jax import lax
from jax.experimental import pallas as pl
from jax.experimental.pallas import tpu as pltpu
from jax.sharding import PartitionSpec as P

REACH = 8
TILE = 384
NF = 32
NK = 16
Q = 64
SLOTS = 6
ROWS = 8
COLS = 16
CELLS = 32
LANES = 128
HALF = NF // 2
EXTRA = 3 * HALF
IDS = EXTRA + SLOTS
DOSES = IDS + 4
PACKET = EXTRA + 16
WINDOW = 4 * 6
REST = WINDOW * HALF // 2
WINDOW_DOSES = REST + WINDOW
OUTGOING = REST + 32
BF16 = jnp.bfloat16
F32 = jnp.float32


def split(table):
    high = table.astype(ml_dtypes.bfloat16)
    low = (table - high.astype(np.float64)).astype(ml_dtypes.bfloat16)
    return high, low


@functools.lru_cache(maxsize=None)
def tables():
    freq = np.arange(NF) - NF // 2
    pixels = np.arange(TILE)
    points = np.arange(Q)
    turn = np.mod(freq[:, None] * pixels[None, :], TILE) * (2.0 * np.pi / TILE)
    forward = np.concatenate([np.cos(turn), np.sin(turn)]) / TILE
    high, low = split(forward)
    forward_rows = np.concatenate([high, low])
    forward_cols = np.ascontiguousarray(forward_rows.T)

    turn = np.mod(points[:, None] * freq[None, :], Q) * (2.0 * np.pi / Q)
    cos, sin = np.cos(turn), np.sin(turn)
    inverse_left = np.concatenate([cos, -sin], axis=1)
    edges = np.concatenate([np.arange(TILE - REACH, TILE), np.arange(REACH)])
    turn = np.mod(edges[:, None] * freq[None, :], TILE) * (2.0 * np.pi / TILE)
    edge_left = np.concatenate([np.cos(turn), -np.sin(turn)], axis=1)
    right = np.zeros((LANES, 2 * LANES))
    for k in range(2):
        re = slice(2 * k * NF, (2 * k + 1) * NF)
        im = slice((2 * k + 1) * NF, (2 * k + 2) * NF)
        out_re = slice(k * LANES, k * LANES + Q)
        out_im = slice(k * LANES + Q, (k + 1) * LANES)
        right[re, out_re], right[re, out_im] = cos.T, sin.T
        right[im, out_re], right[im, out_im] = -sin.T, cos.T

    spread_up = np.zeros((LANES, 4 * LANES))
    spread_low = np.zeros((LANES, 4 * LANES))
    rest = np.zeros((LANES, 2 * LANES))
    for copy in range(4):
        for part in range(2):
            for b in range(NF):
                for tile in range(2):
                    lane = tile * Q + part * NF + b
                    base = tile * 2 * LANES + part * LANES + copy * NF
                    spread_up[lane, base + b] = 1.0
                    if b:
                        spread_low[lane, base + NF - b] = -1.0 if part else 1.0
                rest[part * NF + b, part * LANES + copy * NF + b] = 1.0
            for i in range(1, HALF):
                rest[Q + part * (HALF - 1) + i - 1, part * LANES + copy * NF] = 1.0
        rest[Q + 2 * (HALF - 1), copy * NF + HALF] = 1.0
    rest_mask = np.zeros((HALF, LANES), np.float32)
    rest_mask[0, :Q] = rest_mask[0, Q + 2 * (HALF - 1)] = 1.0
    turned = np.zeros((REST, REST))
    for i in range(1, HALF):
        rest_mask[i, Q + i - 1] = rest_mask[i, Q + HALF - 1 + i - 1] = 1.0
        for pair in range(WINDOW // 2):
            turned[pair * HALF + i, pair * HALF + HALF - i] = 1.0

    harmonic = np.arange(Q) - Q // 2
    fine = np.mod(pixels[:, None] * harmonic[None, :], TILE) * (2.0 * np.pi / TILE)
    grid = np.mod(points[:, None] * harmonic[None, :], Q) * (2.0 * np.pi / Q)
    interp = (np.cos(fine) @ np.cos(grid).T + np.sin(fine) @ np.sin(grid).T) / Q
    interp = interp.astype(ml_dtypes.bfloat16).astype(np.float64)

    offsets = np.arange(2 * REACH + 1) - REACH
    taps = np.exp(-offsets * offsets / 32.0)
    taps = taps / taps.sum()

    def blur(out_pixels, in_pixels):
        gap = out_pixels[:, None] - in_pixels[None, :]
        inside = np.abs(gap) <= REACH
        return np.where(inside, taps[np.clip(gap + REACH, 0, 2 * REACH)], 0.0)

    reach_cols = np.concatenate(
        [np.arange(TILE), np.arange(-LANES, 0), np.arange(TILE, TILE + LANES)]
    )
    spread = (blur(reach_cols, pixels) @ interp).T
    across = np.zeros((LANES, 5 * LANES))
    across[:Q] = spread

    out_rows = np.arange(2 * TILE)
    down = np.concatenate(
        [
            blur(out_rows, pixels) @ interp,
            blur(out_rows, pixels + TILE) @ interp,
            blur(out_rows, np.arange(-REACH, 0)),
            blur(out_rows, np.arange(2 * TILE, 2 * TILE + REACH)),
        ],
        axis=1,
    )
    bf16 = dict(
        forward_rows=forward_rows,
        forward_cols=forward_cols,
        inverse_left=inverse_left,
        edge_left=edge_left,
        inverse_right=right,
        spread_up=spread_up,
        spread_low=spread_low,
        rest=rest,
        turned=turned,
        across=across,
        down=4.0 * down,
    )
    out = {name: value.astype(ml_dtypes.bfloat16) for name, value in bf16.items()}
    out["rest_mask"] = rest_mask
    return out


def dot(a, b):
    return jnp.dot(a, b, preferred_element_type=F32)


def halves(x):
    high = x.astype(BF16)
    return high, (x - high.astype(F32)).astype(BF16)


def lanes_of(shape):
    return lax.broadcasted_iota(jnp.int32, shape, 1)


def spectra_kernel(
    mask, kernels, weights, ids, dose, fwd_cols, fwd_rows,
    out, ker,
    mask_v, kernels_v, weights_s, ids_v, dose_v, cols_v, rows_v, extra, sems,
):
    moves = [(fwd_cols, cols_v)]
    moves += [(mask.at[s], mask_v.at[s]) for s in range(SLOTS)]
    moves += [(kernels, kernels_v), (weights, weights_s), (fwd_rows, rows_v)]
    moves += [(ids, ids_v), (dose, dose_v)]
    copies = [
        pltpu.make_async_copy(src, dst, sems.at[i]) for i, (src, dst) in enumerate(moves)
    ]
    for copy in copies:
        copy.start()
    for copy in copies[:4]:
        copy.wait()

    left = lanes_of((TILE, LANES)) < Q
    pairs = []
    for slot in range(SLOTS):
        if slot == 3:
            for copy in copies[4:]:
                copy.wait()
            for two in range(NK // 2):
                re, im = [], []
                for k in (2 * two, 2 * two + 1):
                    scale = jnp.sqrt(jnp.full((NF, NF), weights_s[k], F32))
                    re.append(kernels_v[0, k] * scale)
                    im.append(kernels_v[1, k] * scale)
                ker[0, two] = jnp.concatenate([re[0], im[0], re[1], im[1]], axis=1)
                ker[1, two] = jnp.concatenate([-im[0], re[0], -im[1], re[1]], axis=1)
        cols = dot(mask_v[slot], cols_v[...])
        cols = cols + pltpu.roll(cols, Q, 1)
        high = cols.astype(BF16).astype(F32)
        pairs.append(jnp.where(left, high, cols - high).astype(BF16))

    lane = lanes_of((NF, LANES))
    line = lax.broadcasted_iota(jnp.int32, (NF, LANES), 0)
    even = (lane // NF) % 2 == 0
    in_re = lane == line + Q - HALF - 1
    in_im = lane == line + Q - HALF - 1 + HALF - 1
    column = line > HALF
    lane1 = lanes_of((1, LANES))
    blocks, rows = [], []
    for slot in range(SLOTS):
        both = dot(rows_v[...], pairs[slot])
        both = both[:Q] + both[Q:]
        both = both + pltpu.roll(both, Q, 1)
        top, bottom = both[:NF], both[NF:]
        real = top - pltpu.roll(bottom, NF, 1)
        imag = -(bottom + pltpu.roll(top, NF, 1))
        blocks.append(jnp.where(even, real, pltpu.roll(imag, NF, 1)))
        first = jnp.where(column & in_re, jnp.broadcast_to(real[:, 0:1], (NF, LANES)), 0.0)
        second = jnp.where(column & in_im, jnp.broadcast_to(imag[:, 0:1], (NF, LANES)), 0.0)
        turned = jnp.sum(first + second, axis=0, keepdims=True)
        mean = real[HALF : HALF + 1, HALF : HALF + 1]
        mean = jnp.broadcast_to(mean - mean.astype(BF16).astype(F32), (1, LANES))
        turned = jnp.where(lane1 == Q + 2 * (HALF - 1), mean, turned)
        rows.append(jnp.where(lane1 < Q, blocks[slot][HALF : HALF + 1], turned))
    half = lanes_of((HALF, LANES)) < Q
    packed = [
        jnp.where(half, blocks[2 * i][:HALF], blocks[2 * i + 1][:HALF]).astype(BF16)
        for i in range(SLOTS // 2)
    ]
    extra[...] = jnp.zeros_like(extra)
    for slot in range(SLOTS):
        extra[slot : slot + 1, :] = rows[slot]
    extra[IDS - EXTRA : IDS - EXTRA + 4, 0:16] = ids_v[...].astype(F32)
    at = slice(DOSES - EXTRA, DOSES - EXTRA + 2)
    high = dose_v[...].astype(BF16).astype(F32)
    middle = (dose_v[...] - high).astype(BF16).astype(F32)
    extra[at, 4:8] = high
    extra[at, 8:12] = middle
    extra[at, 12:16] = dose_v[...] - high - middle
    packed.append(extra[...].astype(BF16))
    for c in range(COLS):
        for i in range(4):
            out[c, i * HALF : (i + 1) * HALF, :] = packed[i]


def routing_kernel(packets, counts, out, held, rests, buffer, where_v, where_s, sem):
    row, col = lax.axis_index("rows"), lax.axis_index("cols")
    for c in range(COLS):
        rests[c * 16 : (c + 1) * 16, :] = packets[c, EXTRA : EXTRA + 16, :].astype(F32)

    def rest_of(c):
        return rests[pl.ds(pl.multiple_of(c * 16, 16), 16), :]

    before = rest_of(jnp.maximum(col - 1, 0))
    here = rest_of(col)
    after = rest_of(jnp.minimum(col + 1, COLS - 1))
    line = lax.broadcasted_iota(jnp.int32, (16, LANES), 0)
    first = IDS - EXTRA
    window = jnp.where(
        line == 0,
        pltpu.roll(before, 16 - first - 3, 0),
        jnp.where(line < 5, pltpu.roll(here, 16 - first + 1, 0), pltpu.roll(after, 16 - first + 5, 0)),
    ).astype(jnp.int32)
    cell = window - row * CELLS
    exists = ((line > 0) | (col > 0)) & ((line < 5) | (col < COLS - 1)) & (line < 6)
    mine = (cell >= 0) & (cell < CELLS) & exists
    where_v[...] = jnp.where(mine, cell, CELLS)
    copy = pltpu.make_async_copy(where_v, where_s, sem)
    copy.start()

    left = lanes_of((HALF, LANES)) < Q
    start = jnp.int32(0)
    for c in range(COLS):
        count = counts[row, c]
        for s in range(SLOTS):
            pair = packets[c, (s // 2) * HALF : (s // 2 + 1) * HALF, :].astype(F32)
            moved = pltpu.roll(pair, Q, 1)
            both = jnp.where(left, moved, pair) if s % 2 else jnp.where(left, pair, moved)
            held[start + s] = both
            buffer[pl.ds(start + s, 1), :] = rests[c * 16 + s : c * 16 + s + 1, :]
        start = start + count
    held[CELLS] = jnp.zeros((HALF, LANES), F32)
    buffer[CELLS : CELLS + 1, :] = jnp.zeros((1, LANES), F32)

    lane = lanes_of((2, LANES))
    at = slice(DOSES - EXTRA, DOSES - EXTRA + 2)
    doses = jnp.where(
        lane < 16,
        before[at],
        jnp.where(lane < 32, pltpu.roll(here[at], 16, 1), pltpu.roll(after[at], 32, 1)),
    )
    tail = jnp.concatenate([doses, jnp.zeros((6, LANES), F32)], axis=0)
    copy.wait()
    for dest in range(ROWS):
        rows = []
        for i in range(4):
            tile_row = 2 * dest - 1 + i
            if not 0 <= tile_row < 2 * ROWS:
                for pair in range(3):
                    at = (3 * i + pair) * HALF
                    out[dest, at : at + HALF, :] = jnp.zeros((HALF, LANES), BF16)
                rows += [jnp.zeros((1, LANES), F32)] * 6
                continue
            for pair in range(3):
                one, two = where_s[2 * pair, tile_row], where_s[2 * pair + 1, tile_row]
                at = (3 * i + pair) * HALF
                out[dest, at : at + HALF, :] = jnp.where(left, held[one], held[two]).astype(BF16)
                rows += [buffer[pl.ds(one, 1), :], buffer[pl.ds(two, 1), :]]
        rest = jnp.concatenate(rows + [tail], axis=0).astype(BF16)
        out[dest, REST : REST + 32, :] = rest


def develop_kernel(
    tiles, ker, threshold, turned, spread_up, spread_low, rest, rest_mask,
    inv_left, edge_left, inv_right, across, down,
    out,
    narrow, stage, sems,
):
    row = lax.axis_index("rows")
    window = tiles[0].astype(F32)
    for source in range(1, ROWS):
        window = window + tiles[source].astype(F32)
    held = window[:REST].astype(BF16)
    upper = dot(held, spread_up[...])
    lower = dot(dot(turned[...], held).astype(BF16), spread_low[...])
    rests = [
        jnp.broadcast_to(window[REST + t : REST + t + 1], (HALF, LANES)) * rest_mask[...]
        for t in range(WINDOW)
    ]
    rests = dot(jnp.concatenate(rests, axis=0).astype(BF16), rest[...])

    def doses(source):
        info = tiles[source, REST + 16 : REST + 32, :].astype(F32)[8:]
        return info + pltpu.roll(info, LANES - 4, 1) + pltpu.roll(info, LANES - 8, 1)

    own = doses(row)
    above = doses(jnp.maximum(row - 1, 0))
    below = doses(jnp.minimum(row + 1, ROWS - 1))

    images = []
    for i in range(4):
        whole_tile = i in (1, 2)
        halfway = []
        for j in range(6):
            m, t = 3 * i + j // 2, 6 * i + j
            a, r = slice(m * HALF, (m + 1) * HALF), slice(t * HALF, (t + 1) * HALF)
            re = slice((j % 2) * 2 * LANES, (j % 2) * 2 * LANES + LANES)
            im = slice(re.stop, re.stop + LANES)
            real = jnp.concatenate([upper[a, re], lower[a, re] + rests[r, :LANES]], axis=0)
            imag = jnp.concatenate([upper[a, im], lower[a, im] + rests[r, LANES:]], axis=0)
            prods = []
            for two in range(NK // 2):
                ka, kb = ker[0, two], ker[1, two]
                prod = jnp.concatenate([ka * real + kb * imag, ka * imag - kb * real], axis=0)
                prods.append(prod.astype(BF16))
            prod = jnp.concatenate(prods, axis=1)
            table = inv_left[...] if whole_tile else edge_left[...]
            half = dot(table, prod)
            if not whole_tile:
                half = half[:REACH] if i == 0 else half[REACH:]
            halfway.append(
                jnp.concatenate(
                    [half[:, n * LANES : (n + 1) * LANES] for n in range(NK // 2)], axis=0
                ).astype(BF16)
            )
        line = []
        for j in range(6):
            field = dot(halfway[j], inv_right[...])
            power = field * field
            power = power[:, :LANES] + power[:, LANES:]
            height = power.shape[0] // (NK // 2)
            total = power[:height]
            for n in range(1, NK // 2):
                total = total + power[n * height : (n + 1) * height]
            line.append(total + pltpu.roll(total, Q, 1))
        images.append(line)

    lane_of = [7] + [20 + j for j in range(4)] + [36]
    values = []
    for j in range(6):
        rows = [images[1][j], images[2][j], images[0][j], images[3][j]]
        block = jnp.concatenate(rows, axis=0).astype(BF16)
        cols = slice(0, 5 * LANES)
        if j == 0:
            cols = slice(4 * LANES, 5 * LANES)
        if j == 5:
            cols = slice(3 * LANES, 4 * LANES)
        value = dot(block, across[:, cols])
        at = slice(lane_of[j], lane_of[j] + 1)
        scales = [own[0:1, at], own[1:2, at], above[1:2, at], below[0:1, at]]
        heights = [Q, Q, REACH, REACH]
        scale = jnp.concatenate(
            [jnp.broadcast_to(s, (h, LANES)) for s, h in zip(scales, heights)], axis=0
        )
        values.append([value[:, n : n + LANES] * scale for n in range(0, value.shape[1], LANES)])
    for j in range(1, 5):
        parts = values[j][:3]
        before = values[j - 1][-1]
        after = values[j + 1][3] if j < 4 else values[j + 1][0]
        parts = [parts[0] + before, parts[1], parts[2] + after]
        for n in range(3):
            at = (j - 1) * TILE + n * LANES
            narrow[:, at : at + LANES] = parts[n].astype(BF16)

    shift = 4.0 * threshold[0]
    chunk = 2 * TILE // 4
    copies = []
    for n in range(4):
        rows = pl.ds(n * chunk, chunk)
        level = dot(down[rows, :], narrow[...])
        stage[rows, :] = (0.5 * jnp.tanh(level - shift) + 0.5).astype(BF16)
        copy = pltpu.make_async_copy(stage.at[rows, :], out.at[rows, :], sems.at[n])
        copy.start()
        copies.append(copy)
    for copy in copies:
        copy.wait()


PARAMS = pltpu.CompilerParams(vmem_limit_bytes=48 * 1024 * 1024)
IN_HBM = pl.BlockSpec(memory_space=pltpu.HBM)
IN_VMEM = pl.BlockSpec(memory_space=pltpu.VMEM)
IN_SMEM = pl.BlockSpec(memory_space=pltpu.SMEM)


def image(masks, cell_ids, kernels, kernel_weights, dose):
    table = tables()
    operands = [masks, kernels, kernel_weights, cell_ids.T, dose]
    operands += [jnp.asarray(table[n]) for n in ("forward_cols", "forward_rows")]
    in_hbm = [pltpu.with_memory_space_constraint(op, pltpu.HBM) for op in operands]
    ker = (2, NK // 2, NF, LANES)
    return pl.pallas_call(
        spectra_kernel,
        out_shape=(
            jax.ShapeDtypeStruct((COLS, PACKET, LANES), BF16),
            jax.ShapeDtypeStruct(ker, F32),
        ),
        in_specs=[IN_HBM] * len(operands),
        out_specs=(IN_VMEM, IN_VMEM),
        scratch_shapes=[
            *[
                (pltpu.SMEM if op is kernel_weights else pltpu.VMEM)(op.shape, op.dtype)
                for op in operands
            ],
            pltpu.VMEM((16, LANES), F32),
            pltpu.SemaphoreType.DMA((len(operands) + SLOTS - 1,)),
        ],
        compiler_params=PARAMS,
    )(*in_hbm)


def route(packets, owned_counts):
    return pl.pallas_call(
        routing_kernel,
        out_shape=jax.ShapeDtypeStruct((ROWS, OUTGOING, LANES), BF16),
        in_specs=[IN_VMEM, IN_SMEM],
        out_specs=IN_VMEM,
        scratch_shapes=[
            pltpu.VMEM((CELLS + SLOTS, HALF, LANES), F32),
            pltpu.VMEM((COLS * 16, LANES), F32),
            pltpu.VMEM((CELLS + 8, LANES), F32),
            pltpu.VMEM((16, LANES), jnp.int32),
            pltpu.SMEM((16, LANES), jnp.int32),
            pltpu.SemaphoreType.DMA,
        ],
        compiler_params=PARAMS,
    )(packets, owned_counts)


def develop(incoming, ker, threshold):
    table = tables()
    names = ("turned", "spread_up", "spread_low", "rest", "rest_mask")
    names += ("inverse_left", "edge_left", "inverse_right", "across", "down")
    constants = [jnp.asarray(table[n]) for n in names]
    return pl.pallas_call(
        develop_kernel,
        out_shape=jax.ShapeDtypeStruct((2 * TILE, 4 * TILE), BF16),
        in_specs=[IN_VMEM, IN_VMEM, IN_SMEM, *[IN_VMEM] * len(constants)],
        out_specs=IN_HBM,
        scratch_shapes=[
            pltpu.VMEM((2 * Q + 2 * REACH, 4 * TILE), BF16),
            pltpu.VMEM((2 * TILE, 4 * TILE), BF16),
            pltpu.SemaphoreType.DMA((4,)),
        ],
        compiler_params=PARAMS,
    )(incoming, ker, threshold, *constants)


def local(masks, owned_counts, cell_ids, kernels, kernel_weights, dose, threshold):
    packet, ker = image(masks, cell_ids, kernels, kernel_weights, dose)
    packets = lax.all_to_all(packet, "cols", split_axis=0, concat_axis=0, tiled=True)
    outgoing = route(packets, owned_counts)
    incoming = lax.all_to_all(outgoing, "rows", split_axis=0, concat_axis=0, tiled=True)
    return develop(incoming, ker, threshold)


def solution(mesh):
    return jax.shard_map(
        local,
        mesh=mesh,
        in_specs=(
            P(("rows", "cols"), None, None),
            P(),
            P(None, "cols"),
            P(),
            P(),
            P("rows", "cols"),
            P(),
        ),
        out_specs=P("rows", "cols"),
        check_vma=False,
    )
```

```python
import functools

import jax
import jax.numpy as jnp
import ml_dtypes
import numpy as np
from jax import lax
from jax.experimental import pallas as pl
from jax.experimental.pallas import tpu as pltpu
from jax.sharding import PartitionSpec as P

REACH = 8
TILE = 384
NF = 32
NK = 16
Q = 64
SLOTS = 6
ROWS = 8
COLS = 16
CELLS = 32
LANES = 128
HALF = NF // 2
EXTRA = 3 * HALF
IDS = EXTRA + SLOTS
DOSES = IDS + 4
PACKET = EXTRA + 16
WINDOW = 4 * 6
MOST = 14
REST = MOST * HALF // 2
OUTGOING = REST + 16
STACK = Q + 2 * REACH
SPLIT = TILE - 2 * REACH
BF16 = jnp.bfloat16
F32 = jnp.float32


def split(table):
    high = table.astype(ml_dtypes.bfloat16)
    low = (table - high.astype(np.float64)).astype(ml_dtypes.bfloat16)
    return high, low


@functools.lru_cache(maxsize=None)
def tables():
    freq = np.arange(NF) - NF // 2
    pixels = np.arange(TILE)
    points = np.arange(Q)
    turn = np.mod(freq[:, None] * pixels[None, :], TILE) * (2.0 * np.pi / TILE)
    forward = np.concatenate([np.cos(turn), np.sin(turn)]) / TILE
    high, low = split(forward)
    forward_rows = np.concatenate([high, low])
    forward_cols = np.ascontiguousarray(forward_rows.T)

    turn = np.mod(points[:, None] * freq[None, :], Q) * (2.0 * np.pi / Q)
    cos, sin = np.cos(turn), np.sin(turn)
    inverse_left = np.concatenate([cos, -sin], axis=1)
    edges = np.concatenate([np.arange(TILE - REACH, TILE), np.arange(REACH)])
    turn = np.mod(edges[:, None] * freq[None, :], TILE) * (2.0 * np.pi / TILE)
    edge_left = np.concatenate([np.cos(turn), -np.sin(turn)], axis=1)
    right = np.zeros((LANES, 2 * LANES))
    for k in range(2):
        re = slice(2 * k * NF, (2 * k + 1) * NF)
        im = slice((2 * k + 1) * NF, (2 * k + 2) * NF)
        out_re = slice(k * LANES, k * LANES + Q)
        out_im = slice(k * LANES + Q, (k + 1) * LANES)
        right[re, out_re], right[re, out_im] = cos.T, sin.T
        right[im, out_re], right[im, out_im] = -sin.T, cos.T

    spread_up = np.zeros((LANES, 4 * LANES))
    spread_low = np.zeros((LANES, 4 * LANES))
    rest = np.zeros((LANES, 2 * LANES))
    for copy in range(4):
        for part in range(2):
            for b in range(NF):
                for tile in range(2):
                    lane = tile * Q + part * NF + b
                    base = tile * 2 * LANES + part * LANES + copy * NF
                    spread_up[lane, base + b] = 1.0
                    if b:
                        spread_low[lane, base + NF - b] = -1.0 if part else 1.0
                rest[part * NF + b, part * LANES + copy * NF + b] = 1.0
            for i in range(1, HALF):
                rest[Q + part * (HALF - 1) + i - 1, part * LANES + copy * NF] = 1.0
        rest[Q + 2 * (HALF - 1), copy * NF + HALF] = 1.0
    rest_mask = np.zeros((HALF, LANES), np.float32)
    rest_mask[0, :Q] = rest_mask[0, Q + 2 * (HALF - 1)] = 1.0
    turned = np.zeros((WINDOW * HALF // 2, WINDOW * HALF // 2))
    for i in range(1, HALF):
        rest_mask[i, Q + i - 1] = rest_mask[i, Q + HALF - 1 + i - 1] = 1.0
        for pair in range(WINDOW // 2):
            turned[pair * HALF + i, pair * HALF + HALF - i] = 1.0

    harmonic = np.arange(Q) - Q // 2
    fine = np.mod(pixels[:, None] * harmonic[None, :], TILE) * (2.0 * np.pi / TILE)
    grid = np.mod(points[:, None] * harmonic[None, :], Q) * (2.0 * np.pi / Q)
    interp = (np.cos(fine) @ np.cos(grid).T + np.sin(fine) @ np.sin(grid).T) / Q
    interp = interp.astype(ml_dtypes.bfloat16).astype(np.float64)

    offsets = np.arange(2 * REACH + 1) - REACH
    taps = np.exp(-offsets * offsets / 32.0)
    taps = taps / taps.sum()

    def blur(out_pixels, in_pixels):
        gap = out_pixels[:, None] - in_pixels[None, :]
        inside = np.abs(gap) <= REACH
        return np.where(inside, taps[np.clip(gap + REACH, 0, 2 * REACH)], 0.0)

    across = np.zeros((4 * Q, TILE))
    for n in range(3):
        across[n * Q : (n + 1) * Q] = (blur(pixels, pixels + (n - 1) * TILE) @ interp).T

    out_rows = np.arange(2 * TILE)
    down = np.zeros((2 * TILE, 2 * STACK))
    down[:, :Q] = blur(out_rows, pixels) @ interp
    down[:, Q : Q + REACH] = blur(out_rows, np.arange(-REACH, 0))
    down[:, STACK : STACK + Q] = blur(out_rows, pixels + TILE) @ interp
    down[:, STACK + Q : STACK + Q + REACH] = blur(out_rows, 2 * TILE + np.arange(REACH))
    assert not down[:SPLIT, STACK:].any()

    bf16 = dict(
        forward_rows=forward_rows,
        forward_cols=forward_cols,
        inverse_left=inverse_left,
        edge_left=edge_left,
        inverse_right=right,
        spread_up=spread_up,
        spread_low=spread_low,
        rest=rest,
        turned=turned,
        across=across,
        down_upper=4.0 * down[:SPLIT, :STACK],
        down_lower=4.0 * down[SPLIT:],
    )
    out = {name: value.astype(ml_dtypes.bfloat16) for name, value in bf16.items()}
    out["rest_mask"] = rest_mask
    return out


def dot(a, b):
    return jnp.dot(a, b, preferred_element_type=F32)


def halves(x):
    high = x.astype(BF16)
    return high, (x - high.astype(F32)).astype(BF16)


def lanes_of(shape):
    return lax.broadcasted_iota(jnp.int32, shape, 1)


def spectra_kernel(
    mask, ids, dose, fwd_cols, fwd_rows, kernels, weights, counts,
    out, ker, starts,
    mask_v, ids_v, dose_v, cols_v, rows_v, kernels_v, weights_s, counts_s, extra, sems,
):
    moves = [(fwd_cols, cols_v)]
    moves += [(mask.at[s], mask_v.at[s]) for s in range(SLOTS)]
    moves += [(kernels, kernels_v), (weights, weights_s), (counts, counts_s)]
    moves += [(fwd_rows, rows_v), (ids, ids_v), (dose, dose_v)]
    copies = [
        pltpu.make_async_copy(src, dst, sems.at[i]) for i, (src, dst) in enumerate(moves)
    ]
    for copy in copies:
        copy.start()
    for copy in copies[:4]:
        copy.wait()

    left = lanes_of((TILE, LANES)) < Q
    pairs = []
    for slot in range(SLOTS):
        if slot == 3:
            for copy in copies[4:]:
                copy.wait()
            for two in range(NK // 2):
                re, im = [], []
                for k in (2 * two, 2 * two + 1):
                    scale = jnp.sqrt(jnp.full((NF, NF), weights_s[k], F32))
                    re.append(kernels_v[0, k] * scale)
                    im.append(kernels_v[1, k] * scale)
                ker[0, two] = jnp.concatenate([re[0], im[0], re[1], im[1]], axis=1)
                ker[1, two] = jnp.concatenate([-im[0], re[0], -im[1], re[1]], axis=1)
            start = jnp.int32(0)
            for c in range(COLS):
                starts[c] = start
                start = start + counts_s[lax.axis_index("rows"), c]
        cols = dot(mask_v[slot], cols_v[...])
        cols = cols + pltpu.roll(cols, Q, 1)
        high = cols.astype(BF16).astype(F32)
        pairs.append(jnp.where(left, high, cols - high).astype(BF16))

    lane = lanes_of((NF, LANES))
    line = lax.broadcasted_iota(jnp.int32, (NF, LANES), 0)
    even = (lane // NF) % 2 == 0
    in_re = lane == line + Q - HALF - 1
    in_im = lane == line + Q - HALF - 1 + HALF - 1
    column = line > HALF
    lane1 = lanes_of((1, LANES))
    blocks, rows = [], []
    for slot in range(SLOTS):
        both = dot(rows_v[...], pairs[slot])
        both = both[:Q] + both[Q:]
        both = both + pltpu.roll(both, Q, 1)
        top, bottom = both[:NF], both[NF:]
        real = top - pltpu.roll(bottom, NF, 1)
        imag = -(bottom + pltpu.roll(top, NF, 1))
        blocks.append(jnp.where(even, real, pltpu.roll(imag, NF, 1)))
        first = jnp.where(column & in_re, jnp.broadcast_to(real[:, 0:1], (NF, LANES)), 0.0)
        second = jnp.where(column & in_im, jnp.broadcast_to(imag[:, 0:1], (NF, LANES)), 0.0)
        turned = jnp.sum(first + second, axis=0, keepdims=True)
        mean = real[HALF : HALF + 1, HALF : HALF + 1]
        mean = jnp.broadcast_to(mean - mean.astype(BF16).astype(F32), (1, LANES))
        turned = jnp.where(lane1 == Q + 2 * (HALF - 1), mean, turned)
        rows.append(jnp.where(lane1 < Q, blocks[slot][HALF : HALF + 1], turned))
    half = lanes_of((HALF, LANES)) < Q
    packed = [
        jnp.where(half, blocks[2 * i][:HALF], blocks[2 * i + 1][:HALF]).astype(BF16)
        for i in range(SLOTS // 2)
    ]
    extra[...] = jnp.zeros_like(extra)
    for slot in range(SLOTS):
        extra[slot : slot + 1, :] = rows[slot]
    extra[IDS - EXTRA : IDS - EXTRA + 4, 0:16] = ids_v[...].astype(F32)
    at = slice(DOSES - EXTRA, DOSES - EXTRA + 2)
    high = dose_v[...].astype(BF16).astype(F32)
    middle = (dose_v[...] - high).astype(BF16).astype(F32)
    extra[at, 4:8] = high
    extra[at, 8:12] = middle
    extra[at, 12:16] = dose_v[...] - high - middle
    packed.append(extra[...].astype(BF16))
    for c in range(COLS):
        for i in range(4):
            out[c, i * HALF : (i + 1) * HALF, :] = packed[i]


def routing_kernel(
    packets, starts,
    out, place,
    held, rests, buffer, where_v, where_s, chosen, taken, sem,
):
    row, col = lax.axis_index("rows"), lax.axis_index("cols")
    for c in range(COLS):
        rests[c * 16 : (c + 1) * 16, :] = packets[c, EXTRA : EXTRA + 16, :].astype(F32)

    def rest_of(c):
        return rests[pl.ds(pl.multiple_of(c * 16, 16), 16), :]

    before = rest_of(jnp.maximum(col - 1, 0))
    here = rest_of(col)
    after = rest_of(jnp.minimum(col + 1, COLS - 1))
    line = lax.broadcasted_iota(jnp.int32, (16, LANES), 0)
    first = IDS - EXTRA
    window = jnp.where(
        line == 0,
        pltpu.roll(before, 16 - first - 3, 0),
        jnp.where(line < 5, pltpu.roll(here, 16 - first + 1, 0), pltpu.roll(after, 16 - first + 5, 0)),
    ).astype(jnp.int32)
    exists = ((line > 0) | (col > 0)) & ((line < 5) | (col < COLS - 1)) & (line < 6)
    where_v[...] = jnp.where(exists, window, -1)
    copy = pltpu.make_async_copy(where_v, where_s, sem)
    copy.start()

    left = lanes_of((HALF, LANES)) < Q
    for c in range(COLS):
        start = starts[c]
        for s in range(SLOTS):
            pair = packets[c, (s // 2) * HALF : (s // 2 + 1) * HALF, :].astype(F32)
            moved = pltpu.roll(pair, Q, 1)
            both = jnp.where(left, moved, pair) if s % 2 else jnp.where(left, pair, moved)
            held[start + s] = both
            buffer[pl.ds(start + s, 1), :] = rests[c * 16 + s : c * 16 + s + 1, :]
    held[CELLS] = jnp.zeros((HALF, LANES), F32)
    buffer[CELLS : CELLS + 1, :] = jnp.zeros((1, LANES), F32)

    lane = lanes_of((2, LANES))
    at = slice(DOSES - EXTRA, DOSES - EXTRA + 2)
    doses = jnp.where(
        lane < 16,
        before[at],
        jnp.where(lane < 32, pltpu.roll(here[at], 16, 1), pltpu.roll(after[at], 32, 1)),
    )
    for n in range(ROWS + 1):
        taken[n] = jnp.int32(0)
    copy.wait()

    for i in range(4):
        tile_row = 2 * row - 1 + i
        inside = (tile_row >= 0) & (tile_row < 2 * ROWS)
        for j in range(6):
            cell = where_s[j, jnp.clip(tile_row, 0, 2 * ROWS - 1)]
            cell = jnp.where(inside, cell, -1)
            source = cell >> 5
            rank = taken[source + 1]
            taken[source + 1] = rank + 1
            place[6 * i + j] = jnp.where(cell >= 0, source * 16 + rank, -1)

    for dest in range(ROWS):
        count = jnp.int32(0)
        for i in range(4):
            tile_row = 2 * dest - 1 + i
            if 0 <= tile_row < 2 * ROWS:
                for j in range(6):
                    cell = where_s[j, tile_row]
                    chosen[dest * 16 + count] = cell & (CELLS - 1)
                    count = count + ((cell >> 5) == row).astype(jnp.int32)
        cells = [jnp.where(n < count, chosen[dest * 16 + n], CELLS) for n in range(MOST)]
        for pair in range(MOST // 2):
            one, two = cells[2 * pair], cells[2 * pair + 1]
            at = pair * HALF
            out[dest, at : at + HALF, :] = jnp.where(left, held[one], held[two]).astype(BF16)
        rows = [buffer[pl.ds(cell, 1), :] for cell in cells]
        out[dest, REST : REST + 16, :] = jnp.concatenate(rows + [doses], axis=0).astype(BF16)


def develop_kernel(
    tiles, place, ker, threshold, turned, spread_up, spread_low, rest, rest_mask,
    inv_left, edge_left, inv_right, across, down_upper, down_lower,
    out,
    after_rows, stage, sems,
):
    row = lax.axis_index("rows")
    for source in range(ROWS):
        at = slice(source * 16, (source + 1) * 16)
        after_rows[at, :] = tiles[source, REST : REST + 16, :].astype(F32)
    left = lanes_of((HALF, LANES)) < Q
    held, rests = [], []
    for t in range(0, WINDOW, 2):
        both = []
        for n in (t, t + 1):
            here = jnp.maximum(place[n], 0)
            rank = here & 15
            at = pl.multiple_of((rank >> 1) * HALF, HALF)
            pair = tiles[here >> 4, pl.ds(at, HALF), :].astype(F32)
            tile = jnp.where((rank & 1) == (n & 1), pair, pltpu.roll(pair, Q, 1))
            both.append(jnp.where(place[n] >= 0, tile, 0.0))
            line = jnp.where(place[n] >= 0, after_rows[pl.ds(here, 1), :], 0.0)
            rests.append(jnp.broadcast_to(line, (HALF, LANES)) * rest_mask[...])
        held.append(jnp.where(left, both[0], both[1]).astype(BF16))
    held = jnp.concatenate(held, axis=0)
    upper = dot(held, spread_up[...])
    lower = dot(dot(turned[...], held).astype(BF16), spread_low[...])
    rests = dot(jnp.concatenate(rests, axis=0).astype(BF16), rest[...])

    def doses(source):
        info = after_rows[pl.ds(pl.multiple_of(source * 16, 16), 16), :][MOST:]
        return info + pltpu.roll(info, LANES - 4, 1) + pltpu.roll(info, LANES - 8, 1)

    own = doses(row)
    above = doses(jnp.maximum(row - 1, 0))
    below = doses(jnp.minimum(row + 1, ROWS - 1))

    def picture(i, j):
        whole_tile = i in (1, 2)
        m, t = 3 * i + j // 2, 6 * i + j
        a, r = slice(m * HALF, (m + 1) * HALF), slice(t * HALF, (t + 1) * HALF)
        re = slice((j % 2) * 2 * LANES, (j % 2) * 2 * LANES + LANES)
        im = slice(re.stop, re.stop + LANES)
        real = jnp.concatenate([upper[a, re], lower[a, re] + rests[r, :LANES]], axis=0)
        imag = jnp.concatenate([upper[a, im], lower[a, im] + rests[r, LANES:]], axis=0)
        prods = []
        for two in range(NK // 2):
            ka, kb = ker[0, two], ker[1, two]
            prod = jnp.concatenate([ka * real + kb * imag, ka * imag - kb * real], axis=0)
            prods.append(prod.astype(BF16))
        prod = jnp.concatenate(prods, axis=1)
        half = dot(inv_left[...] if whole_tile else edge_left[...], prod)
        if not whole_tile:
            half = half[:REACH] if i == 0 else half[REACH:]
        return jnp.concatenate(
            [half[:, n * LANES : (n + 1) * LANES] for n in range(NK // 2)], axis=0
        ).astype(BF16)

    def intensity(halfway):
        field = dot(halfway, inv_right[...])
        power = field * field
        power = power[:, :LANES] + power[:, LANES:]
        height = power.shape[0] // (NK // 2)
        total = power[:height]
        for n in range(1, NK // 2):
            total = total + power[n * height : (n + 1) * height]
        return total + pltpu.roll(total, Q, 1)

    lane_of = [7] + [20 + j for j in range(4)] + [36]
    dose_rows = [above[1:2], own[0:1], own[1:2], below[0:1]]
    left = lanes_of((STACK, LANES)) < Q

    images = {}
    for group in ((0, 3), (1,), (2,)):
        halfway = {(i, j): picture(i, j) for i in group for j in range(6)}
        for i in group:
            for j in range(6):
                scale = dose_rows[i][:, lane_of[j] : lane_of[j] + 1]
                images[i, j] = intensity(halfway[i, j]) * scale

    def columns(strip, tile):
        none = jnp.zeros((REACH, LANES), F32)
        stack = [
            jnp.concatenate([images[tile, j], images[strip, j], none], axis=0) for j in range(6)
        ]
        wide = []
        for j in range(1, 5):
            two = jnp.where(left, stack[j - 1], stack[j])
            three = jnp.concatenate([two, stack[j + 1]], axis=1).astype(BF16)
            wide.append(dot(three, across[...]).astype(BF16))
        return jnp.concatenate(wide, axis=1)

    shift = 4.0 * threshold[0]
    copies = []

    def finish(start, stop, level):
        rows = slice(start, stop)
        stage[rows, :] = (0.5 * jnp.tanh(level - shift) + 0.5).astype(BF16)
        copy = pltpu.make_async_copy(stage.at[rows, :], out.at[rows, :], sems.at[len(copies)])
        copy.start()
        copies.append(copy)

    upper_rows = columns(0, 1)
    finish(0, SPLIT, dot(down_upper[...], upper_rows))
    both_rows = jnp.concatenate([upper_rows, columns(3, 2)], axis=0)
    middle = SPLIT + 192
    finish(SPLIT, middle, dot(down_lower[: middle - SPLIT, :], both_rows))
    finish(middle, 2 * TILE, dot(down_lower[middle - SPLIT :, :], both_rows))
    for copy in copies:
        copy.wait()


PARAMS = pltpu.CompilerParams(vmem_limit_bytes=48 * 1024 * 1024)
IN_HBM = pl.BlockSpec(memory_space=pltpu.HBM)
IN_VMEM = pl.BlockSpec(memory_space=pltpu.VMEM)
IN_SMEM = pl.BlockSpec(memory_space=pltpu.SMEM)


def spectra(masks, cell_ids, dose, kernels, kernel_weights, owned_counts):
    table = tables()
    operands = [masks, cell_ids.T, dose]
    operands += [jnp.asarray(table[n]) for n in ("forward_cols", "forward_rows")]
    operands += [kernels, kernel_weights, owned_counts]
    in_hbm = [pltpu.with_memory_space_constraint(op, pltpu.HBM) for op in operands]
    return pl.pallas_call(
        spectra_kernel,
        out_shape=(
            jax.ShapeDtypeStruct((COLS, PACKET, LANES), BF16),
            jax.ShapeDtypeStruct((2, NK // 2, NF, LANES), F32),
            pltpu.SMEM((COLS,), jnp.int32),
        ),
        in_specs=[IN_HBM] * len(operands),
        out_specs=(IN_VMEM, IN_VMEM, IN_SMEM),
        scratch_shapes=[
            *[pltpu.VMEM(op.shape, op.dtype) for op in operands[:-2]],
            *[pltpu.SMEM(op.shape, op.dtype) for op in operands[-2:]],
            pltpu.VMEM((16, LANES), F32),
            pltpu.SemaphoreType.DMA((len(operands) + SLOTS - 1,)),
        ],
        compiler_params=PARAMS,
    )(*in_hbm)


def route(packets, starts):
    return pl.pallas_call(
        routing_kernel,
        out_shape=(
            jax.ShapeDtypeStruct((ROWS, OUTGOING, LANES), BF16),
            pltpu.SMEM((WINDOW,), jnp.int32),
        ),
        in_specs=[IN_VMEM, IN_SMEM],
        out_specs=(IN_VMEM, IN_SMEM),
        scratch_shapes=[
            pltpu.VMEM((CELLS + SLOTS, HALF, LANES), F32),
            pltpu.VMEM((COLS * 16, LANES), F32),
            pltpu.VMEM((CELLS + 8, LANES), F32),
            pltpu.VMEM((16, LANES), jnp.int32),
            pltpu.SMEM((16, LANES), jnp.int32),
            pltpu.SMEM((ROWS * 16 + 16,), jnp.int32),
            pltpu.SMEM((16,), jnp.int32),
            pltpu.SemaphoreType.DMA,
        ],
        compiler_params=PARAMS,
    )(packets, starts)


def develop(incoming, place, ker, threshold):
    table = tables()
    names = ("turned", "spread_up", "spread_low", "rest", "rest_mask")
    names += ("inverse_left", "edge_left", "inverse_right", "across", "down_upper", "down_lower")
    constants = [jnp.asarray(table[n]) for n in names]
    return pl.pallas_call(
        develop_kernel,
        out_shape=jax.ShapeDtypeStruct((2 * TILE, 4 * TILE), BF16),
        in_specs=[IN_VMEM, IN_SMEM, IN_VMEM, IN_SMEM, *[IN_VMEM] * len(constants)],
        out_specs=IN_HBM,
        scratch_shapes=[
            pltpu.VMEM((ROWS * 16, LANES), F32),
            pltpu.VMEM((2 * TILE, 4 * TILE), BF16),
            pltpu.SemaphoreType.DMA((3,)),
        ],
        compiler_params=PARAMS,
    )(incoming, place, ker, threshold, *constants)


def local(masks, owned_counts, cell_ids, kernels, kernel_weights, dose, threshold):
    packet, ker, starts = spectra(
        masks, cell_ids, dose, kernels, kernel_weights, owned_counts
    )
    packets = lax.all_to_all(packet, "cols", split_axis=0, concat_axis=0, tiled=True)
    outgoing, place = route(packets, starts)
    incoming = lax.all_to_all(outgoing, "rows", split_axis=0, concat_axis=0, tiled=True)
    return develop(incoming, place, ker, threshold)


def solution(mesh):
    return jax.shard_map(
        local,
        mesh=mesh,
        in_specs=(
            P(("rows", "cols"), None, None),
            P(),
            P(None, "cols"),
            P(),
            P(),
            P("rows", "cols"),
            P(),
        ),
        out_specs=P("rows", "cols"),
        check_vma=False,
    )
```

```python
import functools

import jax
import jax.numpy as jnp
import ml_dtypes
import numpy as np
from jax import lax
from jax.experimental import pallas as pl
from jax.experimental.pallas import tpu as pltpu
from jax.sharding import PartitionSpec as P

REACH = 8
TILE = 384
NF = 32
NK = 16
Q = 64
SLOTS = 6
ROWS = 8
COLS = 16
CELLS = 32
LANES = 128
HALF = NF // 2
EXTRA = 3 * HALF
IDS = EXTRA + SLOTS
DOSES = IDS + 4
PACKET = EXTRA + 16
WINDOW = 4 * 6
NEAR = 6
FAR = 8
MOST = NEAR + FAR
REST = MOST * HALF // 2
OUTGOING = REST + 16
STARTS, SEATS, PLACES = 0, COLS, COLS + ROWS * NEAR
STACK = Q + 2 * REACH
SPLIT = TILE - 2 * REACH
BF16 = jnp.bfloat16
F32 = jnp.float32


def split(table):
    high = table.astype(ml_dtypes.bfloat16)
    low = (table - high.astype(np.float64)).astype(ml_dtypes.bfloat16)
    return high, low


@functools.lru_cache(maxsize=None)
def tables():
    freq = np.arange(NF) - NF // 2
    pixels = np.arange(TILE)
    points = np.arange(Q)
    turn = np.mod(freq[:, None] * pixels[None, :], TILE) * (2.0 * np.pi / TILE)
    forward = np.concatenate([np.cos(turn), np.sin(turn)]) / TILE
    high, low = split(forward)
    forward_rows = np.concatenate([high, low])
    forward_cols = np.ascontiguousarray(forward_rows.T)

    turn = np.mod(points[:, None] * freq[None, :], Q) * (2.0 * np.pi / Q)
    cos, sin = np.cos(turn), np.sin(turn)
    inverse_left = np.concatenate([cos, -sin], axis=1)
    edges = np.concatenate([np.arange(TILE - REACH, TILE), np.arange(REACH)])
    turn = np.mod(edges[:, None] * freq[None, :], TILE) * (2.0 * np.pi / TILE)
    edge_left = np.concatenate([np.cos(turn), -np.sin(turn)], axis=1)
    right = np.zeros((LANES, 2 * LANES))
    for k in range(2):
        re = slice(2 * k * NF, (2 * k + 1) * NF)
        im = slice((2 * k + 1) * NF, (2 * k + 2) * NF)
        out_re = slice(k * LANES, k * LANES + Q)
        out_im = slice(k * LANES + Q, (k + 1) * LANES)
        right[re, out_re], right[re, out_im] = cos.T, sin.T
        right[im, out_re], right[im, out_im] = -sin.T, cos.T

    spread_up = np.zeros((LANES, 4 * LANES))
    spread_low = np.zeros((LANES, 4 * LANES))
    rest = np.zeros((LANES, 2 * LANES))
    for copy in range(4):
        for part in range(2):
            for b in range(NF):
                for tile in range(2):
                    lane = tile * Q + part * NF + b
                    base = tile * 2 * LANES + part * LANES + copy * NF
                    spread_up[lane, base + b] = 1.0
                    if b:
                        spread_low[lane, base + NF - b] = -1.0 if part else 1.0
                rest[part * NF + b, part * LANES + copy * NF + b] = 1.0
            for i in range(1, HALF):
                rest[Q + part * (HALF - 1) + i - 1, part * LANES + copy * NF] = 1.0
        rest[Q + 2 * (HALF - 1), copy * NF + HALF] = 1.0
    rest_mask = np.zeros((HALF, LANES), np.float32)
    rest_mask[0, :Q] = rest_mask[0, Q + 2 * (HALF - 1)] = 1.0
    turned = np.zeros((WINDOW * HALF // 2, WINDOW * HALF // 2))
    for i in range(1, HALF):
        rest_mask[i, Q + i - 1] = rest_mask[i, Q + HALF - 1 + i - 1] = 1.0
        for pair in range(WINDOW // 2):
            turned[pair * HALF + i, pair * HALF + HALF - i] = 1.0

    harmonic = np.arange(Q) - Q // 2
    fine = np.mod(pixels[:, None] * harmonic[None, :], TILE) * (2.0 * np.pi / TILE)
    grid = np.mod(points[:, None] * harmonic[None, :], Q) * (2.0 * np.pi / Q)
    interp = (np.cos(fine) @ np.cos(grid).T + np.sin(fine) @ np.sin(grid).T) / Q
    interp = interp.astype(ml_dtypes.bfloat16).astype(np.float64)

    offsets = np.arange(2 * REACH + 1) - REACH
    taps = np.exp(-offsets * offsets / 32.0)
    taps = taps / taps.sum()

    def blur(out_pixels, in_pixels):
        gap = out_pixels[:, None] - in_pixels[None, :]
        inside = np.abs(gap) <= REACH
        return np.where(inside, taps[np.clip(gap + REACH, 0, 2 * REACH)], 0.0)

    across = np.zeros((4 * Q, TILE))
    for n in range(3):
        across[n * Q : (n + 1) * Q] = (blur(pixels, pixels + (n - 1) * TILE) @ interp).T

    out_rows = np.arange(2 * TILE)
    down = np.zeros((2 * TILE, 2 * STACK))
    down[:, :Q] = blur(out_rows, pixels) @ interp
    down[:, Q : Q + REACH] = blur(out_rows, np.arange(-REACH, 0))
    down[:, STACK : STACK + Q] = blur(out_rows, pixels + TILE) @ interp
    down[:, STACK + Q : STACK + Q + REACH] = blur(out_rows, 2 * TILE + np.arange(REACH))
    assert not down[:SPLIT, STACK:].any()

    bf16 = dict(
        forward_rows=forward_rows,
        forward_cols=forward_cols,
        inverse_left=inverse_left,
        edge_left=edge_left,
        inverse_right=right,
        spread_up=spread_up,
        spread_low=spread_low,
        rest=rest,
        turned=turned,
        across=across,
        down_upper=4.0 * down[:SPLIT, :STACK],
        down_lower=4.0 * down[SPLIT:],
    )
    out = {name: value.astype(ml_dtypes.bfloat16) for name, value in bf16.items()}
    out["rest_mask"] = rest_mask
    return out


def dot(a, b):
    return jnp.dot(a, b, preferred_element_type=F32)


def halves(x):
    high = x.astype(BF16)
    return high, (x - high.astype(F32)).astype(BF16)


def lanes_of(shape):
    return lax.broadcasted_iota(jnp.int32, shape, 1)


def seats(cells, chosen, dest, row):
    count = jnp.int32(0)
    for cell in cells:
        chosen[dest * 16 + count] = cell & (CELLS - 1)
        count = count + ((cell >> 5) == row).astype(jnp.int32)
    return count


def sources(cells, place, at, taken, first):
    for n in range(ROWS + 1):
        taken[n] = jnp.int32(first)
    for n, cell in enumerate(cells):
        source = cell >> 5
        rank = taken[source + 1]
        taken[source + 1] = rank + 1
        place[at + n] = jnp.where(cell >= 0, source * 16 + rank, -1)


def rows_of(dest):
    return [i for i in range(2 * dest - 1, 2 * dest + 3) if 0 <= i < 2 * ROWS]


def window_rows(ids_s, columns):
    cells = []
    for i in range(4):
        tile_row = 2 * lax.axis_index("rows") - 1 + i
        inside = (tile_row >= 0) & (tile_row < 2 * ROWS)
        tile_row = jnp.clip(tile_row, 0, 2 * ROWS - 1)
        cells += [jnp.where(inside, ids_s[j, tile_row], -1) for j in columns]
    return cells


def near_table(ids_s, counts_s, table, chosen, taken):
    row = lax.axis_index("rows")
    start = jnp.int32(0)
    for c in range(COLS):
        table[STARTS + c] = start
        start = start + counts_s[row, c]
    for dest in range(ROWS):
        cells = [ids_s[j, i] for i in rows_of(dest) for j in range(4)]
        count = seats(cells, chosen, dest, row)
        for n in range(NEAR):
            cell = jnp.where(n < count, chosen[dest * 16 + n], CELLS)
            table[SEATS + dest * NEAR + n] = cell
    sources(window_rows(ids_s, range(4)), table, PLACES, taken, 0)


def spectra_kernel(
    mask, ids, dose, fwd_cols, fwd_rows, kernels, weights, counts,
    out, ker, table,
    mask_v, ids_v, dose_v, cols_v, rows_v, kernels_v, weights_s, counts_s,
    ids_s, chosen, taken, extra, sems,
):
    moves = [(ids, ids_s), (counts, counts_s), (fwd_cols, cols_v)]
    moves += [(mask.at[s], mask_v.at[s]) for s in range(SLOTS)]
    moves += [(kernels, kernels_v), (weights, weights_s), (fwd_rows, rows_v)]
    moves += [(ids, ids_v), (dose, dose_v)]
    copies = [
        pltpu.make_async_copy(src, dst, sems.at[i]) for i, (src, dst) in enumerate(moves)
    ]
    for copy in copies:
        copy.start()
    for copy in copies[:2]:
        copy.wait()
    near_table(ids_s, counts_s, table, chosen, taken)
    for copy in copies[2:6]:
        copy.wait()

    left = lanes_of((TILE, LANES)) < Q
    pairs = []
    for slot in range(SLOTS):
        if slot == 3:
            for copy in copies[6:]:
                copy.wait()
            for two in range(NK // 2):
                re, im = [], []
                for k in (2 * two, 2 * two + 1):
                    scale = jnp.sqrt(jnp.full((NF, NF), weights_s[k], F32))
                    re.append(kernels_v[0, k] * scale)
                    im.append(kernels_v[1, k] * scale)
                ker[0, two] = jnp.concatenate([re[0], im[0], re[1], im[1]], axis=1)
                ker[1, two] = jnp.concatenate([-im[0], re[0], -im[1], re[1]], axis=1)
        cols = dot(mask_v[slot], cols_v[...])
        cols = cols + pltpu.roll(cols, Q, 1)
        high = cols.astype(BF16).astype(F32)
        pairs.append(jnp.where(left, high, cols - high).astype(BF16))

    lane = lanes_of((NF, LANES))
    line = lax.broadcasted_iota(jnp.int32, (NF, LANES), 0)
    even = (lane // NF) % 2 == 0
    in_re = lane == line + Q - HALF - 1
    in_im = lane == line + Q - HALF - 1 + HALF - 1
    column = line > HALF
    lane1 = lanes_of((1, LANES))
    blocks, rows = [], []
    for slot in range(SLOTS):
        both = dot(rows_v[...], pairs[slot])
        both = both[:Q] + both[Q:]
        both = both + pltpu.roll(both, Q, 1)
        top, bottom = both[:NF], both[NF:]
        real = top - pltpu.roll(bottom, NF, 1)
        imag = -(bottom + pltpu.roll(top, NF, 1))
        blocks.append(jnp.where(even, real, pltpu.roll(imag, NF, 1)))
        first = jnp.where(column & in_re, jnp.broadcast_to(real[:, 0:1], (NF, LANES)), 0.0)
        second = jnp.where(column & in_im, jnp.broadcast_to(imag[:, 0:1], (NF, LANES)), 0.0)
        turned = jnp.sum(first + second, axis=0, keepdims=True)
        mean = real[HALF : HALF + 1, HALF : HALF + 1]
        mean = jnp.broadcast_to(mean - mean.astype(BF16).astype(F32), (1, LANES))
        turned = jnp.where(lane1 == Q + 2 * (HALF - 1), mean, turned)
        rows.append(jnp.where(lane1 < Q, blocks[slot][HALF : HALF + 1], turned))
    half = lanes_of((HALF, LANES)) < Q
    packed = [
        jnp.where(half, blocks[2 * i][:HALF], blocks[2 * i + 1][:HALF]).astype(BF16)
        for i in range(SLOTS // 2)
    ]
    extra[...] = jnp.zeros_like(extra)
    for slot in range(SLOTS):
        extra[slot : slot + 1, :] = rows[slot]
    extra[IDS - EXTRA : IDS - EXTRA + 4, 0:16] = ids_v[...].astype(F32)
    at = slice(DOSES - EXTRA, DOSES - EXTRA + 2)
    high = dose_v[...].astype(BF16).astype(F32)
    middle = (dose_v[...] - high).astype(BF16).astype(F32)
    extra[at, 4:8] = high
    extra[at, 8:12] = middle
    extra[at, 12:16] = dose_v[...] - high - middle
    packed.append(extra[...].astype(BF16))
    for c in range(COLS):
        for i in range(4):
            out[c, i * HALF : (i + 1) * HALF, :] = packed[i]


def routing_kernel(
    packets, table,
    out, place,
    held, rests, buffer, where_v, where_s, chosen, taken, sem,
):
    row, col = lax.axis_index("rows"), lax.axis_index("cols")
    for c in range(COLS):
        rests[c * 16 : (c + 1) * 16, :] = packets[c, EXTRA : EXTRA + 16, :].astype(F32)

    def rest_of(c):
        return rests[pl.ds(pl.multiple_of(c * 16, 16), 16), :]

    before = rest_of(jnp.maximum(col - 1, 0))
    here = rest_of(col)
    after = rest_of(jnp.minimum(col + 1, COLS - 1))
    line = lax.broadcasted_iota(jnp.int32, (16, LANES), 0)
    first = IDS - EXTRA
    window = jnp.where(
        line == 0, pltpu.roll(before, 16 - first - 3, 0), pltpu.roll(after, 16 - first + 1, 0)
    ).astype(jnp.int32)
    exists = ((line == 0) & (col > 0)) | ((line == 1) & (col < COLS - 1))
    where_v[...] = jnp.where(exists, window, -1)
    copy = pltpu.make_async_copy(where_v, where_s, sem)
    copy.start()

    left = lanes_of((HALF, LANES)) < Q
    for c in range(COLS):
        start = table[STARTS + c]
        for s in range(SLOTS):
            pair = packets[c, (s // 2) * HALF : (s // 2 + 1) * HALF, :].astype(F32)
            moved = pltpu.roll(pair, Q, 1)
            both = jnp.where(left, moved, pair) if s % 2 else jnp.where(left, pair, moved)
            held[start + s] = both
            buffer[pl.ds(start + s, 1), :] = rests[c * 16 + s : c * 16 + s + 1, :]
    held[CELLS] = jnp.zeros((HALF, LANES), F32)
    buffer[CELLS : CELLS + 1, :] = jnp.zeros((1, LANES), F32)

    lane = lanes_of((2, LANES))
    at = slice(DOSES - EXTRA, DOSES - EXTRA + 2)
    doses = jnp.where(
        lane < 16,
        before[at],
        jnp.where(lane < 32, pltpu.roll(here[at], 16, 1), pltpu.roll(after[at], 32, 1)),
    )

    def send(dest, cells, at):
        for n in range(0, len(cells), 2):
            one, two = held[cells[n]], held[cells[n + 1]]
            rows = slice(at + n // 2 * HALF, at + (n // 2 + 1) * HALF)
            out[dest, rows, :] = jnp.where(left, one, two).astype(BF16)

    near = [
        [table[SEATS + dest * NEAR + n] for n in range(NEAR)] for dest in range(ROWS)
    ]
    for dest in range(ROWS):
        send(dest, near[dest], 0)
    copy.wait()
    sources(window_rows(where_s, range(2)), place, 0, taken, NEAR)
    for dest in range(ROWS):
        cells = [where_s[j, i] for i in rows_of(dest) for j in range(2)]
        count = seats(cells, chosen, dest, row)
        cells = [jnp.where(n < count, chosen[dest * 16 + n], CELLS) for n in range(FAR)]
        send(dest, cells, NEAR // 2 * HALF)
        rows = [buffer[pl.ds(cell, 1), :] for cell in near[dest] + cells]
        out[dest, REST : REST + 16, :] = jnp.concatenate(rows + [doses], axis=0).astype(BF16)


def develop_kernel(
    tiles, table, place, ker, threshold, turned, spread_up, spread_low, rest, rest_mask,
    inv_left, edge_left, inv_right, across, down_upper, down_lower,
    out,
    after_rows, stage, sems,
):
    row = lax.axis_index("rows")
    for source in range(ROWS):
        at = slice(source * 16, (source + 1) * 16)
        after_rows[at, :] = tiles[source, REST : REST + 16, :].astype(F32)
    left = lanes_of((HALF, LANES)) < Q
    held, rests = [], []
    for t in range(0, WINDOW, 2):
        both = []
        for n in (t, t + 1):
            i, j = n // 6, n % 6
            found = table[PLACES + 4 * i + j - 1] if 1 <= j < 5 else place[2 * i + j // 5]
            here = jnp.maximum(found, 0)
            rank = here & 15
            at = pl.multiple_of((rank >> 1) * HALF, HALF)
            pair = tiles[here >> 4, pl.ds(at, HALF), :].astype(F32)
            tile = jnp.where((rank & 1) == (n & 1), pair, pltpu.roll(pair, Q, 1))
            both.append(jnp.where(found >= 0, tile, 0.0))
            line = jnp.where(found >= 0, after_rows[pl.ds(here, 1), :], 0.0)
            rests.append(jnp.broadcast_to(line, (HALF, LANES)) * rest_mask[...])
        held.append(jnp.where(left, both[0], both[1]).astype(BF16))
    held = jnp.concatenate(held, axis=0)
    upper = dot(held, spread_up[...])
    lower = dot(dot(turned[...], held).astype(BF16), spread_low[...])
    rests = dot(jnp.concatenate(rests, axis=0).astype(BF16), rest[...])

    def doses(source):
        info = after_rows[pl.ds(pl.multiple_of(source * 16, 16), 16), :][MOST:]
        return info + pltpu.roll(info, LANES - 4, 1) + pltpu.roll(info, LANES - 8, 1)

    own = doses(row)
    above = doses(jnp.maximum(row - 1, 0))
    below = doses(jnp.minimum(row + 1, ROWS - 1))

    def picture(i, j):
        whole_tile = i in (1, 2)
        m, t = 3 * i + j // 2, 6 * i + j
        a, r = slice(m * HALF, (m + 1) * HALF), slice(t * HALF, (t + 1) * HALF)
        re = slice((j % 2) * 2 * LANES, (j % 2) * 2 * LANES + LANES)
        im = slice(re.stop, re.stop + LANES)
        real = jnp.concatenate([upper[a, re], lower[a, re] + rests[r, :LANES]], axis=0)
        imag = jnp.concatenate([upper[a, im], lower[a, im] + rests[r, LANES:]], axis=0)
        prods = []
        for two in range(NK // 2):
            ka, kb = ker[0, two], ker[1, two]
            prod = jnp.concatenate([ka * real + kb * imag, ka * imag - kb * real], axis=0)
            prods.append(prod.astype(BF16))
        prod = jnp.concatenate(prods, axis=1)
        half = dot(inv_left[...] if whole_tile else edge_left[...], prod)
        if not whole_tile:
            half = half[:REACH] if i == 0 else half[REACH:]
        return jnp.concatenate(
            [half[:, n * LANES : (n + 1) * LANES] for n in range(NK // 2)], axis=0
        ).astype(BF16)

    def intensity(halfway):
        field = dot(halfway, inv_right[...])
        power = field * field
        power = power[:, :LANES] + power[:, LANES:]
        height = power.shape[0] // (NK // 2)
        total = power[:height]
        for n in range(1, NK // 2):
            total = total + power[n * height : (n + 1) * height]
        return total + pltpu.roll(total, Q, 1)

    lane_of = [7] + [20 + j for j in range(4)] + [36]
    dose_rows = [above[1:2], own[0:1], own[1:2], below[0:1]]
    left = lanes_of((STACK, LANES)) < Q

    images = {}
    for group in ((0, 3), (1,), (2,)):
        halfway = {(i, j): picture(i, j) for i in group for j in range(6)}
        for i in group:
            for j in range(6):
                scale = dose_rows[i][:, lane_of[j] : lane_of[j] + 1]
                images[i, j] = intensity(halfway[i, j]) * scale

    def columns(strip, tile):
        none = jnp.zeros((REACH, LANES), F32)
        stack = [
            jnp.concatenate([images[tile, j], images[strip, j], none], axis=0) for j in range(6)
        ]
        wide = []
        for j in range(1, 5):
            two = jnp.where(left, stack[j - 1], stack[j])
            three = jnp.concatenate([two, stack[j + 1]], axis=1).astype(BF16)
            wide.append(dot(three, across[...]).astype(BF16))
        return jnp.concatenate(wide, axis=1)

    shift = 4.0 * threshold[0]
    copies = []

    def finish(start, stop, level):
        rows = slice(start, stop)
        stage[rows, :] = (0.5 * jnp.tanh(level - shift) + 0.5).astype(BF16)
        copy = pltpu.make_async_copy(stage.at[rows, :], out.at[rows, :], sems.at[len(copies)])
        copy.start()
        copies.append(copy)

    upper_rows = columns(0, 1)
    finish(0, SPLIT, dot(down_upper[...], upper_rows))
    both_rows = jnp.concatenate([upper_rows, columns(3, 2)], axis=0)
    middle = SPLIT + 192
    finish(SPLIT, middle, dot(down_lower[: middle - SPLIT, :], both_rows))
    finish(middle, 2 * TILE, dot(down_lower[middle - SPLIT :, :], both_rows))
    for copy in copies:
        copy.wait()


PARAMS = pltpu.CompilerParams(vmem_limit_bytes=48 * 1024 * 1024)
IN_HBM = pl.BlockSpec(memory_space=pltpu.HBM)
IN_VMEM = pl.BlockSpec(memory_space=pltpu.VMEM)
IN_SMEM = pl.BlockSpec(memory_space=pltpu.SMEM)


def spectra(masks, cell_ids, dose, kernels, kernel_weights, owned_counts):
    table = tables()
    operands = [masks, cell_ids.T, dose]
    operands += [jnp.asarray(table[n]) for n in ("forward_cols", "forward_rows")]
    operands += [kernels, kernel_weights, owned_counts]
    in_hbm = [pltpu.with_memory_space_constraint(op, pltpu.HBM) for op in operands]
    return pl.pallas_call(
        spectra_kernel,
        out_shape=(
            jax.ShapeDtypeStruct((COLS, PACKET, LANES), BF16),
            jax.ShapeDtypeStruct((2, NK // 2, NF, LANES), F32),
            pltpu.SMEM((PLACES + 16,), jnp.int32),
        ),
        in_specs=[IN_HBM] * len(operands),
        out_specs=(IN_VMEM, IN_VMEM, IN_SMEM),
        scratch_shapes=[
            *[pltpu.VMEM(op.shape, op.dtype) for op in operands[:-2]],
            *[pltpu.SMEM(op.shape, op.dtype) for op in operands[-2:]],
            pltpu.SMEM((4, 2 * ROWS), jnp.int32),
            pltpu.SMEM((ROWS * 16 + 16,), jnp.int32),
            pltpu.SMEM((16,), jnp.int32),
            pltpu.VMEM((16, LANES), F32),
            pltpu.SemaphoreType.DMA((len(operands) + SLOTS,)),
        ],
        compiler_params=PARAMS,
    )(*in_hbm)


def route(packets, seating):
    return pl.pallas_call(
        routing_kernel,
        out_shape=(
            jax.ShapeDtypeStruct((ROWS, OUTGOING, LANES), BF16),
            pltpu.SMEM((8,), jnp.int32),
        ),
        in_specs=[IN_VMEM, IN_SMEM],
        out_specs=(IN_VMEM, IN_SMEM),
        scratch_shapes=[
            pltpu.VMEM((CELLS + SLOTS, HALF, LANES), F32),
            pltpu.VMEM((COLS * 16, LANES), F32),
            pltpu.VMEM((CELLS + 8, LANES), F32),
            pltpu.VMEM((16, LANES), jnp.int32),
            pltpu.SMEM((16, LANES), jnp.int32),
            pltpu.SMEM((ROWS * 16 + 16,), jnp.int32),
            pltpu.SMEM((16,), jnp.int32),
            pltpu.SemaphoreType.DMA,
        ],
        compiler_params=PARAMS,
    )(packets, seating)


def develop(incoming, seating, place, ker, threshold):
    table = tables()
    names = ("turned", "spread_up", "spread_low", "rest", "rest_mask")
    names += ("inverse_left", "edge_left", "inverse_right", "across", "down_upper", "down_lower")
    constants = [jnp.asarray(table[n]) for n in names]
    return pl.pallas_call(
        develop_kernel,
        out_shape=jax.ShapeDtypeStruct((2 * TILE, 4 * TILE), BF16),
        in_specs=[IN_VMEM, IN_SMEM, IN_SMEM, IN_VMEM, IN_SMEM, *[IN_VMEM] * len(constants)],
        out_specs=IN_HBM,
        scratch_shapes=[
            pltpu.VMEM((ROWS * 16, LANES), F32),
            pltpu.VMEM((2 * TILE, 4 * TILE), BF16),
            pltpu.SemaphoreType.DMA((3,)),
        ],
        compiler_params=PARAMS,
    )(incoming, seating, place, ker, threshold, *constants)


def local(masks, owned_counts, cell_ids, kernels, kernel_weights, dose, threshold):
    packet, ker, seating = spectra(
        masks, cell_ids, dose, kernels, kernel_weights, owned_counts
    )
    packets = lax.all_to_all(packet, "cols", split_axis=0, concat_axis=0, tiled=True)
    outgoing, place = route(packets, seating)
    incoming = lax.all_to_all(outgoing, "rows", split_axis=0, concat_axis=0, tiled=True)
    return develop(incoming, seating, place, ker, threshold)


def solution(mesh):
    return jax.shard_map(
        local,
        mesh=mesh,
        in_specs=(
            P(("rows", "cols"), None, None),
            P(),
            P(None, "cols"),
            P(),
            P(),
            P("rows", "cols"),
            P(),
        ),
        out_specs=P("rows", "cols"),
        check_vma=False,
    )
```

```python
import functools

import jax
import jax.numpy as jnp
import ml_dtypes
import numpy as np
from jax import lax
from jax.experimental import pallas as pl
from jax.experimental.pallas import tpu as pltpu
from jax.sharding import PartitionSpec as P

REACH = 8
TILE = 384
NF = 32
NK = 16
Q = 64
SLOTS = 6
ROWS = 8
COLS = 16
CELLS = 32
LANES = 128
HALF = NF // 2
EXTRA = 3 * HALF
IDS = EXTRA + SLOTS
DOSES = IDS + 4
PACKET = EXTRA + 16
WINDOW = 4 * 6
NEAR = 6
FAR = 8
MOST = NEAR + FAR
REST = MOST * HALF // 2
OUTGOING = REST + 16
STARTS, SEATS, PLACES = 0, COLS, COLS + ROWS * NEAR
STACK = Q + 2 * REACH
SPLIT = TILE - 2 * REACH
BF16 = jnp.bfloat16
F32 = jnp.float32


def split(table):
    high = table.astype(ml_dtypes.bfloat16)
    low = (table - high.astype(np.float64)).astype(ml_dtypes.bfloat16)
    return high, low


@functools.lru_cache(maxsize=None)
def tables():
    freq = np.arange(NF) - NF // 2
    pixels = np.arange(TILE)
    points = np.arange(Q)
    turn = np.mod(freq[:, None] * pixels[None, :], TILE) * (2.0 * np.pi / TILE)
    forward = np.concatenate([np.cos(turn), np.sin(turn)]) / TILE
    high, low = split(forward)
    forward_rows = np.concatenate([high, low])
    forward_cols = np.ascontiguousarray(forward_rows.T)

    turn = np.mod(points[:, None] * freq[None, :], Q) * (2.0 * np.pi / Q)
    cos, sin = np.cos(turn), np.sin(turn)
    inverse_left = np.concatenate([cos, -sin], axis=1)
    edges = np.concatenate([np.arange(TILE - REACH, TILE), np.arange(REACH)])
    turn = np.mod(edges[:, None] * freq[None, :], TILE) * (2.0 * np.pi / TILE)
    edge_left = np.concatenate([np.cos(turn), -np.sin(turn)], axis=1)
    right = np.zeros((LANES, 2 * LANES))
    for k in range(2):
        re = slice(2 * k * NF, (2 * k + 1) * NF)
        im = slice((2 * k + 1) * NF, (2 * k + 2) * NF)
        out_re = slice(k * LANES, k * LANES + Q)
        out_im = slice(k * LANES + Q, (k + 1) * LANES)
        right[re, out_re], right[re, out_im] = cos.T, sin.T
        right[im, out_re], right[im, out_im] = -sin.T, cos.T

    spread_up = np.zeros((LANES, 4 * LANES))
    spread_low = np.zeros((LANES, 4 * LANES))
    rest = np.zeros((LANES, 2 * LANES))
    for copy in range(4):
        for part in range(2):
            for b in range(NF):
                for tile in range(2):
                    lane = tile * Q + part * NF + b
                    base = tile * 2 * LANES + part * LANES + copy * NF
                    spread_up[lane, base + b] = 1.0
                    if b:
                        spread_low[lane, base + NF - b] = -1.0 if part else 1.0
                rest[part * NF + b, part * LANES + copy * NF + b] = 1.0
            for i in range(1, HALF):
                rest[Q + part * (HALF - 1) + i - 1, part * LANES + copy * NF] = 1.0
        rest[Q + 2 * (HALF - 1), copy * NF + HALF] = 1.0
    rest_mask = np.zeros((HALF, LANES), np.float32)
    rest_mask[0, :Q] = rest_mask[0, Q + 2 * (HALF - 1)] = 1.0
    turned = np.zeros((WINDOW * HALF // 2, WINDOW * HALF // 2))
    for i in range(1, HALF):
        rest_mask[i, Q + i - 1] = rest_mask[i, Q + HALF - 1 + i - 1] = 1.0
        for pair in range(WINDOW // 2):
            turned[pair * HALF + i, pair * HALF + HALF - i] = 1.0

    harmonic = np.arange(Q) - Q // 2
    fine = np.mod(pixels[:, None] * harmonic[None, :], TILE) * (2.0 * np.pi / TILE)
    grid = np.mod(points[:, None] * harmonic[None, :], Q) * (2.0 * np.pi / Q)
    interp = (np.cos(fine) @ np.cos(grid).T + np.sin(fine) @ np.sin(grid).T) / Q
    interp = interp.astype(ml_dtypes.bfloat16).astype(np.float64)

    offsets = np.arange(2 * REACH + 1) - REACH
    taps = np.exp(-offsets * offsets / 32.0)
    taps = taps / taps.sum()

    def blur(out_pixels, in_pixels):
        gap = out_pixels[:, None] - in_pixels[None, :]
        inside = np.abs(gap) <= REACH
        return np.where(inside, taps[np.clip(gap + REACH, 0, 2 * REACH)], 0.0)

    across = np.zeros((4 * Q, TILE))
    for n in range(3):
        across[n * Q : (n + 1) * Q] = (blur(pixels, pixels + (n - 1) * TILE) @ interp).T

    out_rows = np.arange(2 * TILE)
    down = np.zeros((2 * TILE, 2 * STACK))
    down[:, :Q] = blur(out_rows, pixels) @ interp
    down[:, Q : Q + REACH] = blur(out_rows, np.arange(-REACH, 0))
    down[:, STACK : STACK + Q] = blur(out_rows, pixels + TILE) @ interp
    down[:, STACK + Q : STACK + Q + REACH] = blur(out_rows, 2 * TILE + np.arange(REACH))
    assert not down[:SPLIT, STACK:].any()

    bf16 = dict(
        forward_rows=forward_rows,
        forward_cols=forward_cols,
        inverse_left=inverse_left,
        edge_left=edge_left,
        inverse_right=right,
        spread_up=spread_up,
        spread_low=spread_low,
        rest=rest,
        turned=turned,
        across=across,
        down_upper=4.0 * down[:SPLIT, :STACK],
        down_lower=4.0 * down[SPLIT:],
    )
    out = {name: value.astype(ml_dtypes.bfloat16) for name, value in bf16.items()}
    out["rest_mask"] = rest_mask
    return out


def dot(a, b):
    return jnp.dot(a, b, preferred_element_type=F32)


def halves(x):
    high = x.astype(BF16)
    return high, (x - high.astype(F32)).astype(BF16)


def lanes_of(shape):
    return lax.broadcasted_iota(jnp.int32, shape, 1)


def seats(cells, chosen, dest, row):
    count = jnp.int32(0)
    for cell in cells:
        chosen[dest * 16 + count] = cell & (CELLS - 1)
        count = count + ((cell >> 5) == row).astype(jnp.int32)
    return count


def sources(cells, place, at, taken, first):
    for n in range(ROWS + 1):
        taken[n] = jnp.int32(first)
    for n, cell in enumerate(cells):
        source = cell >> 5
        rank = taken[source + 1]
        taken[source + 1] = rank + 1
        place[at + n] = jnp.where(cell >= 0, source * 16 + rank, -1)


def rows_of(dest):
    return [i for i in range(2 * dest - 1, 2 * dest + 3) if 0 <= i < 2 * ROWS]


def window_rows(ids_s, columns):
    cells = []
    for i in range(4):
        tile_row = 2 * lax.axis_index("rows") - 1 + i
        inside = (tile_row >= 0) & (tile_row < 2 * ROWS)
        tile_row = jnp.clip(tile_row, 0, 2 * ROWS - 1)
        cells += [jnp.where(inside, ids_s[j, tile_row], -1) for j in columns]
    return cells


def near_table(ids_s, counts_s, table, chosen, taken):
    row = lax.axis_index("rows")
    start = jnp.int32(0)
    for c in range(COLS):
        table[STARTS + c] = start
        start = start + counts_s[row, c]
    for dest in range(ROWS):
        cells = [ids_s[j, i] for i in rows_of(dest) for j in range(4)]
        count = seats(cells, chosen, dest, row)
        for n in range(NEAR):
            cell = jnp.where(n < count, chosen[dest * 16 + n], CELLS)
            table[SEATS + dest * NEAR + n] = cell
    sources(window_rows(ids_s, range(4)), table, PLACES, taken, 0)


def spectra_kernel(
    mask, ids, dose, fwd_cols, fwd_rows, kernels, weights, counts,
    out, ker, table,
    mask_v, ids_v, dose_v, cols_v, rows_v, kernels_v, weights_s, counts_s,
    ids_s, chosen, taken, extra, sems,
):
    moves = [(ids, ids_s), (counts, counts_s), (fwd_rows, rows_v)]
    moves += [(mask.at[s], mask_v.at[s]) for s in range(SLOTS)]
    moves += [(kernels, kernels_v), (weights, weights_s), (fwd_cols, cols_v)]
    moves += [(ids, ids_v), (dose, dose_v)]
    copies = [
        pltpu.make_async_copy(src, dst, sems.at[i]) for i, (src, dst) in enumerate(moves)
    ]
    for copy in copies:
        copy.start()
    for copy in copies[:2]:
        copy.wait()
    near_table(ids_s, counts_s, table, chosen, taken)
    for copy in copies[2:6]:
        copy.wait()

    pairs = []
    for slot in range(SLOTS):
        if slot == 3:
            for copy in copies[6:]:
                copy.wait()
            for two in range(NK // 2):
                re, im = [], []
                for k in (2 * two, 2 * two + 1):
                    scale = jnp.sqrt(jnp.full((NF, NF), weights_s[k], F32))
                    re.append(kernels_v[0, k] * scale)
                    im.append(kernels_v[1, k] * scale)
                ker[0, two] = jnp.concatenate([re[0], im[0], re[1], im[1]], axis=1)
                ker[1, two] = jnp.concatenate([-im[0], re[0], -im[1], re[1]], axis=1)
        cols = dot(rows_v[...], mask_v[slot])
        high, low = halves(cols[:Q] + cols[Q:])
        pairs.append(jnp.concatenate([high, low], axis=0))

    lane = lanes_of((NF, LANES))
    line = lax.broadcasted_iota(jnp.int32, (NF, LANES), 0)
    even = (lane // NF) % 2 == 0
    in_re = lane == line + Q - HALF - 1
    in_im = lane == line + Q - HALF - 1 + HALF - 1
    column = line > HALF
    lane1 = lanes_of((1, LANES))
    blocks, rows = [], []
    for slot in range(SLOTS):
        both = dot(pairs[slot], cols_v[...])
        both = both[:Q] + both[Q:]
        both = both + pltpu.roll(both, Q, 1)
        top, bottom = both[:NF], both[NF:]
        real = top - pltpu.roll(bottom, NF, 1)
        imag = -(bottom + pltpu.roll(top, NF, 1))
        blocks.append(jnp.where(even, real, pltpu.roll(imag, NF, 1)))
        first = jnp.where(column & in_re, jnp.broadcast_to(real[:, 0:1], (NF, LANES)), 0.0)
        second = jnp.where(column & in_im, jnp.broadcast_to(imag[:, 0:1], (NF, LANES)), 0.0)
        turned = jnp.sum(first + second, axis=0, keepdims=True)
        mean = real[HALF : HALF + 1, HALF : HALF + 1]
        mean = jnp.broadcast_to(mean - mean.astype(BF16).astype(F32), (1, LANES))
        turned = jnp.where(lane1 == Q + 2 * (HALF - 1), mean, turned)
        rows.append(jnp.where(lane1 < Q, blocks[slot][HALF : HALF + 1], turned))
    half = lanes_of((HALF, LANES)) < Q
    packed = [
        jnp.where(half, blocks[2 * i][:HALF], blocks[2 * i + 1][:HALF]).astype(BF16)
        for i in range(SLOTS // 2)
    ]
    extra[...] = jnp.zeros_like(extra)
    for slot in range(SLOTS):
        extra[slot : slot + 1, :] = rows[slot]
    extra[IDS - EXTRA : IDS - EXTRA + 4, 0:16] = ids_v[...].astype(F32)
    at = slice(DOSES - EXTRA, DOSES - EXTRA + 2)
    high = dose_v[...].astype(BF16).astype(F32)
    middle = (dose_v[...] - high).astype(BF16).astype(F32)
    extra[at, 4:8] = high
    extra[at, 8:12] = middle
    extra[at, 12:16] = dose_v[...] - high - middle
    packed.append(extra[...].astype(BF16))
    for c in range(COLS):
        for i in range(4):
            out[c, i * HALF : (i + 1) * HALF, :] = packed[i]


def routing_kernel(
    packets, table,
    out, place,
    held, rests, buffer, where_v, where_s, chosen, taken, sem,
):
    row, col = lax.axis_index("rows"), lax.axis_index("cols")
    def rest_of(c):
        return packets[c, EXTRA : EXTRA + 16, :].astype(F32)

    before = rest_of(jnp.maximum(col - 1, 0))
    after = rest_of(jnp.minimum(col + 1, COLS - 1))
    line = lax.broadcasted_iota(jnp.int32, (16, LANES), 0)
    first = IDS - EXTRA
    window = jnp.where(
        line == 0, pltpu.roll(before, 16 - first - 3, 0), pltpu.roll(after, 16 - first + 1, 0)
    ).astype(jnp.int32)
    exists = ((line == 0) & (col > 0)) | ((line == 1) & (col < COLS - 1))
    where_v[...] = jnp.where(exists, window, -1)
    copy = pltpu.make_async_copy(where_v, where_s, sem)
    copy.start()

    here = rest_of(col)
    for c in range(COLS):
        rests[c * 16 : (c + 1) * 16, :] = rest_of(c)
    left = lanes_of((HALF, LANES)) < Q
    for c in range(COLS):
        start = table[STARTS + c]
        for s in range(SLOTS):
            pair = packets[c, (s // 2) * HALF : (s // 2 + 1) * HALF, :].astype(F32)
            moved = pltpu.roll(pair, Q, 1)
            both = jnp.where(left, moved, pair) if s % 2 else jnp.where(left, pair, moved)
            held[start + s] = both
            buffer[pl.ds(start + s, 1), :] = rests[c * 16 + s : c * 16 + s + 1, :]
    held[CELLS] = jnp.zeros((HALF, LANES), F32)
    buffer[CELLS : CELLS + 1, :] = jnp.zeros((1, LANES), F32)

    lane = lanes_of((2, LANES))
    at = slice(DOSES - EXTRA, DOSES - EXTRA + 2)
    doses = jnp.where(
        lane < 16,
        before[at],
        jnp.where(lane < 32, pltpu.roll(here[at], 16, 1), pltpu.roll(after[at], 32, 1)),
    )

    def send(dest, cells, at):
        for n in range(0, len(cells), 2):
            one, two = held[cells[n]], held[cells[n + 1]]
            rows = slice(at + n // 2 * HALF, at + (n // 2 + 1) * HALF)
            out[dest, rows, :] = jnp.where(left, one, two).astype(BF16)

    near = [
        [table[SEATS + dest * NEAR + n] for n in range(NEAR)] for dest in range(ROWS)
    ]
    for dest in range(ROWS):
        send(dest, near[dest], 0)
    copy.wait()
    sources(window_rows(where_s, range(2)), place, 0, taken, NEAR)
    for dest in range(ROWS):
        cells = [where_s[j, i] for i in rows_of(dest) for j in range(2)]
        count = seats(cells, chosen, dest, row)
        cells = [jnp.where(n < count, chosen[dest * 16 + n], CELLS) for n in range(FAR)]
        send(dest, cells, NEAR // 2 * HALF)
        rows = [buffer[pl.ds(cell, 1), :] for cell in near[dest] + cells]
        out[dest, REST : REST + 16, :] = jnp.concatenate(rows + [doses], axis=0).astype(BF16)


def develop_kernel(
    tiles, table, place, ker, threshold, turned, spread_up, spread_low, rest, rest_mask,
    inv_left, edge_left, inv_right, across, down_upper, down_lower,
    out,
    after_rows, stage, sems,
):
    row = lax.axis_index("rows")
    for source in range(ROWS):
        at = slice(source * 16, (source + 1) * 16)
        after_rows[at, :] = tiles[source, REST : REST + 16, :].astype(F32)
    left = lanes_of((HALF, LANES)) < Q
    held, rests = [], []
    for t in range(0, WINDOW, 2):
        both = []
        for n in (t, t + 1):
            i, j = n // 6, n % 6
            found = table[PLACES + 4 * i + j - 1] if 1 <= j < 5 else place[2 * i + j // 5]
            here = jnp.maximum(found, 0)
            rank = here & 15
            at = pl.multiple_of((rank >> 1) * HALF, HALF)
            pair = tiles[here >> 4, pl.ds(at, HALF), :].astype(F32)
            tile = jnp.where((rank & 1) == (n & 1), pair, pltpu.roll(pair, Q, 1))
            both.append(jnp.where(found >= 0, tile, 0.0))
            line = jnp.where(found >= 0, after_rows[pl.ds(here, 1), :], 0.0)
            rests.append(jnp.broadcast_to(line, (HALF, LANES)) * rest_mask[...])
        held.append(jnp.where(left, both[0], both[1]).astype(BF16))
    held = jnp.concatenate(held, axis=0)
    upper = dot(held, spread_up[...])
    lower = dot(dot(turned[...], held).astype(BF16), spread_low[...])
    rests = dot(jnp.concatenate(rests, axis=0).astype(BF16), rest[...])

    def doses(source):
        info = after_rows[pl.ds(pl.multiple_of(source * 16, 16), 16), :][MOST:]
        return info + pltpu.roll(info, LANES - 4, 1) + pltpu.roll(info, LANES - 8, 1)

    own = doses(row)
    above = doses(jnp.maximum(row - 1, 0))
    below = doses(jnp.minimum(row + 1, ROWS - 1))

    def picture(i, j):
        whole_tile = i in (1, 2)
        m, t = 3 * i + j // 2, 6 * i + j
        a, r = slice(m * HALF, (m + 1) * HALF), slice(t * HALF, (t + 1) * HALF)
        re = slice((j % 2) * 2 * LANES, (j % 2) * 2 * LANES + LANES)
        im = slice(re.stop, re.stop + LANES)
        real = jnp.concatenate([upper[a, re], lower[a, re] + rests[r, :LANES]], axis=0)
        imag = jnp.concatenate([upper[a, im], lower[a, im] + rests[r, LANES:]], axis=0)
        prods = []
        for two in range(NK // 2):
            ka, kb = ker[0, two], ker[1, two]
            prod = jnp.concatenate([ka * real + kb * imag, ka * imag - kb * real], axis=0)
            prods.append(prod.astype(BF16))
        prod = jnp.concatenate(prods, axis=1)
        half = dot(inv_left[...] if whole_tile else edge_left[...], prod)
        if not whole_tile:
            half = half[:REACH] if i == 0 else half[REACH:]
        return jnp.concatenate(
            [half[:, n * LANES : (n + 1) * LANES] for n in range(NK // 2)], axis=0
        ).astype(BF16)

    def intensity(halfway):
        field = dot(halfway, inv_right[...])
        power = field * field
        power = power[:, :LANES] + power[:, LANES:]
        height = power.shape[0] // (NK // 2)
        total = power[:height]
        for n in range(1, NK // 2):
            total = total + power[n * height : (n + 1) * height]
        return total + pltpu.roll(total, Q, 1)

    lane_of = [7] + [20 + j for j in range(4)] + [36]
    dose_rows = [above[1:2], own[0:1], own[1:2], below[0:1]]
    left = lanes_of((STACK, LANES)) < Q

    images = {}
    for group in ((0, 3), (1,), (2,)):
        halfway = {(i, j): picture(i, j) for i in group for j in range(6)}
        for i in group:
            for j in range(6):
                scale = dose_rows[i][:, lane_of[j] : lane_of[j] + 1]
                images[i, j] = intensity(halfway[i, j]) * scale

    def columns(strip, tile):
        none = jnp.zeros((REACH, LANES), F32)
        stack = [
            jnp.concatenate([images[tile, j], images[strip, j], none], axis=0) for j in range(6)
        ]
        wide = []
        for j in range(1, 5):
            two = jnp.where(left, stack[j - 1], stack[j])
            three = jnp.concatenate([two, stack[j + 1]], axis=1).astype(BF16)
            wide.append(dot(three, across[...]).astype(BF16))
        return jnp.concatenate(wide, axis=1)

    shift = 4.0 * threshold[0]
    copies = []

    def finish(start, stop, level):
        rows = slice(start, stop)
        stage[rows, :] = (0.5 * jnp.tanh(level - shift) + 0.5).astype(BF16)
        copy = pltpu.make_async_copy(stage.at[rows, :], out.at[rows, :], sems.at[len(copies)])
        copy.start()
        copies.append(copy)

    upper_rows = columns(0, 1)
    finish(0, SPLIT, dot(down_upper[...], upper_rows))
    both_rows = jnp.concatenate([upper_rows, columns(3, 2)], axis=0)
    middle = SPLIT + 192
    finish(SPLIT, middle, dot(down_lower[: middle - SPLIT, :], both_rows))
    finish(middle, 2 * TILE, dot(down_lower[middle - SPLIT :, :], both_rows))
    for copy in copies:
        copy.wait()


PARAMS = pltpu.CompilerParams(vmem_limit_bytes=48 * 1024 * 1024)
IN_HBM = pl.BlockSpec(memory_space=pltpu.HBM)
IN_VMEM = pl.BlockSpec(memory_space=pltpu.VMEM)
IN_SMEM = pl.BlockSpec(memory_space=pltpu.SMEM)


def spectra(masks, cell_ids, dose, kernels, kernel_weights, owned_counts):
    table = tables()
    operands = [masks, cell_ids.T, dose]
    operands += [jnp.asarray(table[n]) for n in ("forward_cols", "forward_rows")]
    operands += [kernels, kernel_weights, owned_counts]
    in_hbm = [pltpu.with_memory_space_constraint(op, pltpu.HBM) for op in operands]
    return pl.pallas_call(
        spectra_kernel,
        out_shape=(
            jax.ShapeDtypeStruct((COLS, PACKET, LANES), BF16),
            jax.ShapeDtypeStruct((2, NK // 2, NF, LANES), F32),
            pltpu.SMEM((PLACES + 16,), jnp.int32),
        ),
        in_specs=[IN_HBM] * len(operands),
        out_specs=(IN_VMEM, IN_VMEM, IN_SMEM),
        scratch_shapes=[
            *[pltpu.VMEM(op.shape, op.dtype) for op in operands[:-2]],
            *[pltpu.SMEM(op.shape, op.dtype) for op in operands[-2:]],
            pltpu.SMEM((4, 2 * ROWS), jnp.int32),
            pltpu.SMEM((ROWS * 16 + 16,), jnp.int32),
            pltpu.SMEM((16,), jnp.int32),
            pltpu.VMEM((16, LANES), F32),
            pltpu.SemaphoreType.DMA((len(operands) + SLOTS,)),
        ],
        compiler_params=PARAMS,
    )(*in_hbm)


def route(packets, seating):
    return pl.pallas_call(
        routing_kernel,
        out_shape=(
            jax.ShapeDtypeStruct((ROWS, OUTGOING, LANES), BF16),
            pltpu.SMEM((8,), jnp.int32),
        ),
        in_specs=[IN_VMEM, IN_SMEM],
        out_specs=(IN_VMEM, IN_SMEM),
        scratch_shapes=[
            pltpu.VMEM((CELLS + SLOTS, HALF, LANES), F32),
            pltpu.VMEM((COLS * 16, LANES), F32),
            pltpu.VMEM((CELLS + 8, LANES), F32),
            pltpu.VMEM((16, LANES), jnp.int32),
            pltpu.SMEM((16, LANES), jnp.int32),
            pltpu.SMEM((ROWS * 16 + 16,), jnp.int32),
            pltpu.SMEM((16,), jnp.int32),
            pltpu.SemaphoreType.DMA,
        ],
        compiler_params=PARAMS,
    )(packets, seating)


def develop(incoming, seating, place, ker, threshold):
    table = tables()
    names = ("turned", "spread_up", "spread_low", "rest", "rest_mask")
    names += ("inverse_left", "edge_left", "inverse_right", "across", "down_upper", "down_lower")
    constants = [jnp.asarray(table[n]) for n in names]
    return pl.pallas_call(
        develop_kernel,
        out_shape=jax.ShapeDtypeStruct((2 * TILE, 4 * TILE), BF16),
        in_specs=[IN_VMEM, IN_SMEM, IN_SMEM, IN_VMEM, IN_SMEM, *[IN_VMEM] * len(constants)],
        out_specs=IN_HBM,
        scratch_shapes=[
            pltpu.VMEM((ROWS * 16, LANES), F32),
            pltpu.VMEM((2 * TILE, 4 * TILE), BF16),
            pltpu.SemaphoreType.DMA((3,)),
        ],
        compiler_params=PARAMS,
    )(incoming, seating, place, ker, threshold, *constants)


def local(masks, owned_counts, cell_ids, kernels, kernel_weights, dose, threshold):
    packet, ker, seating = spectra(
        masks, cell_ids, dose, kernels, kernel_weights, owned_counts
    )
    packets = lax.all_to_all(packet, "cols", split_axis=0, concat_axis=0, tiled=True)
    outgoing, place = route(packets, seating)
    incoming = lax.all_to_all(outgoing, "rows", split_axis=0, concat_axis=0, tiled=True)
    return develop(incoming, seating, place, ker, threshold)


def solution(mesh):
    return jax.shard_map(
        local,
        mesh=mesh,
        in_specs=(
            P(("rows", "cols"), None, None),
            P(),
            P(None, "cols"),
            P(),
            P(),
            P("rows", "cols"),
            P(),
        ),
        out_specs=P("rows", "cols"),
        check_vma=False,
    )
```

```python
import functools

import jax
import jax.numpy as jnp
import ml_dtypes
import numpy as np
from jax import lax
from jax.experimental import pallas as pl
from jax.experimental.pallas import tpu as pltpu
from jax.sharding import PartitionSpec as P

REACH = 8
TILE = 384
NF = 32
NK = 16
Q = 64
SLOTS = 6
ROWS = 8
COLS = 16
CELLS = 32
LANES = 128
HALF = NF // 2
EXTRA = 3 * HALF
IDS = EXTRA + SLOTS
DOSES = IDS + 4
PACKET = EXTRA + 16
WINDOW = 4 * 6
NEAR = 6
FAR = 8
MOST = NEAR + FAR
REST = MOST * HALF // 2
OUTGOING = REST + 16
STARTS, SEATS, PLACES = 0, COLS, COLS + ROWS * NEAR
STACK = Q + 2 * REACH
SPLIT = TILE - 2 * REACH
BF16 = jnp.bfloat16
F32 = jnp.float32


def split(table):
    high = table.astype(ml_dtypes.bfloat16)
    low = (table - high.astype(np.float64)).astype(ml_dtypes.bfloat16)
    return high, low


@functools.lru_cache(maxsize=None)
def tables():
    freq = np.arange(NF) - NF // 2
    pixels = np.arange(TILE)
    points = np.arange(Q)
    turn = np.mod(freq[:, None] * pixels[None, :], TILE) * (2.0 * np.pi / TILE)
    forward = np.concatenate([np.cos(turn), np.sin(turn)]) / TILE
    high, low = split(forward)
    forward_rows = np.concatenate([high, low])
    forward_cols = np.ascontiguousarray(forward_rows.T)

    turn = np.mod(points[:, None] * freq[None, :], Q) * (2.0 * np.pi / Q)
    cos, sin = np.cos(turn), np.sin(turn)
    inverse_left = np.concatenate([cos, -sin], axis=1)
    edges = np.concatenate([np.arange(TILE - REACH, TILE), np.arange(REACH)])
    turn = np.mod(edges[:, None] * freq[None, :], TILE) * (2.0 * np.pi / TILE)
    edge_left = np.concatenate([np.cos(turn), -np.sin(turn)], axis=1)
    right = np.zeros((LANES, 2 * LANES))
    for k in range(2):
        re = slice(2 * k * NF, (2 * k + 1) * NF)
        im = slice((2 * k + 1) * NF, (2 * k + 2) * NF)
        out_re = slice(k * LANES, k * LANES + Q)
        out_im = slice(k * LANES + Q, (k + 1) * LANES)
        right[re, out_re], right[re, out_im] = cos.T, sin.T
        right[im, out_re], right[im, out_im] = -sin.T, cos.T

    spread_up = np.zeros((LANES, 4 * LANES))
    spread_low = np.zeros((LANES, 4 * LANES))
    rest = np.zeros((LANES, 2 * LANES))
    for copy in range(4):
        for part in range(2):
            for b in range(NF):
                for tile in range(2):
                    lane = tile * Q + part * NF + b
                    base = tile * 2 * LANES + part * LANES + copy * NF
                    spread_up[lane, base + b] = 1.0
                    if b:
                        spread_low[lane, base + NF - b] = -1.0 if part else 1.0
                rest[part * NF + b, part * LANES + copy * NF + b] = 1.0
            for i in range(1, HALF):
                rest[Q + part * (HALF - 1) + i - 1, part * LANES + copy * NF] = 1.0
        rest[Q + 2 * (HALF - 1), copy * NF + HALF] = 1.0
    rest_mask = np.zeros((HALF, LANES), np.float32)
    rest_mask[0, :Q] = rest_mask[0, Q + 2 * (HALF - 1)] = 1.0
    turned = np.zeros((WINDOW * HALF // 2, WINDOW * HALF // 2))
    for i in range(1, HALF):
        rest_mask[i, Q + i - 1] = rest_mask[i, Q + HALF - 1 + i - 1] = 1.0
        for pair in range(WINDOW // 2):
            turned[pair * HALF + i, pair * HALF + HALF - i] = 1.0

    harmonic = np.arange(Q) - Q // 2
    fine = np.mod(pixels[:, None] * harmonic[None, :], TILE) * (2.0 * np.pi / TILE)
    grid = np.mod(points[:, None] * harmonic[None, :], Q) * (2.0 * np.pi / Q)
    interp = (np.cos(fine) @ np.cos(grid).T + np.sin(fine) @ np.sin(grid).T) / Q
    interp = interp.astype(ml_dtypes.bfloat16).astype(np.float64)

    offsets = np.arange(2 * REACH + 1) - REACH
    taps = np.exp(-offsets * offsets / 32.0)
    taps = taps / taps.sum()

    def blur(out_pixels, in_pixels):
        gap = out_pixels[:, None] - in_pixels[None, :]
        inside = np.abs(gap) <= REACH
        return np.where(inside, taps[np.clip(gap + REACH, 0, 2 * REACH)], 0.0)

    across = np.zeros((4 * Q, TILE))
    for n in range(3):
        across[n * Q : (n + 1) * Q] = (blur(pixels, pixels + (n - 1) * TILE) @ interp).T

    out_rows = np.arange(2 * TILE)
    down = np.zeros((2 * TILE, 2 * STACK))
    down[:, :Q] = blur(out_rows, pixels) @ interp
    down[:, Q : Q + REACH] = blur(out_rows, np.arange(-REACH, 0))
    down[:, STACK : STACK + Q] = blur(out_rows, pixels + TILE) @ interp
    down[:, STACK + Q : STACK + Q + REACH] = blur(out_rows, 2 * TILE + np.arange(REACH))
    assert not down[:SPLIT, STACK:].any()

    bf16 = dict(
        forward_rows=forward_rows,
        forward_cols=forward_cols,
        inverse_left=inverse_left,
        edge_left=edge_left,
        inverse_right=right,
        spread_up=spread_up,
        spread_low=spread_low,
        rest=rest,
        turned=turned,
        across=across,
        down_upper=4.0 * down[:SPLIT, :STACK],
        down_lower=4.0 * down[SPLIT:],
    )
    out = {name: value.astype(ml_dtypes.bfloat16) for name, value in bf16.items()}
    out["rest_mask"] = rest_mask
    return out


def dot(a, b):
    return jnp.dot(a, b, preferred_element_type=F32)


def halves(x):
    high = x.astype(BF16)
    return high, (x - high.astype(F32)).astype(BF16)


def lanes_of(shape):
    return lax.broadcasted_iota(jnp.int32, shape, 1)


def seats(cells, chosen, dest, row):
    count = jnp.int32(0)
    for cell in cells:
        chosen[dest * 16 + count] = cell & (CELLS - 1)
        count = count + ((cell >> 5) == row).astype(jnp.int32)
    return count


def sources(cells, place, at, taken, first):
    for n in range(ROWS + 1):
        taken[n] = jnp.int32(first)
    for n, cell in enumerate(cells):
        source = cell >> 5
        rank = taken[source + 1]
        taken[source + 1] = rank + 1
        place[at + n] = jnp.where(cell >= 0, source * 16 + rank, -1)


def rows_of(dest):
    return [i for i in range(2 * dest - 1, 2 * dest + 3) if 0 <= i < 2 * ROWS]


def window_rows(ids_s, columns):
    cells = []
    for i in range(4):
        tile_row = 2 * lax.axis_index("rows") - 1 + i
        inside = (tile_row >= 0) & (tile_row < 2 * ROWS)
        tile_row = jnp.clip(tile_row, 0, 2 * ROWS - 1)
        cells += [jnp.where(inside, ids_s[j, tile_row], -1) for j in columns]
    return cells


def near_table(ids_s, counts_s, table, chosen, taken):
    row = lax.axis_index("rows")
    start = jnp.int32(0)
    for c in range(COLS):
        table[STARTS + c] = start
        start = start + counts_s[row, c]
    for dest in range(ROWS):
        cells = [ids_s[j, i] for i in rows_of(dest) for j in range(4)]
        count = seats(cells, chosen, dest, row)
        for n in range(NEAR):
            cell = jnp.where(n < count, chosen[dest * 16 + n], CELLS)
            table[SEATS + dest * NEAR + n] = cell
    sources(window_rows(ids_s, range(4)), table, PLACES, taken, 0)


def spectra_kernel(
    mask, ids, dose, fwd_cols, fwd_rows, kernels, weights, counts, threshold,
    out, ker, table, threshold_s,
    mask_v, ids_v, dose_v, cols_v, rows_v, kernels_v, weights_s, counts_s,
    ids_s, chosen, taken, extra, sems,
):
    moves = [(ids, ids_s), (counts, counts_s), (fwd_rows, rows_v)]
    moves += [(mask.at[s], mask_v.at[s]) for s in range(SLOTS)]
    moves += [(kernels, kernels_v), (weights, weights_s), (fwd_cols, cols_v)]
    moves += [(ids, ids_v), (dose, dose_v)]
    copies = [
        pltpu.make_async_copy(src, dst, sems.at[i]) for i, (src, dst) in enumerate(moves)
    ]
    for copy in copies:
        copy.start()
    threshold_s[0] = threshold[0]
    for copy in copies[:2]:
        copy.wait()
    near_table(ids_s, counts_s, table, chosen, taken)
    for copy in copies[2:6]:
        copy.wait()

    pairs = []
    for slot in range(SLOTS):
        if slot == 3:
            for copy in copies[6:]:
                copy.wait()
            for two in range(NK // 2):
                re, im = [], []
                for k in (2 * two, 2 * two + 1):
                    scale = jnp.sqrt(jnp.full((NF, NF), weights_s[k], F32))
                    re.append(kernels_v[0, k] * scale)
                    im.append(kernels_v[1, k] * scale)
                ker[0, two] = jnp.concatenate([re[0], im[0], re[1], im[1]], axis=1)
                ker[1, two] = jnp.concatenate([-im[0], re[0], -im[1], re[1]], axis=1)
        cols = dot(rows_v[...], mask_v[slot])
        high, low = halves(cols[:Q] + cols[Q:])
        pairs.append(jnp.concatenate([high, low], axis=0))

    lane = lanes_of((NF, LANES))
    line = lax.broadcasted_iota(jnp.int32, (NF, LANES), 0)
    even = (lane // NF) % 2 == 0
    in_re = lane == line + Q - HALF - 1
    in_im = lane == line + Q - HALF - 1 + HALF - 1
    column = line > HALF
    lane1 = lanes_of((1, LANES))
    blocks, rows = [], []
    for slot in range(SLOTS):
        both = dot(pairs[slot], cols_v[...])
        both = both[:Q] + both[Q:]
        both = both + pltpu.roll(both, Q, 1)
        top, bottom = both[:NF], both[NF:]
        real = top - pltpu.roll(bottom, NF, 1)
        imag = -(bottom + pltpu.roll(top, NF, 1))
        blocks.append(jnp.where(even, real, pltpu.roll(imag, NF, 1)))
        first = jnp.where(column & in_re, jnp.broadcast_to(real[:, 0:1], (NF, LANES)), 0.0)
        second = jnp.where(column & in_im, jnp.broadcast_to(imag[:, 0:1], (NF, LANES)), 0.0)
        turned = jnp.sum(first + second, axis=0, keepdims=True)
        mean = real[HALF : HALF + 1, HALF : HALF + 1]
        mean = jnp.broadcast_to(mean - mean.astype(BF16).astype(F32), (1, LANES))
        turned = jnp.where(lane1 == Q + 2 * (HALF - 1), mean, turned)
        rows.append(jnp.where(lane1 < Q, blocks[slot][HALF : HALF + 1], turned))
    half = lanes_of((HALF, LANES)) < Q
    packed = [
        jnp.where(half, blocks[2 * i][:HALF], blocks[2 * i + 1][:HALF]).astype(BF16)
        for i in range(SLOTS // 2)
    ]
    extra[...] = jnp.zeros_like(extra)
    for slot in range(SLOTS):
        extra[slot : slot + 1, :] = rows[slot]
    extra[IDS - EXTRA : IDS - EXTRA + 4, 0:16] = ids_v[...].astype(F32)
    at = slice(DOSES - EXTRA, DOSES - EXTRA + 2)
    high = dose_v[...].astype(BF16).astype(F32)
    middle = (dose_v[...] - high).astype(BF16).astype(F32)
    extra[at, 4:8] = high
    extra[at, 8:12] = middle
    extra[at, 12:16] = dose_v[...] - high - middle
    packed.append(extra[...].astype(BF16))
    for c in range(COLS):
        for i in range(4):
            out[c, i * HALF : (i + 1) * HALF, :] = packed[i]


def routing_kernel(
    packets, table,
    out, place,
    held, rests, buffer, where_v, where_s, chosen, taken, sem,
):
    row, col = lax.axis_index("rows"), lax.axis_index("cols")
    def rest_of(c):
        return packets[c, EXTRA : EXTRA + 16, :].astype(F32)

    before = rest_of(jnp.maximum(col - 1, 0))
    after = rest_of(jnp.minimum(col + 1, COLS - 1))
    line = lax.broadcasted_iota(jnp.int32, (16, LANES), 0)
    first = IDS - EXTRA
    window = jnp.where(
        line == 0, pltpu.roll(before, 16 - first - 3, 0), pltpu.roll(after, 16 - first + 1, 0)
    ).astype(jnp.int32)
    exists = ((line == 0) & (col > 0)) | ((line == 1) & (col < COLS - 1))
    where_v[...] = jnp.where(exists, window, -1)
    copy = pltpu.make_async_copy(where_v, where_s, sem)
    copy.start()

    here = rest_of(col)
    for c in range(COLS):
        rests[c * 16 : (c + 1) * 16, :] = rest_of(c)
    left = lanes_of((HALF, LANES)) < Q
    for c in range(COLS):
        start = table[STARTS + c]
        for s in range(SLOTS):
            pair = packets[c, (s // 2) * HALF : (s // 2 + 1) * HALF, :].astype(F32)
            moved = pltpu.roll(pair, Q, 1)
            both = jnp.where(left, moved, pair) if s % 2 else jnp.where(left, pair, moved)
            held[start + s] = both
            buffer[pl.ds(start + s, 1), :] = rests[c * 16 + s : c * 16 + s + 1, :]
    held[CELLS] = jnp.zeros((HALF, LANES), F32)
    buffer[CELLS : CELLS + 1, :] = jnp.zeros((1, LANES), F32)

    lane = lanes_of((2, LANES))
    at = slice(DOSES - EXTRA, DOSES - EXTRA + 2)
    doses = jnp.where(
        lane < 16,
        before[at],
        jnp.where(lane < 32, pltpu.roll(here[at], 16, 1), pltpu.roll(after[at], 32, 1)),
    )

    def send(dest, cells, at):
        for n in range(0, len(cells), 2):
            one, two = held[cells[n]], held[cells[n + 1]]
            rows = slice(at + n // 2 * HALF, at + (n // 2 + 1) * HALF)
            out[dest, rows, :] = jnp.where(left, one, two).astype(BF16)

    near = [
        [table[SEATS + dest * NEAR + n] for n in range(NEAR)] for dest in range(ROWS)
    ]
    for dest in range(ROWS):
        send(dest, near[dest], 0)
    copy.wait()
    sources(window_rows(where_s, range(2)), place, 0, taken, NEAR)
    for dest in range(ROWS):
        cells = [where_s[j, i] for i in rows_of(dest) for j in range(2)]
        count = seats(cells, chosen, dest, row)
        cells = [jnp.where(n < count, chosen[dest * 16 + n], CELLS) for n in range(FAR)]
        send(dest, cells, NEAR // 2 * HALF)
        rows = [buffer[pl.ds(cell, 1), :] for cell in near[dest] + cells]
        out[dest, REST : REST + 16, :] = jnp.concatenate(rows + [doses], axis=0).astype(BF16)


def develop_kernel(
    tiles, table, place, ker, threshold, turned, spread_up, spread_low, rest, rest_mask,
    inv_left, edge_left, inv_right, across, down_upper, down_lower,
    out,
    after_rows, stage, sems,
):
    row = lax.axis_index("rows")
    for source in range(ROWS):
        at = slice(source * 16, (source + 1) * 16)
        after_rows[at, :] = tiles[source, REST : REST + 16, :].astype(F32)
    left = lanes_of((HALF, LANES)) < Q
    held, rests = [], []
    for t in range(0, WINDOW, 2):
        both = []
        for n in (t, t + 1):
            i, j = n // 6, n % 6
            found = table[PLACES + 4 * i + j - 1] if 1 <= j < 5 else place[2 * i + j // 5]
            here = jnp.maximum(found, 0)
            rank = here & 15
            at = pl.multiple_of((rank >> 1) * HALF, HALF)
            pair = tiles[here >> 4, pl.ds(at, HALF), :].astype(F32)
            tile = jnp.where((rank & 1) == (n & 1), pair, pltpu.roll(pair, Q, 1))
            both.append(jnp.where(found >= 0, tile, 0.0))
            line = jnp.where(found >= 0, after_rows[pl.ds(here, 1), :], 0.0)
            rests.append(jnp.broadcast_to(line, (HALF, LANES)) * rest_mask[...])
        held.append(jnp.where(left, both[0], both[1]).astype(BF16))
    held = jnp.concatenate(held, axis=0)
    upper = dot(held, spread_up[...])
    lower = dot(dot(turned[...], held).astype(BF16), spread_low[...])
    rests = dot(jnp.concatenate(rests, axis=0).astype(BF16), rest[...])

    def doses(source):
        info = after_rows[pl.ds(pl.multiple_of(source * 16, 16), 16), :][MOST:]
        return info + pltpu.roll(info, LANES - 4, 1) + pltpu.roll(info, LANES - 8, 1)

    own = doses(row)
    above = doses(jnp.maximum(row - 1, 0))
    below = doses(jnp.minimum(row + 1, ROWS - 1))

    def picture(i, j):
        whole_tile = i in (1, 2)
        m, t = 3 * i + j // 2, 6 * i + j
        a, r = slice(m * HALF, (m + 1) * HALF), slice(t * HALF, (t + 1) * HALF)
        re = slice((j % 2) * 2 * LANES, (j % 2) * 2 * LANES + LANES)
        im = slice(re.stop, re.stop + LANES)
        real = jnp.concatenate([upper[a, re], lower[a, re] + rests[r, :LANES]], axis=0)
        imag = jnp.concatenate([upper[a, im], lower[a, im] + rests[r, LANES:]], axis=0)
        prods = []
        for two in range(NK // 2):
            ka, kb = ker[0, two], ker[1, two]
            prod = jnp.concatenate([ka * real + kb * imag, ka * imag - kb * real], axis=0)
            prods.append(prod.astype(BF16))
        prod = jnp.concatenate(prods, axis=1)
        half = dot(inv_left[...] if whole_tile else edge_left[...], prod)
        if not whole_tile:
            half = half[:REACH] if i == 0 else half[REACH:]
        return jnp.concatenate(
            [half[:, n * LANES : (n + 1) * LANES] for n in range(NK // 2)], axis=0
        ).astype(BF16)

    def intensity(halfway):
        field = dot(halfway, inv_right[...])
        power = field * field
        power = power[:, :LANES] + power[:, LANES:]
        height = power.shape[0] // (NK // 2)
        total = power[:height]
        for n in range(1, NK // 2):
            total = total + power[n * height : (n + 1) * height]
        return total + pltpu.roll(total, Q, 1)

    lane_of = [7] + [20 + j for j in range(4)] + [36]
    dose_rows = [above[1:2], own[0:1], own[1:2], below[0:1]]
    left = lanes_of((STACK, LANES)) < Q

    images = {}
    for group in ((0, 3), (1,), (2,)):
        halfway = {(i, j): picture(i, j) for i in group for j in range(6)}
        for i in group:
            for j in range(6):
                scale = dose_rows[i][:, lane_of[j] : lane_of[j] + 1]
                images[i, j] = intensity(halfway[i, j]) * scale

    def columns(strip, tile):
        none = jnp.zeros((REACH, LANES), F32)
        stack = [
            jnp.concatenate([images[tile, j], images[strip, j], none], axis=0) for j in range(6)
        ]
        wide = []
        for j in range(1, 5):
            two = jnp.where(left, stack[j - 1], stack[j])
            three = jnp.concatenate([two, stack[j + 1]], axis=1).astype(BF16)
            wide.append(dot(three, across[...]).astype(BF16))
        return jnp.concatenate(wide, axis=1)

    shift = 4.0 * threshold[0]
    copies = []

    def finish(start, stop, level):
        rows = slice(start, stop)
        stage[rows, :] = (0.5 * jnp.tanh(level - shift) + 0.5).astype(BF16)
        copy = pltpu.make_async_copy(stage.at[rows, :], out.at[rows, :], sems.at[len(copies)])
        copy.start()
        copies.append(copy)

    upper_rows = columns(0, 1)
    finish(0, SPLIT, dot(down_upper[...], upper_rows))
    both_rows = jnp.concatenate([upper_rows, columns(3, 2)], axis=0)
    middle = SPLIT + 192
    finish(SPLIT, middle, dot(down_lower[: middle - SPLIT, :], both_rows))
    finish(middle, 2 * TILE, dot(down_lower[middle - SPLIT :, :], both_rows))
    for copy in copies:
        copy.wait()


PARAMS = pltpu.CompilerParams(vmem_limit_bytes=48 * 1024 * 1024)
IN_HBM = pl.BlockSpec(memory_space=pltpu.HBM)
IN_VMEM = pl.BlockSpec(memory_space=pltpu.VMEM)
IN_SMEM = pl.BlockSpec(memory_space=pltpu.SMEM)


def spectra(masks, cell_ids, dose, kernels, kernel_weights, owned_counts, threshold):
    table = tables()
    operands = [masks, cell_ids.T, dose]
    operands += [jnp.asarray(table[n]) for n in ("forward_cols", "forward_rows")]
    operands += [kernels, kernel_weights, owned_counts, threshold]
    in_hbm = [pltpu.with_memory_space_constraint(op, pltpu.HBM) for op in operands[:-1]]
    in_hbm.append(operands[-1])
    return pl.pallas_call(
        spectra_kernel,
        out_shape=(
            jax.ShapeDtypeStruct((COLS, PACKET, LANES), BF16),
            jax.ShapeDtypeStruct((2, NK // 2, NF, LANES), F32),
            pltpu.SMEM((PLACES + 16,), jnp.int32),
            pltpu.SMEM((1,), F32),
        ),
        in_specs=[IN_HBM] * (len(operands) - 1) + [IN_SMEM],
        out_specs=(IN_VMEM, IN_VMEM, IN_SMEM, IN_SMEM),
        scratch_shapes=[
            *[pltpu.VMEM(op.shape, op.dtype) for op in operands[:-3]],
            *[pltpu.SMEM(op.shape, op.dtype) for op in operands[-3:-1]],
            pltpu.SMEM((4, 2 * ROWS), jnp.int32),
            pltpu.SMEM((ROWS * 16 + 16,), jnp.int32),
            pltpu.SMEM((16,), jnp.int32),
            pltpu.VMEM((16, LANES), F32),
            pltpu.SemaphoreType.DMA((len(operands) + SLOTS - 1,)),
        ],
        compiler_params=PARAMS,
    )(*in_hbm)


def route(packets, seating):
    return pl.pallas_call(
        routing_kernel,
        out_shape=(
            jax.ShapeDtypeStruct((ROWS, OUTGOING, LANES), BF16),
            pltpu.SMEM((8,), jnp.int32),
        ),
        in_specs=[IN_VMEM, IN_SMEM],
        out_specs=(IN_VMEM, IN_SMEM),
        scratch_shapes=[
            pltpu.VMEM((CELLS + SLOTS, HALF, LANES), F32),
            pltpu.VMEM((COLS * 16, LANES), F32),
            pltpu.VMEM((CELLS + 8, LANES), F32),
            pltpu.VMEM((16, LANES), jnp.int32),
            pltpu.SMEM((16, LANES), jnp.int32),
            pltpu.SMEM((ROWS * 16 + 16,), jnp.int32),
            pltpu.SMEM((16,), jnp.int32),
            pltpu.SemaphoreType.DMA,
        ],
        compiler_params=PARAMS,
    )(packets, seating)


def develop(incoming, seating, place, ker, threshold):
    table = tables()
    names = ("turned", "spread_up", "spread_low", "rest", "rest_mask")
    names += ("inverse_left", "edge_left", "inverse_right", "across", "down_upper", "down_lower")
    constants = [jnp.asarray(table[n]) for n in names]
    return pl.pallas_call(
        develop_kernel,
        out_shape=jax.ShapeDtypeStruct((2 * TILE, 4 * TILE), BF16),
        in_specs=[IN_VMEM, IN_SMEM, IN_SMEM, IN_VMEM, IN_SMEM, *[IN_VMEM] * len(constants)],
        out_specs=IN_HBM,
        scratch_shapes=[
            pltpu.VMEM((ROWS * 16, LANES), F32),
            pltpu.VMEM((2 * TILE, 4 * TILE), BF16),
            pltpu.SemaphoreType.DMA((3,)),
        ],
        compiler_params=PARAMS,
    )(incoming, seating, place, ker, threshold, *constants)


def local(masks, owned_counts, cell_ids, kernels, kernel_weights, dose, threshold):
    packet, ker, seating, threshold = spectra(
        masks, cell_ids, dose, kernels, kernel_weights, owned_counts, threshold
    )
    packets = lax.all_to_all(packet, "cols", split_axis=0, concat_axis=0, tiled=True)
    outgoing, place = route(packets, seating)
    incoming = lax.all_to_all(outgoing, "rows", split_axis=0, concat_axis=0, tiled=True)
    return develop(incoming, seating, place, ker, threshold)


def solution(mesh):
    return jax.shard_map(
        local,
        mesh=mesh,
        in_specs=(
            P(("rows", "cols"), None, None),
            P(),
            P(None, "cols"),
            P(),
            P(),
            P("rows", "cols"),
            P(),
        ),
        out_specs=P("rows", "cols"),
        check_vma=False,
    )
```

```python
import functools

import jax
import jax.numpy as jnp
import ml_dtypes
import numpy as np
from jax import lax
from jax.experimental import pallas as pl
from jax.experimental.pallas import tpu as pltpu
from jax.sharding import PartitionSpec as P

REACH = 8
TILE = 384
NF = 32
NK = 16
Q = 64
SLOTS = 6
ROWS = 8
COLS = 16
CELLS = 32
LANES = 128
HALF = NF // 2
EXTRA = 3 * HALF
IDS = EXTRA + SLOTS
DOSES = IDS + 4
PACKET = EXTRA + 16
WINDOW = 4 * 6
NEAR = 6
FAR = 8
MOST = NEAR + FAR
REST = MOST * HALF // 2
OUTGOING = REST + 16
STARTS, SEATS, PLACES = 0, COLS, COLS + ROWS * NEAR
STACK = Q + 2 * REACH
SPLIT = TILE - 2 * REACH
BF16 = jnp.bfloat16
F32 = jnp.float32


def split(table):
    high = table.astype(ml_dtypes.bfloat16)
    low = (table - high.astype(np.float64)).astype(ml_dtypes.bfloat16)
    return high, low


@functools.lru_cache(maxsize=None)
def tables():
    freq = np.arange(NF) - NF // 2
    pixels = np.arange(TILE)
    points = np.arange(Q)
    turn = np.mod(freq[:, None] * pixels[None, :], TILE) * (2.0 * np.pi / TILE)
    forward = np.concatenate([np.cos(turn), np.sin(turn)]) / TILE
    high, low = split(forward)
    forward_rows = np.concatenate([high, low])
    forward_cols = np.ascontiguousarray(forward_rows.T)

    turn = np.mod(points[:, None] * freq[None, :], Q) * (2.0 * np.pi / Q)
    cos, sin = np.cos(turn), np.sin(turn)
    order = np.concatenate([np.arange(HALF + 1), np.arange(NF - 1, HALF, -1)])
    inverse_left = np.concatenate([cos[:, order], -sin[:, order]], axis=1)
    edges = np.concatenate([np.arange(TILE - REACH, TILE), np.arange(REACH)])
    turn = np.mod(edges[:, None] * freq[None, :], TILE) * (2.0 * np.pi / TILE)
    edge_left = np.concatenate([np.cos(turn)[:, order], -np.sin(turn)[:, order]], axis=1)
    right = np.zeros((LANES, 2 * LANES))
    for k in range(2):
        re = slice(2 * k * NF, (2 * k + 1) * NF)
        im = slice((2 * k + 1) * NF, (2 * k + 2) * NF)
        out_re = slice(k * LANES, k * LANES + Q)
        out_im = slice(k * LANES + Q, (k + 1) * LANES)
        right[re, out_re], right[re, out_im] = cos.T, sin.T
        right[im, out_re], right[im, out_im] = -sin.T, cos.T

    spread_up = np.zeros((LANES, 4 * LANES))
    spread_low = np.zeros((LANES, 4 * LANES))
    rest = np.zeros((LANES, 2 * LANES))
    for copy in range(4):
        for part in range(2):
            for b in range(NF):
                for tile in range(2):
                    lane = tile * Q + part * NF + b
                    base = tile * 2 * LANES + part * LANES + copy * NF
                    spread_up[lane, base + b] = 1.0
                    if b:
                        spread_low[lane, base + NF - b] = -1.0 if part else 1.0
                rest[part * NF + b, part * LANES + copy * NF + b] = 1.0
            for i in range(1, HALF):
                rest[Q + part * (HALF - 1) + i - 1, part * LANES + copy * NF] = 1.0
        rest[Q + 2 * (HALF - 1), copy * NF + HALF] = 1.0
    rest_mask = np.zeros((HALF, LANES), np.float32)
    rest_mask[0, :Q] = rest_mask[0, Q + 2 * (HALF - 1)] = 1.0
    for i in range(1, HALF):
        rest_mask[HALF - i, Q + i - 1] = rest_mask[HALF - i, Q + HALF - 1 + i - 1] = 1.0

    harmonic = np.arange(Q) - Q // 2
    fine = np.mod(pixels[:, None] * harmonic[None, :], TILE) * (2.0 * np.pi / TILE)
    grid = np.mod(points[:, None] * harmonic[None, :], Q) * (2.0 * np.pi / Q)
    interp = (np.cos(fine) @ np.cos(grid).T + np.sin(fine) @ np.sin(grid).T) / Q
    interp = interp.astype(ml_dtypes.bfloat16).astype(np.float64)

    offsets = np.arange(2 * REACH + 1) - REACH
    taps = np.exp(-offsets * offsets / 32.0)
    taps = taps / taps.sum()

    def blur(out_pixels, in_pixels):
        gap = out_pixels[:, None] - in_pixels[None, :]
        inside = np.abs(gap) <= REACH
        return np.where(inside, taps[np.clip(gap + REACH, 0, 2 * REACH)], 0.0)

    across = np.zeros((4 * Q, TILE))
    for n in range(3):
        across[n * Q : (n + 1) * Q] = (blur(pixels, pixels + (n - 1) * TILE) @ interp).T

    out_rows = np.arange(2 * TILE)
    down = np.zeros((2 * TILE, 2 * STACK))
    down[:, :Q] = blur(out_rows, pixels) @ interp
    down[:, Q : Q + REACH] = blur(out_rows, np.arange(-REACH, 0))
    down[:, STACK : STACK + Q] = blur(out_rows, pixels + TILE) @ interp
    down[:, STACK + Q : STACK + Q + REACH] = blur(out_rows, 2 * TILE + np.arange(REACH))
    assert not down[:SPLIT, STACK:].any()

    bf16 = dict(
        forward_rows=forward_rows,
        forward_cols=forward_cols,
        inverse_left=inverse_left,
        edge_left=edge_left,
        inverse_right=right,
        spread_up=spread_up,
        spread_low=spread_low,
        rest=rest,
        across=across,
        down_upper=4.0 * down[:SPLIT, :STACK],
        down_lower=4.0 * down[SPLIT:],
    )
    out = {name: value.astype(ml_dtypes.bfloat16) for name, value in bf16.items()}
    out["rest_mask"] = rest_mask
    return out


def dot(a, b):
    return jnp.dot(a, b, preferred_element_type=F32)


def halves(x):
    high = x.astype(BF16)
    return high, (x - high.astype(F32)).astype(BF16)


def lanes_of(shape):
    return lax.broadcasted_iota(jnp.int32, shape, 1)


def seats(cells, chosen, dest, row):
    count = jnp.int32(0)
    for cell in cells:
        chosen[dest * 16 + count] = cell & (CELLS - 1)
        count = count + ((cell >> 5) == row).astype(jnp.int32)
    return count


def sources(cells, place, at, taken, first):
    for n in range(ROWS + 1):
        taken[n] = jnp.int32(first)
    for n, cell in enumerate(cells):
        source = cell >> 5
        rank = taken[source + 1]
        taken[source + 1] = rank + 1
        place[at + n] = jnp.where(cell >= 0, source * 16 + rank, -1)


def rows_of(dest):
    return [i for i in range(2 * dest - 1, 2 * dest + 3) if 0 <= i < 2 * ROWS]


def window_rows(ids_s, columns):
    cells = []
    for i in range(4):
        tile_row = 2 * lax.axis_index("rows") - 1 + i
        inside = (tile_row >= 0) & (tile_row < 2 * ROWS)
        tile_row = jnp.clip(tile_row, 0, 2 * ROWS - 1)
        cells += [jnp.where(inside, ids_s[j, tile_row], -1) for j in columns]
    return cells


def near_table(ids_s, counts_s, table, chosen, taken):
    row = lax.axis_index("rows")
    start = jnp.int32(0)
    for c in range(COLS):
        table[STARTS + c] = start
        start = start + counts_s[row, c]
    for dest in range(ROWS):
        cells = [ids_s[j, i] for i in rows_of(dest) for j in range(4)]
        count = seats(cells, chosen, dest, row)
        for n in range(NEAR):
            cell = jnp.where(n < count, chosen[dest * 16 + n], CELLS)
            table[SEATS + dest * NEAR + n] = cell
    sources(window_rows(ids_s, range(4)), table, PLACES, taken, 0)


def spectra_kernel(
    mask, ids, dose, fwd_cols, fwd_rows, kernels, weights, counts, threshold,
    out, ker, table, threshold_s,
    mask_v, ids_v, dose_v, cols_v, rows_v, kernels_v, weights_s, counts_s,
    ids_s, chosen, taken, extra, sems,
):
    moves = [(ids, ids_s), (counts, counts_s), (fwd_rows, rows_v)]
    moves += [(mask.at[s], mask_v.at[s]) for s in range(SLOTS)]
    moves += [(kernels, kernels_v), (weights, weights_s), (fwd_cols, cols_v)]
    moves += [(ids, ids_v), (dose, dose_v)]
    copies = [
        pltpu.make_async_copy(src, dst, sems.at[i]) for i, (src, dst) in enumerate(moves)
    ]
    for copy in copies:
        copy.start()
    threshold_s[0] = threshold[0]
    for copy in copies[:2]:
        copy.wait()
    near_table(ids_s, counts_s, table, chosen, taken)
    for copy in copies[2:6]:
        copy.wait()

    pairs = []
    for slot in range(SLOTS):
        if slot == 3:
            for copy in copies[6:]:
                copy.wait()
            for two in range(NK // 2):
                re, im = [], []
                for k in (2 * two, 2 * two + 1):
                    scale = jnp.sqrt(jnp.full((NF, NF), weights_s[k], F32))
                    re.append(kernels_v[0, k] * scale)
                    im.append(kernels_v[1, k] * scale)
                for part, four in enumerate(
                    ([re[0], im[0], re[1], im[1]], [-im[0], re[0], -im[1], re[1]])
                ):
                    block = jnp.concatenate(four, axis=1)
                    turned = [block[n : n + 1] for n in range(NF - 1, HALF, -1)]
                    ker[part, two] = jnp.concatenate([block[: HALF + 1], *turned], axis=0)
        cols = dot(rows_v[...], mask_v[slot])
        high, low = halves(cols[:Q] + cols[Q:])
        pairs.append(jnp.concatenate([high, low], axis=0))

    lane = lanes_of((NF, LANES))
    line = lax.broadcasted_iota(jnp.int32, (NF, LANES), 0)
    even = (lane // NF) % 2 == 0
    in_re = lane == line + Q - HALF - 1
    in_im = lane == line + Q - HALF - 1 + HALF - 1
    column = line > HALF
    lane1 = lanes_of((1, LANES))
    blocks, rows = [], []
    for slot in range(SLOTS):
        both = dot(pairs[slot], cols_v[...])
        both = both[:Q] + both[Q:]
        both = both + pltpu.roll(both, Q, 1)
        top, bottom = both[:NF], both[NF:]
        real = top - pltpu.roll(bottom, NF, 1)
        imag = -(bottom + pltpu.roll(top, NF, 1))
        blocks.append(jnp.where(even, real, pltpu.roll(imag, NF, 1)))
        first = jnp.where(column & in_re, jnp.broadcast_to(real[:, 0:1], (NF, LANES)), 0.0)
        second = jnp.where(column & in_im, jnp.broadcast_to(imag[:, 0:1], (NF, LANES)), 0.0)
        turned = jnp.sum(first + second, axis=0, keepdims=True)
        mean = real[HALF : HALF + 1, HALF : HALF + 1]
        mean = jnp.broadcast_to(mean - mean.astype(BF16).astype(F32), (1, LANES))
        turned = jnp.where(lane1 == Q + 2 * (HALF - 1), mean, turned)
        rows.append(jnp.where(lane1 < Q, blocks[slot][HALF : HALF + 1], turned))
    half = lanes_of((HALF, LANES)) < Q
    packed = [
        jnp.where(half, blocks[2 * i][:HALF], blocks[2 * i + 1][:HALF]).astype(BF16)
        for i in range(SLOTS // 2)
    ]
    extra[...] = jnp.zeros_like(extra)
    for slot in range(SLOTS):
        extra[slot : slot + 1, :] = rows[slot]
    extra[IDS - EXTRA : IDS - EXTRA + 4, 0:16] = ids_v[...].astype(F32)
    at = slice(DOSES - EXTRA, DOSES - EXTRA + 2)
    high = dose_v[...].astype(BF16).astype(F32)
    middle = (dose_v[...] - high).astype(BF16).astype(F32)
    extra[at, 4:8] = high
    extra[at, 8:12] = middle
    extra[at, 12:16] = dose_v[...] - high - middle
    packed.append(extra[...].astype(BF16))
    for c in range(COLS):
        for i in range(4):
            out[c, i * HALF : (i + 1) * HALF, :] = packed[i]


def routing_kernel(
    packets, table,
    out, place,
    held, rests, buffer, where_v, where_s, chosen, taken, sem,
):
    row, col = lax.axis_index("rows"), lax.axis_index("cols")
    def rest_of(c):
        return packets[c, EXTRA : EXTRA + 16, :].astype(F32)

    before = rest_of(jnp.maximum(col - 1, 0))
    after = rest_of(jnp.minimum(col + 1, COLS - 1))
    line = lax.broadcasted_iota(jnp.int32, (16, LANES), 0)
    first = IDS - EXTRA
    window = jnp.where(
        line == 0, pltpu.roll(before, 16 - first - 3, 0), pltpu.roll(after, 16 - first + 1, 0)
    ).astype(jnp.int32)
    exists = ((line == 0) & (col > 0)) | ((line == 1) & (col < COLS - 1))
    where_v[...] = jnp.where(exists, window, -1)
    copy = pltpu.make_async_copy(where_v, where_s, sem)
    copy.start()

    here = rest_of(col)
    for c in range(COLS):
        rests[c * 16 : (c + 1) * 16, :] = rest_of(c)
    left = lanes_of((HALF, LANES)) < Q
    for c in range(COLS):
        start = table[STARTS + c]
        for s in range(SLOTS):
            pair = packets[c, (s // 2) * HALF : (s // 2 + 1) * HALF, :].astype(F32)
            moved = pltpu.roll(pair, Q, 1)
            both = jnp.where(left, moved, pair) if s % 2 else jnp.where(left, pair, moved)
            held[start + s] = both
            buffer[pl.ds(start + s, 1), :] = rests[c * 16 + s : c * 16 + s + 1, :]
    held[CELLS] = jnp.zeros((HALF, LANES), F32)
    buffer[CELLS : CELLS + 1, :] = jnp.zeros((1, LANES), F32)

    lane = lanes_of((2, LANES))
    at = slice(DOSES - EXTRA, DOSES - EXTRA + 2)
    doses = jnp.where(
        lane < 16,
        before[at],
        jnp.where(lane < 32, pltpu.roll(here[at], 16, 1), pltpu.roll(after[at], 32, 1)),
    )

    def send(dest, cells, at):
        for n in range(0, len(cells), 2):
            one, two = held[cells[n]], held[cells[n + 1]]
            rows = slice(at + n // 2 * HALF, at + (n // 2 + 1) * HALF)
            out[dest, rows, :] = jnp.where(left, one, two).astype(BF16)

    near = [
        [table[SEATS + dest * NEAR + n] for n in range(NEAR)] for dest in range(ROWS)
    ]
    for dest in range(ROWS):
        send(dest, near[dest], 0)
    copy.wait()
    sources(window_rows(where_s, range(2)), place, 0, taken, NEAR)
    for dest in range(ROWS):
        cells = [where_s[j, i] for i in rows_of(dest) for j in range(2)]
        count = seats(cells, chosen, dest, row)
        cells = [jnp.where(n < count, chosen[dest * 16 + n], CELLS) for n in range(FAR)]
        send(dest, cells, NEAR // 2 * HALF)
        rows = [buffer[pl.ds(cell, 1), :] for cell in near[dest] + cells]
        out[dest, REST : REST + 16, :] = jnp.concatenate(rows + [doses], axis=0).astype(BF16)


def develop_kernel(
    tiles, table, place, ker, threshold, spread_up, spread_low, rest, rest_mask,
    inv_left, edge_left, inv_right, across, down_upper, down_lower,
    out,
    after_rows, stage, sems,
):
    row = lax.axis_index("rows")
    for source in range(ROWS):
        at = slice(source * 16, (source + 1) * 16)
        after_rows[at, :] = tiles[source, REST : REST + 16, :].astype(F32)
    left = lanes_of((HALF, LANES)) < Q
    first = lax.broadcasted_iota(jnp.int32, (HALF, LANES), 0) == 0
    held, paired, rests = [], [], []
    for t in range(0, WINDOW, 2):
        both = []
        for n in (t, t + 1):
            i, j = n // 6, n % 6
            found = table[PLACES + 4 * i + j - 1] if 1 <= j < 5 else place[2 * i + j // 5]
            here = jnp.maximum(found, 0)
            rank = here & 15
            at = pl.multiple_of((rank >> 1) * HALF, HALF)
            pair = tiles[here >> 4, pl.ds(at, HALF), :].astype(F32)
            tile = jnp.where((rank & 1) == (n & 1), pair, pltpu.roll(pair, Q, 1))
            both.append(jnp.where(found >= 0, tile, 0.0))
            line = jnp.where(found >= 0, after_rows[pl.ds(here, 1), :], 0.0)
            rests.append(jnp.broadcast_to(line, (HALF, LANES)) * rest_mask[...])
        pair = jnp.where(left, both[0], both[1])
        held.append(pair.astype(BF16))
        paired.append(jnp.where(first, 0.0, pair).astype(BF16))
    held = jnp.concatenate(held, axis=0)
    paired = jnp.concatenate(paired, axis=0)
    upper = dot(held, spread_up[...])
    lower = dot(paired, spread_low[...])
    rests = dot(jnp.concatenate(rests, axis=0).astype(BF16), rest[...])

    def doses(source):
        info = after_rows[pl.ds(pl.multiple_of(source * 16, 16), 16), :][MOST:]
        return info + pltpu.roll(info, LANES - 4, 1) + pltpu.roll(info, LANES - 8, 1)

    own = doses(row)
    above = doses(jnp.maximum(row - 1, 0))
    below = doses(jnp.minimum(row + 1, ROWS - 1))

    def picture(i, j):
        whole_tile = i in (1, 2)
        m, t = 3 * i + j // 2, 6 * i + j
        a, r = slice(m * HALF, (m + 1) * HALF), slice(t * HALF, (t + 1) * HALF)
        re = slice((j % 2) * 2 * LANES, (j % 2) * 2 * LANES + LANES)
        im = slice(re.stop, re.stop + LANES)
        real = jnp.concatenate([upper[a, re], lower[a, re] + rests[r, :LANES]], axis=0)
        imag = jnp.concatenate([upper[a, im], lower[a, im] + rests[r, LANES:]], axis=0)
        prods = []
        for two in range(NK // 2):
            ka, kb = ker[0, two], ker[1, two]
            prod = jnp.concatenate([ka * real + kb * imag, ka * imag - kb * real], axis=0)
            prods.append(prod.astype(BF16))
        prod = jnp.concatenate(prods, axis=1)
        half = dot(inv_left[...] if whole_tile else edge_left[...], prod)
        if not whole_tile:
            half = half[:REACH] if i == 0 else half[REACH:]
        return jnp.concatenate(
            [half[:, n * LANES : (n + 1) * LANES] for n in range(NK // 2)], axis=0
        ).astype(BF16)

    def intensity(halfway):
        field = dot(halfway, inv_right[...])
        power = field * field
        power = power[:, :LANES] + power[:, LANES:]
        height = power.shape[0] // (NK // 2)
        total = power[:height]
        for n in range(1, NK // 2):
            total = total + power[n * height : (n + 1) * height]
        return total + pltpu.roll(total, Q, 1)

    lane_of = [7] + [20 + j for j in range(4)] + [36]
    dose_rows = [above[1:2], own[0:1], own[1:2], below[0:1]]
    left = lanes_of((STACK, LANES)) < Q

    images = {}
    for group in ((0, 3), (1,), (2,)):
        halfway = {(i, j): picture(i, j) for i in group for j in range(6)}
        for i in group:
            for j in range(6):
                scale = dose_rows[i][:, lane_of[j] : lane_of[j] + 1]
                images[i, j] = intensity(halfway[i, j]) * scale

    def columns(strip, tile):
        none = jnp.zeros((REACH, LANES), F32)
        stack = [
            jnp.concatenate([images[tile, j], images[strip, j], none], axis=0) for j in range(6)
        ]
        wide = []
        for j in range(1, 5):
            two = jnp.where(left, stack[j - 1], stack[j])
            three = jnp.concatenate([two, stack[j + 1]], axis=1).astype(BF16)
            wide.append(dot(three, across[...]).astype(BF16))
        return jnp.concatenate(wide, axis=1)

    shift = 4.0 * threshold[0]
    copies = []

    def finish(start, stop, level):
        rows = slice(start, stop)
        stage[rows, :] = (0.5 * jnp.tanh(level - shift) + 0.5).astype(BF16)
        copy = pltpu.make_async_copy(stage.at[rows, :], out.at[rows, :], sems.at[len(copies)])
        copy.start()
        copies.append(copy)

    upper_rows = columns(0, 1)
    finish(0, SPLIT, dot(down_upper[...], upper_rows))
    both_rows = jnp.concatenate([upper_rows, columns(3, 2)], axis=0)
    middle = SPLIT + 192
    finish(SPLIT, middle, dot(down_lower[: middle - SPLIT, :], both_rows))
    finish(middle, 2 * TILE, dot(down_lower[middle - SPLIT :, :], both_rows))
    for copy in copies:
        copy.wait()


PARAMS = pltpu.CompilerParams(vmem_limit_bytes=48 * 1024 * 1024)
IN_HBM = pl.BlockSpec(memory_space=pltpu.HBM)
IN_VMEM = pl.BlockSpec(memory_space=pltpu.VMEM)
IN_SMEM = pl.BlockSpec(memory_space=pltpu.SMEM)


def spectra(masks, cell_ids, dose, kernels, kernel_weights, owned_counts, threshold):
    table = tables()
    operands = [masks, cell_ids.T, dose]
    operands += [jnp.asarray(table[n]) for n in ("forward_cols", "forward_rows")]
    operands += [kernels, kernel_weights, owned_counts, threshold]
    in_hbm = [pltpu.with_memory_space_constraint(op, pltpu.HBM) for op in operands[:-1]]
    in_hbm.append(operands[-1])
    return pl.pallas_call(
        spectra_kernel,
        out_shape=(
            jax.ShapeDtypeStruct((COLS, PACKET, LANES), BF16),
            jax.ShapeDtypeStruct((2, NK // 2, NF, LANES), F32),
            pltpu.SMEM((PLACES + 16,), jnp.int32),
            pltpu.SMEM((1,), F32),
        ),
        in_specs=[IN_HBM] * (len(operands) - 1) + [IN_SMEM],
        out_specs=(IN_VMEM, IN_VMEM, IN_SMEM, IN_SMEM),
        scratch_shapes=[
            *[pltpu.VMEM(op.shape, op.dtype) for op in operands[:-3]],
            *[pltpu.SMEM(op.shape, op.dtype) for op in operands[-3:-1]],
            pltpu.SMEM((4, 2 * ROWS), jnp.int32),
            pltpu.SMEM((ROWS * 16 + 16,), jnp.int32),
            pltpu.SMEM((16,), jnp.int32),
            pltpu.VMEM((16, LANES), F32),
            pltpu.SemaphoreType.DMA((len(operands) + SLOTS - 1,)),
        ],
        compiler_params=PARAMS,
    )(*in_hbm)


def route(packets, seating):
    return pl.pallas_call(
        routing_kernel,
        out_shape=(
            jax.ShapeDtypeStruct((ROWS, OUTGOING, LANES), BF16),
            pltpu.SMEM((8,), jnp.int32),
        ),
        in_specs=[IN_VMEM, IN_SMEM],
        out_specs=(IN_VMEM, IN_SMEM),
        scratch_shapes=[
            pltpu.VMEM((CELLS + SLOTS, HALF, LANES), F32),
            pltpu.VMEM((COLS * 16, LANES), F32),
            pltpu.VMEM((CELLS + 8, LANES), F32),
            pltpu.VMEM((16, LANES), jnp.int32),
            pltpu.SMEM((16, LANES), jnp.int32),
            pltpu.SMEM((ROWS * 16 + 16,), jnp.int32),
            pltpu.SMEM((16,), jnp.int32),
            pltpu.SemaphoreType.DMA,
        ],
        compiler_params=PARAMS,
    )(packets, seating)


def develop(incoming, seating, place, ker, threshold):
    table = tables()
    names = ("spread_up", "spread_low", "rest", "rest_mask")
    names += ("inverse_left", "edge_left", "inverse_right", "across", "down_upper", "down_lower")
    constants = [jnp.asarray(table[n]) for n in names]
    return pl.pallas_call(
        develop_kernel,
        out_shape=jax.ShapeDtypeStruct((2 * TILE, 4 * TILE), BF16),
        in_specs=[IN_VMEM, IN_SMEM, IN_SMEM, IN_VMEM, IN_SMEM, *[IN_VMEM] * len(constants)],
        out_specs=IN_HBM,
        scratch_shapes=[
            pltpu.VMEM((ROWS * 16, LANES), F32),
            pltpu.VMEM((2 * TILE, 4 * TILE), BF16),
            pltpu.SemaphoreType.DMA((3,)),
        ],
        compiler_params=PARAMS,
    )(incoming, seating, place, ker, threshold, *constants)


def local(masks, owned_counts, cell_ids, kernels, kernel_weights, dose, threshold):
    packet, ker, seating, threshold = spectra(
        masks, cell_ids, dose, kernels, kernel_weights, owned_counts, threshold
    )
    packets = lax.all_to_all(packet, "cols", split_axis=0, concat_axis=0, tiled=True)
    outgoing, place = route(packets, seating)
    incoming = lax.all_to_all(outgoing, "rows", split_axis=0, concat_axis=0, tiled=True)
    return develop(incoming, seating, place, ker, threshold)


def solution(mesh):
    return jax.shard_map(
        local,
        mesh=mesh,
        in_specs=(
            P(("rows", "cols"), None, None),
            P(),
            P(None, "cols"),
            P(),
            P(),
            P("rows", "cols"),
            P(),
        ),
        out_specs=P("rows", "cols"),
        check_vma=False,
    )
```

```python
import functools

import jax
import jax.numpy as jnp
import ml_dtypes
import numpy as np
from jax import lax
from jax.experimental import pallas as pl
from jax.experimental.pallas import tpu as pltpu
from jax.sharding import PartitionSpec as P

REACH = 8
TILE = 384
NF = 32
NK = 16
Q = 64
SLOTS = 6
ROWS = 8
COLS = 16
CELLS = 32
LANES = 128
HALF = NF // 2
EXTRA = 3 * HALF
IDS = EXTRA + SLOTS
DOSES = IDS + 4
PACKET = EXTRA + 16
WINDOW = 4 * 6
NEAR = 6
FAR = 8
MOST = NEAR + FAR
REST = MOST * HALF // 2
OUTGOING = REST + 16
STARTS, SEATS, PLACES = 0, COLS, COLS + ROWS * NEAR
STACK = Q + 2 * REACH
SPLIT = TILE - 2 * REACH
BF16 = jnp.bfloat16
F32 = jnp.float32


def split(table):
    high = table.astype(ml_dtypes.bfloat16)
    low = (table - high.astype(np.float64)).astype(ml_dtypes.bfloat16)
    return high, low


@functools.lru_cache(maxsize=None)
def tables():
    freq = np.arange(NF) - NF // 2
    pixels = np.arange(TILE)
    points = np.arange(Q)
    turn = np.mod(freq[:, None] * pixels[None, :], TILE) * (2.0 * np.pi / TILE)
    forward = np.concatenate([np.cos(turn), np.sin(turn)]) / TILE
    high, low = split(forward)
    forward_rows = np.concatenate([high, low])
    forward_cols = np.ascontiguousarray(forward_rows.T)

    turn = np.mod(points[:, None] * freq[None, :], Q) * (2.0 * np.pi / Q)
    cos, sin = np.cos(turn), np.sin(turn)
    order = np.concatenate([np.arange(HALF + 1), np.arange(NF - 1, HALF, -1)])
    inverse_left = np.concatenate([cos[:, order], -sin[:, order]], axis=1)
    edges = np.concatenate([np.arange(TILE - REACH, TILE), np.arange(REACH)])
    turn = np.mod(edges[:, None] * freq[None, :], TILE) * (2.0 * np.pi / TILE)
    edge_left = np.concatenate([np.cos(turn)[:, order], -np.sin(turn)[:, order]], axis=1)
    right = np.zeros((LANES, 2 * LANES))
    for k in range(2):
        re = slice(2 * k * NF, (2 * k + 1) * NF)
        im = slice((2 * k + 1) * NF, (2 * k + 2) * NF)
        out_re = slice(k * LANES, k * LANES + Q)
        out_im = slice(k * LANES + Q, (k + 1) * LANES)
        right[re, out_re], right[re, out_im] = cos.T, sin.T
        right[im, out_re], right[im, out_im] = -sin.T, cos.T

    spread_up = np.zeros((LANES, 4 * LANES))
    spread_low = np.zeros((LANES, 4 * LANES))
    rest = np.zeros((LANES, 2 * LANES))
    for copy in range(4):
        for part in range(2):
            for b in range(NF):
                for tile in range(2):
                    lane = tile * Q + part * NF + b
                    base = tile * 2 * LANES + part * LANES + copy * NF
                    spread_up[lane, base + b] = 1.0
                    if b:
                        spread_low[lane, base + NF - b] = -1.0 if part else 1.0
                rest[part * NF + b, part * LANES + copy * NF + b] = 1.0
            for i in range(1, HALF):
                rest[Q + part * (HALF - 1) + i - 1, part * LANES + copy * NF] = 1.0
        rest[Q + 2 * (HALF - 1), copy * NF + HALF] = 1.0
    rest_mask = np.zeros((HALF, LANES), np.float32)
    rest_mask[0, :Q] = rest_mask[0, Q + 2 * (HALF - 1)] = 1.0
    for i in range(1, HALF):
        rest_mask[HALF - i, Q + i - 1] = rest_mask[HALF - i, Q + HALF - 1 + i - 1] = 1.0

    harmonic = np.arange(Q) - Q // 2
    fine = np.mod(pixels[:, None] * harmonic[None, :], TILE) * (2.0 * np.pi / TILE)
    grid = np.mod(points[:, None] * harmonic[None, :], Q) * (2.0 * np.pi / Q)
    interp = (np.cos(fine) @ np.cos(grid).T + np.sin(fine) @ np.sin(grid).T) / Q
    interp = interp.astype(ml_dtypes.bfloat16).astype(np.float64)

    offsets = np.arange(2 * REACH + 1) - REACH
    taps = np.exp(-offsets * offsets / 32.0)
    taps = taps / taps.sum()

    def blur(out_pixels, in_pixels):
        gap = out_pixels[:, None] - in_pixels[None, :]
        inside = np.abs(gap) <= REACH
        return np.where(inside, taps[np.clip(gap + REACH, 0, 2 * REACH)], 0.0)

    across = np.zeros((4 * Q, TILE))
    for n in range(3):
        across[n * Q : (n + 1) * Q] = (blur(pixels, pixels + (n - 1) * TILE) @ interp).T

    out_rows = np.arange(2 * TILE)
    down = np.zeros((2 * TILE, 2 * STACK))
    down[:, :Q] = blur(out_rows, pixels) @ interp
    down[:, Q : Q + REACH] = blur(out_rows, np.arange(-REACH, 0))
    down[:, STACK : STACK + Q] = blur(out_rows, pixels + TILE) @ interp
    down[:, STACK + Q : STACK + Q + REACH] = blur(out_rows, 2 * TILE + np.arange(REACH))
    assert not down[:SPLIT, STACK:].any()

    bf16 = dict(
        forward_rows=forward_rows,
        forward_cols=forward_cols,
        inverse_left=inverse_left,
        edge_left=edge_left,
        inverse_right=right,
        spread_up=spread_up,
        spread_low=spread_low,
        rest=rest,
        across=across,
        down_upper=4.0 * down[:SPLIT, :STACK],
        down_lower=4.0 * down[SPLIT:],
    )
    out = {name: value.astype(ml_dtypes.bfloat16) for name, value in bf16.items()}
    out["rest_mask"] = rest_mask
    return out


def dot(a, b):
    return jnp.dot(a, b, preferred_element_type=F32)


def halves(x):
    high = x.astype(BF16)
    return high, (x - high.astype(F32)).astype(BF16)


def lanes_of(shape):
    return lax.broadcasted_iota(jnp.int32, shape, 1)


def seats(cells, chosen, dest, row):
    count = jnp.int32(0)
    for cell in cells:
        chosen[dest * 16 + count] = cell & (CELLS - 1)
        count = count + ((cell >> 5) == row).astype(jnp.int32)
    return count


def sources(cells, place, at, taken, first):
    for n in range(ROWS + 1):
        taken[n] = jnp.int32(first)
    for n, cell in enumerate(cells):
        source = cell >> 5
        rank = taken[source + 1]
        taken[source + 1] = rank + 1
        place[at + n] = jnp.where(cell >= 0, source * 16 + rank, -1)


def rows_of(dest):
    return [i for i in range(2 * dest - 1, 2 * dest + 3) if 0 <= i < 2 * ROWS]


def window_rows(ids_s, columns):
    cells = []
    for i in range(4):
        tile_row = 2 * lax.axis_index("rows") - 1 + i
        inside = (tile_row >= 0) & (tile_row < 2 * ROWS)
        tile_row = jnp.clip(tile_row, 0, 2 * ROWS - 1)
        cells += [jnp.where(inside, ids_s[j, tile_row], -1) for j in columns]
    return cells


def near_table(ids_s, counts_s, table, chosen, taken):
    row = lax.axis_index("rows")
    start = jnp.int32(0)
    for c in range(COLS):
        table[STARTS + c] = start
        start = start + counts_s[row, c]
    for dest in range(ROWS):
        cells = [ids_s[j, i] for i in rows_of(dest) for j in range(4)]
        count = seats(cells, chosen, dest, row)
        for n in range(NEAR):
            cell = jnp.where(n < count, chosen[dest * 16 + n], CELLS)
            table[SEATS + dest * NEAR + n] = cell
    sources(window_rows(ids_s, range(4)), table, PLACES, taken, 0)


def spectra_kernel(
    mask, ids, dose, fwd_cols, fwd_rows, kernels, weights, counts, threshold,
    out, ker, table, threshold_s,
    mask_v, ids_v, dose_v, cols_v, rows_v, kernels_v, weights_s, counts_s,
    ids_s, chosen, taken, extra, sems,
):
    moves = [(ids, ids_s), (counts, counts_s), (fwd_rows, rows_v)]
    moves += [(mask.at[s], mask_v.at[s]) for s in range(SLOTS)]
    moves += [(kernels, kernels_v), (weights, weights_s), (fwd_cols, cols_v)]
    moves += [(ids, ids_v), (dose, dose_v)]
    copies = [
        pltpu.make_async_copy(src, dst, sems.at[i]) for i, (src, dst) in enumerate(moves)
    ]
    for copy in copies:
        copy.start()
    threshold_s[0] = threshold[0]
    for copy in copies[:2]:
        copy.wait()
    near_table(ids_s, counts_s, table, chosen, taken)
    for copy in copies[2:6]:
        copy.wait()

    pairs = []
    for slot in range(SLOTS):
        if slot == 3:
            for copy in copies[6:]:
                copy.wait()
            for two in range(NK // 2):
                re, im = [], []
                for k in (2 * two, 2 * two + 1):
                    scale = jnp.sqrt(jnp.full((NF, NF), weights_s[k], F32))
                    re.append(kernels_v[0, k] * scale)
                    im.append(kernels_v[1, k] * scale)
                for part, four in enumerate(
                    ([re[0], im[0], re[1], im[1]], [-im[0], re[0], -im[1], re[1]])
                ):
                    block = jnp.concatenate(four, axis=1)
                    turned = [block[n : n + 1] for n in range(NF - 1, HALF, -1)]
                    ker[part, two] = jnp.concatenate([block[: HALF + 1], *turned], axis=0)
        cols = dot(rows_v[...], mask_v[slot])
        high, low = halves(cols[:Q] + cols[Q:])
        pairs.append(jnp.concatenate([high, low], axis=0))

    lane = lanes_of((NF, LANES))
    line = lax.broadcasted_iota(jnp.int32, (NF, LANES), 0)
    even = (lane // NF) % 2 == 0
    in_re = lane == line + Q - HALF - 1
    in_im = lane == line + Q - HALF - 1 + HALF - 1
    column = line > HALF
    lane1 = lanes_of((1, LANES))
    blocks, rows = [], []
    for slot in range(SLOTS):
        both = dot(pairs[slot], cols_v[...])
        both = both[:Q] + both[Q:]
        both = both + pltpu.roll(both, Q, 1)
        top, bottom = both[:NF], both[NF:]
        real = top - pltpu.roll(bottom, NF, 1)
        imag = -(bottom + pltpu.roll(top, NF, 1))
        blocks.append(jnp.where(even, real, pltpu.roll(imag, NF, 1)))
        first = jnp.where(column & in_re, jnp.broadcast_to(real[:, 0:1], (NF, LANES)), 0.0)
        second = jnp.where(column & in_im, jnp.broadcast_to(imag[:, 0:1], (NF, LANES)), 0.0)
        turned = jnp.sum(first + second, axis=0, keepdims=True)
        mean = real[HALF : HALF + 1, HALF : HALF + 1]
        mean = jnp.broadcast_to(mean - mean.astype(BF16).astype(F32), (1, LANES))
        turned = jnp.where(lane1 == Q + 2 * (HALF - 1), mean, turned)
        rows.append(jnp.where(lane1 < Q, blocks[slot][HALF : HALF + 1], turned))
    half = lanes_of((HALF, LANES)) < Q
    packed = [
        jnp.where(half, blocks[2 * i][:HALF], blocks[2 * i + 1][:HALF]).astype(BF16)
        for i in range(SLOTS // 2)
    ]
    extra[...] = jnp.zeros_like(extra)
    for slot in range(SLOTS):
        extra[slot : slot + 1, :] = rows[slot]
    extra[IDS - EXTRA : IDS - EXTRA + 4, 0:16] = ids_v[...].astype(F32)
    at = slice(DOSES - EXTRA, DOSES - EXTRA + 2)
    high = dose_v[...].astype(BF16).astype(F32)
    middle = (dose_v[...] - high).astype(BF16).astype(F32)
    extra[at, 4:8] = high
    extra[at, 8:12] = middle
    extra[at, 12:16] = dose_v[...] - high - middle
    packed.append(extra[...].astype(BF16))
    for c in range(COLS):
        for i in range(4):
            out[c, i * HALF : (i + 1) * HALF, :] = packed[i]


def routing_kernel(
    packets, table,
    out, place,
    held, rests, buffer, chosen, taken,
):
    row, col = lax.axis_index("rows"), lax.axis_index("cols")
    def rest_of(c):
        return packets[c, EXTRA : EXTRA + 16, :].astype(F32)

    before = rest_of(jnp.maximum(col - 1, 0))
    after = rest_of(jnp.minimum(col + 1, COLS - 1))
    line = lax.broadcasted_iota(jnp.int32, (16, LANES), 0)
    first = IDS - EXTRA
    window = jnp.where(
        line == 0, pltpu.roll(before, 16 - first - 3, 0), pltpu.roll(after, 16 - first + 1, 0)
    ).astype(jnp.int32)
    exists = ((line == 0) & (col > 0)) | ((line == 1) & (col < COLS - 1))
    outer = jnp.where(exists, window, -1)
    shift = jnp.where(row > 0, LANES + 1 - 2 * row, 1)
    mine = pltpu.roll(outer, shift, 1)
    ids = [[outer[j, i] for i in range(2 * ROWS)] for j in range(2)]
    own = [[mine[j, i] for i in range(4)] for j in range(2)]

    here = rest_of(col)
    for c in range(COLS):
        rests[c * 16 : (c + 1) * 16, :] = rest_of(c)
    left = lanes_of((HALF, LANES)) < Q
    for c in range(COLS):
        start = table[STARTS + c]
        for s in range(SLOTS):
            pair = packets[c, (s // 2) * HALF : (s // 2 + 1) * HALF, :].astype(F32)
            moved = pltpu.roll(pair, Q, 1)
            both = jnp.where(left, moved, pair) if s % 2 else jnp.where(left, pair, moved)
            held[start + s] = both
            buffer[pl.ds(start + s, 1), :] = rests[c * 16 + s : c * 16 + s + 1, :]
    held[CELLS] = jnp.zeros((HALF, LANES), F32)
    buffer[CELLS : CELLS + 1, :] = jnp.zeros((1, LANES), F32)

    lane = lanes_of((2, LANES))
    at = slice(DOSES - EXTRA, DOSES - EXTRA + 2)
    doses = jnp.where(
        lane < 16,
        before[at],
        jnp.where(lane < 32, pltpu.roll(here[at], 16, 1), pltpu.roll(after[at], 32, 1)),
    )

    def send(dest, cells, at):
        for n in range(0, len(cells), 2):
            one, two = held[cells[n]], held[cells[n + 1]]
            rows = slice(at + n // 2 * HALF, at + (n // 2 + 1) * HALF)
            out[dest, rows, :] = jnp.where(left, one, two).astype(BF16)

    near = [
        [table[SEATS + dest * NEAR + n] for n in range(NEAR)] for dest in range(ROWS)
    ]
    for dest in range(ROWS):
        send(dest, near[dest], 0)
    cells = []
    for i in range(4):
        inside = (2 * row - 1 + i >= 0) & (2 * row - 1 + i < 2 * ROWS)
        cells += [jnp.where(inside, own[j][i], -1) for j in range(2)]
    sources(cells, place, 0, taken, NEAR)
    for dest in range(ROWS):
        cells = [ids[j][i] for i in rows_of(dest) for j in range(2)]
        count = seats(cells, chosen, dest, row)
        cells = [jnp.where(n < count, chosen[dest * 16 + n], CELLS) for n in range(FAR)]
        send(dest, cells, NEAR // 2 * HALF)
        rows = [buffer[pl.ds(cell, 1), :] for cell in near[dest] + cells]
        out[dest, REST : REST + 16, :] = jnp.concatenate(rows + [doses], axis=0).astype(BF16)


def develop_kernel(
    tiles, table, place, ker, threshold, spread_up, spread_low, rest, rest_mask,
    inv_left, edge_left, inv_right, across, down_upper, down_lower,
    out,
    after_rows, stage, sems,
):
    row = lax.axis_index("rows")
    for source in range(ROWS):
        at = slice(source * 16, (source + 1) * 16)
        after_rows[at, :] = tiles[source, REST : REST + 16, :].astype(F32)
    left = lanes_of((HALF, LANES)) < Q
    first = lax.broadcasted_iota(jnp.int32, (HALF, LANES), 0) == 0
    held, paired, rests = [], [], []
    for t in range(0, WINDOW, 2):
        both = []
        for n in (t, t + 1):
            i, j = n // 6, n % 6
            found = table[PLACES + 4 * i + j - 1] if 1 <= j < 5 else place[2 * i + j // 5]
            here = jnp.maximum(found, 0)
            rank = here & 15
            at = pl.multiple_of((rank >> 1) * HALF, HALF)
            pair = tiles[here >> 4, pl.ds(at, HALF), :].astype(F32)
            tile = jnp.where((rank & 1) == (n & 1), pair, pltpu.roll(pair, Q, 1))
            both.append(jnp.where(found >= 0, tile, 0.0))
            line = jnp.where(found >= 0, after_rows[pl.ds(here, 1), :], 0.0)
            rests.append(jnp.broadcast_to(line, (HALF, LANES)) * rest_mask[...])
        pair = jnp.where(left, both[0], both[1])
        held.append(pair.astype(BF16))
        paired.append(jnp.where(first, 0.0, pair).astype(BF16))
    held = jnp.concatenate(held, axis=0)
    paired = jnp.concatenate(paired, axis=0)
    upper = dot(held, spread_up[...])
    lower = dot(paired, spread_low[...])
    rests = dot(jnp.concatenate(rests, axis=0).astype(BF16), rest[...])

    def doses(source):
        info = after_rows[pl.ds(pl.multiple_of(source * 16, 16), 16), :][MOST:]
        return info + pltpu.roll(info, LANES - 4, 1) + pltpu.roll(info, LANES - 8, 1)

    own = doses(row)
    above = doses(jnp.maximum(row - 1, 0))
    below = doses(jnp.minimum(row + 1, ROWS - 1))

    def picture(i, j):
        whole_tile = i in (1, 2)
        m, t = 3 * i + j // 2, 6 * i + j
        a, r = slice(m * HALF, (m + 1) * HALF), slice(t * HALF, (t + 1) * HALF)
        re = slice((j % 2) * 2 * LANES, (j % 2) * 2 * LANES + LANES)
        im = slice(re.stop, re.stop + LANES)
        real = jnp.concatenate([upper[a, re], lower[a, re] + rests[r, :LANES]], axis=0)
        imag = jnp.concatenate([upper[a, im], lower[a, im] + rests[r, LANES:]], axis=0)
        prods = []
        for two in range(NK // 2):
            ka, kb = ker[0, two], ker[1, two]
            prod = jnp.concatenate([ka * real + kb * imag, ka * imag - kb * real], axis=0)
            prods.append(prod.astype(BF16))
        prod = jnp.concatenate(prods, axis=1)
        half = dot(inv_left[...] if whole_tile else edge_left[...], prod)
        if not whole_tile:
            half = half[:REACH] if i == 0 else half[REACH:]
        return jnp.concatenate(
            [half[:, n * LANES : (n + 1) * LANES] for n in range(NK // 2)], axis=0
        ).astype(BF16)

    def intensity(halfway):
        field = dot(halfway, inv_right[...])
        power = field * field
        power = power[:, :LANES] + power[:, LANES:]
        height = power.shape[0] // (NK // 2)
        total = power[:height]
        for n in range(1, NK // 2):
            total = total + power[n * height : (n + 1) * height]
        return total + pltpu.roll(total, Q, 1)

    lane_of = [7] + [20 + j for j in range(4)] + [36]
    dose_rows = [above[1:2], own[0:1], own[1:2], below[0:1]]
    left = lanes_of((STACK, LANES)) < Q

    images = {}
    for group in ((0, 3), (1,), (2,)):
        halfway = {(i, j): picture(i, j) for i in group for j in range(6)}
        for i in group:
            for j in range(6):
                scale = dose_rows[i][:, lane_of[j] : lane_of[j] + 1]
                images[i, j] = intensity(halfway[i, j]) * scale

    def columns(strip, tile):
        none = jnp.zeros((REACH, LANES), F32)
        stack = [
            jnp.concatenate([images[tile, j], images[strip, j], none], axis=0) for j in range(6)
        ]
        wide = []
        for j in range(1, 5):
            two = jnp.where(left, stack[j - 1], stack[j])
            three = jnp.concatenate([two, stack[j + 1]], axis=1).astype(BF16)
            wide.append(dot(three, across[...]).astype(BF16))
        return jnp.concatenate(wide, axis=1)

    shift = 4.0 * threshold[0]
    copies = []

    def finish(start, stop, level):
        rows = slice(start, stop)
        stage[rows, :] = (0.5 * jnp.tanh(level - shift) + 0.5).astype(BF16)
        copy = pltpu.make_async_copy(stage.at[rows, :], out.at[rows, :], sems.at[len(copies)])
        copy.start()
        copies.append(copy)

    upper_rows = columns(0, 1)
    finish(0, SPLIT, dot(down_upper[...], upper_rows))
    both_rows = jnp.concatenate([upper_rows, columns(3, 2)], axis=0)
    middle = SPLIT + 192
    finish(SPLIT, middle, dot(down_lower[: middle - SPLIT, :], both_rows))
    finish(middle, 2 * TILE, dot(down_lower[middle - SPLIT :, :], both_rows))
    for copy in copies:
        copy.wait()


PARAMS = pltpu.CompilerParams(vmem_limit_bytes=48 * 1024 * 1024)
IN_HBM = pl.BlockSpec(memory_space=pltpu.HBM)
IN_VMEM = pl.BlockSpec(memory_space=pltpu.VMEM)
IN_SMEM = pl.BlockSpec(memory_space=pltpu.SMEM)


def spectra(masks, cell_ids, dose, kernels, kernel_weights, owned_counts, threshold):
    table = tables()
    operands = [masks, cell_ids.T, dose]
    operands += [jnp.asarray(table[n]) for n in ("forward_cols", "forward_rows")]
    operands += [kernels, kernel_weights, owned_counts, threshold]
    in_hbm = [pltpu.with_memory_space_constraint(op, pltpu.HBM) for op in operands[:-1]]
    in_hbm.append(operands[-1])
    return pl.pallas_call(
        spectra_kernel,
        out_shape=(
            jax.ShapeDtypeStruct((COLS, PACKET, LANES), BF16),
            jax.ShapeDtypeStruct((2, NK // 2, NF, LANES), F32),
            pltpu.SMEM((PLACES + 16,), jnp.int32),
            pltpu.SMEM((1,), F32),
        ),
        in_specs=[IN_HBM] * (len(operands) - 1) + [IN_SMEM],
        out_specs=(IN_VMEM, IN_VMEM, IN_SMEM, IN_SMEM),
        scratch_shapes=[
            *[pltpu.VMEM(op.shape, op.dtype) for op in operands[:-3]],
            *[pltpu.SMEM(op.shape, op.dtype) for op in operands[-3:-1]],
            pltpu.SMEM((4, 2 * ROWS), jnp.int32),
            pltpu.SMEM((ROWS * 16 + 16,), jnp.int32),
            pltpu.SMEM((16,), jnp.int32),
            pltpu.VMEM((16, LANES), F32),
            pltpu.SemaphoreType.DMA((len(operands) + SLOTS - 1,)),
        ],
        compiler_params=PARAMS,
    )(*in_hbm)


def route(packets, seating):
    return pl.pallas_call(
        routing_kernel,
        out_shape=(
            jax.ShapeDtypeStruct((ROWS, OUTGOING, LANES), BF16),
            pltpu.SMEM((8,), jnp.int32),
        ),
        in_specs=[IN_VMEM, IN_SMEM],
        out_specs=(IN_VMEM, IN_SMEM),
        scratch_shapes=[
            pltpu.VMEM((CELLS + SLOTS, HALF, LANES), F32),
            pltpu.VMEM((COLS * 16, LANES), F32),
            pltpu.VMEM((CELLS + 8, LANES), F32),
            pltpu.SMEM((ROWS * 16 + 16,), jnp.int32),
            pltpu.SMEM((16,), jnp.int32),
        ],
        compiler_params=PARAMS,
    )(packets, seating)


def develop(incoming, seating, place, ker, threshold):
    table = tables()
    names = ("spread_up", "spread_low", "rest", "rest_mask")
    names += ("inverse_left", "edge_left", "inverse_right", "across", "down_upper", "down_lower")
    constants = [jnp.asarray(table[n]) for n in names]
    return pl.pallas_call(
        develop_kernel,
        out_shape=jax.ShapeDtypeStruct((2 * TILE, 4 * TILE), BF16),
        in_specs=[IN_VMEM, IN_SMEM, IN_SMEM, IN_VMEM, IN_SMEM, *[IN_VMEM] * len(constants)],
        out_specs=IN_HBM,
        scratch_shapes=[
            pltpu.VMEM((ROWS * 16, LANES), F32),
            pltpu.VMEM((2 * TILE, 4 * TILE), BF16),
            pltpu.SemaphoreType.DMA((3,)),
        ],
        compiler_params=PARAMS,
    )(incoming, seating, place, ker, threshold, *constants)


def local(masks, owned_counts, cell_ids, kernels, kernel_weights, dose, threshold):
    packet, ker, seating, threshold = spectra(
        masks, cell_ids, dose, kernels, kernel_weights, owned_counts, threshold
    )
    packets = lax.all_to_all(packet, "cols", split_axis=0, concat_axis=0, tiled=True)
    outgoing, place = route(packets, seating)
    incoming = lax.all_to_all(outgoing, "rows", split_axis=0, concat_axis=0, tiled=True)
    return develop(incoming, seating, place, ker, threshold)


def solution(mesh):
    return jax.shard_map(
        local,
        mesh=mesh,
        in_specs=(
            P(("rows", "cols"), None, None),
            P(),
            P(None, "cols"),
            P(),
            P(),
            P("rows", "cols"),
            P(),
        ),
        out_specs=P("rows", "cols"),
        check_vma=False,
    )
```

```python
import functools

import jax
import jax.numpy as jnp
import ml_dtypes
import numpy as np
from jax import lax
from jax.experimental import pallas as pl
from jax.experimental.pallas import tpu as pltpu
from jax.sharding import PartitionSpec as P

REACH = 8
TILE = 384
NF = 32
NK = 16
Q = 64
SLOTS = 6
ROWS = 8
COLS = 16
CELLS = 32
LANES = 128
FORWARD = NF + 8
HALF = NF // 2
EXTRA = 3 * HALF
IDS = EXTRA + SLOTS
DOSES = IDS + 4
PACKET = EXTRA + 16
WINDOW = 4 * 6
NEAR = 6
FAR = 8
MOST = NEAR + FAR
REST = MOST * HALF // 2
OUTGOING = REST + 16
STARTS, SEATS, PLACES = 0, COLS, COLS + ROWS * NEAR
STACK = Q + 2 * REACH
SPLIT = TILE - 2 * REACH
BF16 = jnp.bfloat16
F32 = jnp.float32


def split(table):
    high = table.astype(ml_dtypes.bfloat16)
    low = (table - high.astype(np.float64)).astype(ml_dtypes.bfloat16)
    return high, low


@functools.lru_cache(maxsize=None)
def tables():
    freq = np.arange(NF) - NF // 2
    pixels = np.arange(TILE)
    points = np.arange(Q)
    turn = np.mod(freq[:, None] * pixels[None, :], TILE) * (2.0 * np.pi / TILE)
    forward = np.concatenate([np.cos(turn), np.sin(turn)]) / TILE
    high, low = split(forward)
    forward_cols = np.ascontiguousarray(np.concatenate([high, low]).T)
    turn = np.mod(freq[: HALF + 1, None] * pixels[None, :], TILE) * (2.0 * np.pi / TILE)
    forward = np.zeros((FORWARD, TILE))
    forward[:HALF] = np.cos(turn[:HALF])
    forward[HALF:NF] = -np.sin(turn[:HALF])
    forward[NF] = np.cos(turn[HALF])
    forward_rows = np.concatenate(split(forward / TILE))

    turn = np.mod(points[:, None] * freq[None, :], Q) * (2.0 * np.pi / Q)
    cos, sin = np.cos(turn), np.sin(turn)
    order = np.concatenate([np.arange(HALF + 1), np.arange(NF - 1, HALF, -1)])
    inverse_left = np.concatenate([cos[:, order], -sin[:, order]], axis=1)
    edges = np.concatenate([np.arange(TILE - REACH, TILE), np.arange(REACH)])
    turn = np.mod(edges[:, None] * freq[None, :], TILE) * (2.0 * np.pi / TILE)
    edge_left = np.concatenate([np.cos(turn)[:, order], -np.sin(turn)[:, order]], axis=1)
    right = np.zeros((LANES, 2 * LANES))
    for k in range(2):
        re = slice(2 * k * NF, (2 * k + 1) * NF)
        im = slice((2 * k + 1) * NF, (2 * k + 2) * NF)
        out_re = slice(k * LANES, k * LANES + Q)
        out_im = slice(k * LANES + Q, (k + 1) * LANES)
        right[re, out_re], right[re, out_im] = cos.T, sin.T
        right[im, out_re], right[im, out_im] = -sin.T, cos.T

    spread_up = np.zeros((LANES, 4 * LANES))
    spread_low = np.zeros((LANES, 4 * LANES))
    rest = np.zeros((LANES, 2 * LANES))
    for copy in range(4):
        for part in range(2):
            for b in range(NF):
                for tile in range(2):
                    lane = tile * Q + part * NF + b
                    base = tile * 2 * LANES + part * LANES + copy * NF
                    spread_up[lane, base + b] = 1.0
                    if b:
                        spread_low[lane, base + NF - b] = -1.0 if part else 1.0
                rest[part * NF + b, part * LANES + copy * NF + b] = 1.0
            for i in range(1, HALF):
                rest[Q + part * (HALF - 1) + i - 1, part * LANES + copy * NF] = 1.0
        rest[Q + 2 * (HALF - 1), copy * NF + HALF] = 1.0
    rest_mask = np.zeros((HALF, LANES), np.float32)
    rest_mask[0, :Q] = rest_mask[0, Q + 2 * (HALF - 1)] = 1.0
    for i in range(1, HALF):
        rest_mask[HALF - i, Q + i - 1] = rest_mask[HALF - i, Q + HALF - 1 + i - 1] = 1.0

    harmonic = np.arange(Q) - Q // 2
    fine = np.mod(pixels[:, None] * harmonic[None, :], TILE) * (2.0 * np.pi / TILE)
    grid = np.mod(points[:, None] * harmonic[None, :], Q) * (2.0 * np.pi / Q)
    interp = (np.cos(fine) @ np.cos(grid).T + np.sin(fine) @ np.sin(grid).T) / Q
    interp = interp.astype(ml_dtypes.bfloat16).astype(np.float64)

    offsets = np.arange(2 * REACH + 1) - REACH
    taps = np.exp(-offsets * offsets / 32.0)
    taps = taps / taps.sum()

    def blur(out_pixels, in_pixels):
        gap = out_pixels[:, None] - in_pixels[None, :]
        inside = np.abs(gap) <= REACH
        return np.where(inside, taps[np.clip(gap + REACH, 0, 2 * REACH)], 0.0)

    across = np.zeros((4 * Q, TILE))
    for n in range(3):
        across[n * Q : (n + 1) * Q] = (blur(pixels, pixels + (n - 1) * TILE) @ interp).T

    out_rows = np.arange(2 * TILE)
    down = np.zeros((2 * TILE, 2 * STACK))
    down[:, :Q] = blur(out_rows, pixels) @ interp
    down[:, Q : Q + REACH] = blur(out_rows, np.arange(-REACH, 0))
    down[:, STACK : STACK + Q] = blur(out_rows, pixels + TILE) @ interp
    down[:, STACK + Q : STACK + Q + REACH] = blur(out_rows, 2 * TILE + np.arange(REACH))
    assert not down[:SPLIT, STACK:].any()

    bf16 = dict(
        forward_rows=forward_rows,
        forward_cols=forward_cols,
        inverse_left=inverse_left,
        edge_left=edge_left,
        inverse_right=right,
        spread_up=spread_up,
        spread_low=spread_low,
        rest=rest,
        across=across,
        down_upper=4.0 * down[:SPLIT, :STACK],
        down_lower=4.0 * down[SPLIT:],
    )
    out = {name: value.astype(ml_dtypes.bfloat16) for name, value in bf16.items()}
    out["rest_mask"] = rest_mask
    return out


def dot(a, b):
    return jnp.dot(a, b, preferred_element_type=F32)


def halves(x):
    high = x.astype(BF16)
    return high, (x - high.astype(F32)).astype(BF16)


def lanes_of(shape):
    return lax.broadcasted_iota(jnp.int32, shape, 1)


def seats(cells, chosen, dest, row):
    count = jnp.int32(0)
    for cell in cells:
        chosen[dest * 16 + count] = cell & (CELLS - 1)
        count = count + ((cell >> 5) == row).astype(jnp.int32)
    return count


def sources(cells, place, at, taken, first):
    for n in range(ROWS + 1):
        taken[n] = jnp.int32(first)
    for n, cell in enumerate(cells):
        source = cell >> 5
        rank = taken[source + 1]
        taken[source + 1] = rank + 1
        place[at + n] = jnp.where(cell >= 0, source * 16 + rank, -1)


def rows_of(dest):
    return [i for i in range(2 * dest - 1, 2 * dest + 3) if 0 <= i < 2 * ROWS]


def window_rows(ids_s, columns):
    cells = []
    for i in range(4):
        tile_row = 2 * lax.axis_index("rows") - 1 + i
        inside = (tile_row >= 0) & (tile_row < 2 * ROWS)
        tile_row = jnp.clip(tile_row, 0, 2 * ROWS - 1)
        cells += [jnp.where(inside, ids_s[j, tile_row], -1) for j in columns]
    return cells


def near_table(ids_s, counts_s, table, chosen, taken):
    row = lax.axis_index("rows")
    start = jnp.int32(0)
    for c in range(COLS):
        table[STARTS + c] = start
        start = start + counts_s[row, c]
    for dest in range(ROWS):
        cells = [ids_s[j, i] for i in rows_of(dest) for j in range(4)]
        count = seats(cells, chosen, dest, row)
        for n in range(NEAR):
            cell = jnp.where(n < count, chosen[dest * 16 + n], CELLS)
            table[SEATS + dest * NEAR + n] = cell
    sources(window_rows(ids_s, range(4)), table, PLACES, taken, 0)


def spectra_kernel(
    mask, ids, dose, fwd_cols, fwd_rows, kernels, weights, counts, threshold,
    out, ker, table, threshold_s,
    mask_v, ids_v, dose_v, cols_v, rows_v, kernels_v, weights_s, counts_s,
    ids_s, chosen, taken, extra, sems,
):
    moves = [(ids, ids_s), (counts, counts_s), (fwd_rows, rows_v)]
    moves += [(mask.at[s], mask_v.at[s]) for s in range(SLOTS)]
    moves += [(kernels, kernels_v), (weights, weights_s), (fwd_cols, cols_v)]
    moves += [(ids, ids_v), (dose, dose_v)]
    copies = [
        pltpu.make_async_copy(src, dst, sems.at[i]) for i, (src, dst) in enumerate(moves)
    ]
    for copy in copies:
        copy.start()
    threshold_s[0] = threshold[0]
    for copy in copies[:2]:
        copy.wait()
    near_table(ids_s, counts_s, table, chosen, taken)
    for copy in copies[2:6]:
        copy.wait()

    pairs = []
    for slot in range(SLOTS):
        if slot == 3:
            for copy in copies[6:]:
                copy.wait()
            for two in range(NK // 2):
                re, im = [], []
                for k in (2 * two, 2 * two + 1):
                    scale = jnp.sqrt(jnp.full((NF, NF), weights_s[k], F32))
                    re.append(kernels_v[0, k] * scale)
                    im.append(kernels_v[1, k] * scale)
                for part, four in enumerate(
                    ([re[0], im[0], re[1], im[1]], [-im[0], re[0], -im[1], re[1]])
                ):
                    block = jnp.concatenate(four, axis=1)
                    turned = [block[n : n + 1] for n in range(NF - 1, HALF, -1)]
                    ker[part, two] = jnp.concatenate([block[: HALF + 1], *turned], axis=0)
        cols = dot(rows_v[...], mask_v[slot])
        cols = cols[:FORWARD] + cols[FORWARD:]
        high = cols.astype(BF16).astype(F32)
        pairs.append(jnp.concatenate([high, cols - high], axis=0).astype(BF16))

    lane = lanes_of((HALF, LANES))
    line = lax.broadcasted_iota(jnp.int32, (HALF, LANES), 0)
    even = (lane // NF) % 2 == 0
    in_re = (lane == Q + HALF - 1 - line) & (line > 0)
    in_im = (lane == Q + 2 * (HALF - 1) - line) & (line > 0)
    lane1 = lanes_of((1, LANES))
    blocks, rows = [], []
    for slot in range(SLOTS):
        both = dot(pairs[slot], cols_v[...])
        both = both[:FORWARD] + both[FORWARD:]
        both = both + pltpu.roll(both, Q, 1)
        cos, sin, zero = both[:HALF], both[HALF:NF], both[NF : NF + 1]
        cos_sin, sin_sin = pltpu.roll(cos, NF, 1), pltpu.roll(sin, NF, 1)
        real = cos + sin_sin
        imag = sin - cos_sin
        blocks.append(jnp.where(even, real, pltpu.roll(imag, NF, 1)))
        first = jnp.broadcast_to((cos - sin_sin)[:, 0:1], (HALF, LANES))
        second = jnp.broadcast_to(-(sin + cos_sin)[:, 0:1], (HALF, LANES))
        turned = jnp.where(in_re, first, 0.0) + jnp.where(in_im, second, 0.0)
        turned = jnp.sum(turned, axis=0, keepdims=True)
        mean = zero[:, HALF : HALF + 1]
        mean = jnp.broadcast_to(mean - mean.astype(BF16).astype(F32), (1, LANES))
        turned = jnp.where(lane1 == Q + 2 * (HALF - 1), mean, turned)
        rows.append(jnp.where(lane1 < NF, zero, jnp.where(lane1 < Q, -zero, turned)))
    half = lanes_of((HALF, LANES)) < Q
    packed = [
        jnp.where(half, blocks[2 * i], blocks[2 * i + 1]).astype(BF16)
        for i in range(SLOTS // 2)
    ]
    extra[...] = jnp.zeros_like(extra)
    for slot in range(SLOTS):
        extra[slot : slot + 1, :] = rows[slot]
    extra[IDS - EXTRA : IDS - EXTRA + 4, 0:16] = ids_v[...].astype(F32)
    at = slice(DOSES - EXTRA, DOSES - EXTRA + 2)
    high = dose_v[...].astype(BF16).astype(F32)
    middle = (dose_v[...] - high).astype(BF16).astype(F32)
    extra[at, 4:8] = high
    extra[at, 8:12] = middle
    extra[at, 12:16] = dose_v[...] - high - middle
    packed.append(extra[...].astype(BF16))
    for c in range(COLS):
        for i in range(4):
            out[c, i * HALF : (i + 1) * HALF, :] = packed[i]


def routing_kernel(
    packets, table,
    out, place,
    held, rests, buffer, chosen, taken,
):
    row, col = lax.axis_index("rows"), lax.axis_index("cols")
    def rest_of(c):
        return packets[c, EXTRA : EXTRA + 16, :].astype(F32)

    before = rest_of(jnp.maximum(col - 1, 0))
    after = rest_of(jnp.minimum(col + 1, COLS - 1))
    line = lax.broadcasted_iota(jnp.int32, (16, LANES), 0)
    first = IDS - EXTRA
    window = jnp.where(
        line == 0, pltpu.roll(before, 16 - first - 3, 0), pltpu.roll(after, 16 - first + 1, 0)
    ).astype(jnp.int32)
    exists = ((line == 0) & (col > 0)) | ((line == 1) & (col < COLS - 1))
    outer = jnp.where(exists, window, -1)
    shift = jnp.where(row > 0, LANES + 1 - 2 * row, 1)
    mine = pltpu.roll(outer, shift, 1)
    ids = [[outer[j, i] for i in range(2 * ROWS)] for j in range(2)]
    own = [[mine[j, i] for i in range(4)] for j in range(2)]

    here = rest_of(col)
    for c in range(COLS):
        rests[c * 16 : (c + 1) * 16, :] = rest_of(c)
    left = lanes_of((HALF, LANES)) < Q
    for c in range(COLS):
        start = table[STARTS + c]
        for s in range(SLOTS):
            pair = packets[c, (s // 2) * HALF : (s // 2 + 1) * HALF, :].astype(F32)
            moved = pltpu.roll(pair, Q, 1)
            both = jnp.where(left, moved, pair) if s % 2 else jnp.where(left, pair, moved)
            held[start + s] = both
            buffer[pl.ds(start + s, 1), :] = rests[c * 16 + s : c * 16 + s + 1, :]
    held[CELLS] = jnp.zeros((HALF, LANES), F32)
    buffer[CELLS : CELLS + 1, :] = jnp.zeros((1, LANES), F32)

    lane = lanes_of((2, LANES))
    at = slice(DOSES - EXTRA, DOSES - EXTRA + 2)
    doses = jnp.where(
        lane < 16,
        before[at],
        jnp.where(lane < 32, pltpu.roll(here[at], 16, 1), pltpu.roll(after[at], 32, 1)),
    )

    def send(dest, cells, at):
        for n in range(0, len(cells), 2):
            one, two = held[cells[n]], held[cells[n + 1]]
            rows = slice(at + n // 2 * HALF, at + (n // 2 + 1) * HALF)
            out[dest, rows, :] = jnp.where(left, one, two).astype(BF16)

    near = [
        [table[SEATS + dest * NEAR + n] for n in range(NEAR)] for dest in range(ROWS)
    ]
    for dest in range(ROWS):
        send(dest, near[dest], 0)
    cells = []
    for i in range(4):
        inside = (2 * row - 1 + i >= 0) & (2 * row - 1 + i < 2 * ROWS)
        cells += [jnp.where(inside, own[j][i], -1) for j in range(2)]
    sources(cells, place, 0, taken, NEAR)
    for dest in range(ROWS):
        cells = [ids[j][i] for i in rows_of(dest) for j in range(2)]
        count = seats(cells, chosen, dest, row)
        cells = [jnp.where(n < count, chosen[dest * 16 + n], CELLS) for n in range(FAR)]
        send(dest, cells, NEAR // 2 * HALF)
        rows = [buffer[pl.ds(cell, 1), :] for cell in near[dest] + cells]
        out[dest, REST : REST + 16, :] = jnp.concatenate(rows + [doses], axis=0).astype(BF16)


def develop_kernel(
    tiles, table, place, ker, threshold, spread_up, spread_low, rest, rest_mask,
    inv_left, edge_left, inv_right, across, down_upper, down_lower,
    out,
    after_rows, stage, sems,
):
    row = lax.axis_index("rows")
    for source in range(ROWS):
        at = slice(source * 16, (source + 1) * 16)
        after_rows[at, :] = tiles[source, REST : REST + 16, :].astype(F32)
    left = lanes_of((HALF, LANES)) < Q
    first = lax.broadcasted_iota(jnp.int32, (HALF, LANES), 0) == 0
    held, paired, rests = [], [], []
    for t in range(0, WINDOW, 2):
        both = []
        for n in (t, t + 1):
            i, j = n // 6, n % 6
            found = table[PLACES + 4 * i + j - 1] if 1 <= j < 5 else place[2 * i + j // 5]
            here = jnp.maximum(found, 0)
            rank = here & 15
            at = pl.multiple_of((rank >> 1) * HALF, HALF)
            pair = tiles[here >> 4, pl.ds(at, HALF), :].astype(F32)
            tile = jnp.where((rank & 1) == (n & 1), pair, pltpu.roll(pair, Q, 1))
            both.append(jnp.where(found >= 0, tile, 0.0))
            line = jnp.where(found >= 0, after_rows[pl.ds(here, 1), :], 0.0)
            rests.append(jnp.broadcast_to(line, (HALF, LANES)) * rest_mask[...])
        pair = jnp.where(left, both[0], both[1])
        held.append(pair.astype(BF16))
        paired.append(jnp.where(first, 0.0, pair).astype(BF16))
    held = jnp.concatenate(held, axis=0)
    paired = jnp.concatenate(paired, axis=0)
    upper = dot(held, spread_up[...])
    lower = dot(paired, spread_low[...])
    rests = dot(jnp.concatenate(rests, axis=0).astype(BF16), rest[...])

    def doses(source):
        info = after_rows[pl.ds(pl.multiple_of(source * 16, 16), 16), :][MOST:]
        return info + pltpu.roll(info, LANES - 4, 1) + pltpu.roll(info, LANES - 8, 1)

    own = doses(row)
    above = doses(jnp.maximum(row - 1, 0))
    below = doses(jnp.minimum(row + 1, ROWS - 1))

    def picture(i, j):
        whole_tile = i in (1, 2)
        m, t = 3 * i + j // 2, 6 * i + j
        a, r = slice(m * HALF, (m + 1) * HALF), slice(t * HALF, (t + 1) * HALF)
        re = slice((j % 2) * 2 * LANES, (j % 2) * 2 * LANES + LANES)
        im = slice(re.stop, re.stop + LANES)
        real = jnp.concatenate([upper[a, re], lower[a, re] + rests[r, :LANES]], axis=0)
        imag = jnp.concatenate([upper[a, im], lower[a, im] + rests[r, LANES:]], axis=0)
        prods = []
        for two in range(NK // 2):
            ka, kb = ker[0, two], ker[1, two]
            prod = jnp.concatenate([ka * real + kb * imag, ka * imag - kb * real], axis=0)
            prods.append(prod.astype(BF16))
        prod = jnp.concatenate(prods, axis=1)
        half = dot(inv_left[...] if whole_tile else edge_left[...], prod)
        if not whole_tile:
            half = half[:REACH] if i == 0 else half[REACH:]
        return jnp.concatenate(
            [half[:, n * LANES : (n + 1) * LANES] for n in range(NK // 2)], axis=0
        ).astype(BF16)

    def intensity(halfway):
        field = dot(halfway, inv_right[...])
        power = field * field
        power = power[:, :LANES] + power[:, LANES:]
        height = power.shape[0] // (NK // 2)
        total = power[:height]
        for n in range(1, NK // 2):
            total = total + power[n * height : (n + 1) * height]
        return total + pltpu.roll(total, Q, 1)

    lane_of = [7] + [20 + j for j in range(4)] + [36]
    dose_rows = [above[1:2], own[0:1], own[1:2], below[0:1]]
    left = lanes_of((STACK, LANES)) < Q

    images = {}
    for group in ((0, 3), (1,), (2,)):
        halfway = {(i, j): picture(i, j) for i in group for j in range(6)}
        for i in group:
            for j in range(6):
                scale = dose_rows[i][:, lane_of[j] : lane_of[j] + 1]
                images[i, j] = intensity(halfway[i, j]) * scale

    def columns(strip, tile):
        none = jnp.zeros((REACH, LANES), F32)
        stack = [
            jnp.concatenate([images[tile, j], images[strip, j], none], axis=0) for j in range(6)
        ]
        wide = []
        for j in range(1, 5):
            two = jnp.where(left, stack[j - 1], stack[j])
            three = jnp.concatenate([two, stack[j + 1]], axis=1).astype(BF16)
            wide.append(dot(three, across[...]).astype(BF16))
        return jnp.concatenate(wide, axis=1)

    shift = 4.0 * threshold[0]
    copies = []

    def finish(start, stop, level):
        rows = slice(start, stop)
        stage[rows, :] = (0.5 * jnp.tanh(level - shift) + 0.5).astype(BF16)
        copy = pltpu.make_async_copy(stage.at[rows, :], out.at[rows, :], sems.at[len(copies)])
        copy.start()
        copies.append(copy)

    upper_rows = columns(0, 1)
    finish(0, SPLIT, dot(down_upper[...], upper_rows))
    both_rows = jnp.concatenate([upper_rows, columns(3, 2)], axis=0)
    middle = SPLIT + 192
    finish(SPLIT, middle, dot(down_lower[: middle - SPLIT, :], both_rows))
    finish(middle, 2 * TILE, dot(down_lower[middle - SPLIT :, :], both_rows))
    for copy in copies:
        copy.wait()


PARAMS = pltpu.CompilerParams(vmem_limit_bytes=48 * 1024 * 1024)
IN_HBM = pl.BlockSpec(memory_space=pltpu.HBM)
IN_VMEM = pl.BlockSpec(memory_space=pltpu.VMEM)
IN_SMEM = pl.BlockSpec(memory_space=pltpu.SMEM)


def spectra(masks, cell_ids, dose, kernels, kernel_weights, owned_counts, threshold):
    table = tables()
    operands = [masks, cell_ids.T, dose]
    operands += [jnp.asarray(table[n]) for n in ("forward_cols", "forward_rows")]
    operands += [kernels, kernel_weights, owned_counts, threshold]
    in_hbm = [pltpu.with_memory_space_constraint(op, pltpu.HBM) for op in operands[:-1]]
    in_hbm.append(operands[-1])
    return pl.pallas_call(
        spectra_kernel,
        out_shape=(
            jax.ShapeDtypeStruct((COLS, PACKET, LANES), BF16),
            jax.ShapeDtypeStruct((2, NK // 2, NF, LANES), F32),
            pltpu.SMEM((PLACES + 16,), jnp.int32),
            pltpu.SMEM((1,), F32),
        ),
        in_specs=[IN_HBM] * (len(operands) - 1) + [IN_SMEM],
        out_specs=(IN_VMEM, IN_VMEM, IN_SMEM, IN_SMEM),
        scratch_shapes=[
            *[pltpu.VMEM(op.shape, op.dtype) for op in operands[:-3]],
            *[pltpu.SMEM(op.shape, op.dtype) for op in operands[-3:-1]],
            pltpu.SMEM((4, 2 * ROWS), jnp.int32),
            pltpu.SMEM((ROWS * 16 + 16,), jnp.int32),
            pltpu.SMEM((16,), jnp.int32),
            pltpu.VMEM((16, LANES), F32),
            pltpu.SemaphoreType.DMA((len(operands) + SLOTS - 1,)),
        ],
        compiler_params=PARAMS,
    )(*in_hbm)


def route(packets, seating):
    return pl.pallas_call(
        routing_kernel,
        out_shape=(
            jax.ShapeDtypeStruct((ROWS, OUTGOING, LANES), BF16),
            pltpu.SMEM((8,), jnp.int32),
        ),
        in_specs=[IN_VMEM, IN_SMEM],
        out_specs=(IN_VMEM, IN_SMEM),
        scratch_shapes=[
            pltpu.VMEM((CELLS + SLOTS, HALF, LANES), F32),
            pltpu.VMEM((COLS * 16, LANES), F32),
            pltpu.VMEM((CELLS + 8, LANES), F32),
            pltpu.SMEM((ROWS * 16 + 16,), jnp.int32),
            pltpu.SMEM((16,), jnp.int32),
        ],
        compiler_params=PARAMS,
    )(packets, seating)


def develop(incoming, seating, place, ker, threshold):
    table = tables()
    names = ("spread_up", "spread_low", "rest", "rest_mask")
    names += ("inverse_left", "edge_left", "inverse_right", "across", "down_upper", "down_lower")
    constants = [jnp.asarray(table[n]) for n in names]
    return pl.pallas_call(
        develop_kernel,
        out_shape=jax.ShapeDtypeStruct((2 * TILE, 4 * TILE), BF16),
        in_specs=[IN_VMEM, IN_SMEM, IN_SMEM, IN_VMEM, IN_SMEM, *[IN_VMEM] * len(constants)],
        out_specs=IN_HBM,
        scratch_shapes=[
            pltpu.VMEM((ROWS * 16, LANES), F32),
            pltpu.VMEM((2 * TILE, 4 * TILE), BF16),
            pltpu.SemaphoreType.DMA((3,)),
        ],
        compiler_params=PARAMS,
    )(incoming, seating, place, ker, threshold, *constants)


def local(masks, owned_counts, cell_ids, kernels, kernel_weights, dose, threshold):
    packet, ker, seating, threshold = spectra(
        masks, cell_ids, dose, kernels, kernel_weights, owned_counts, threshold
    )
    packets = lax.all_to_all(packet, "cols", split_axis=0, concat_axis=0, tiled=True)
    outgoing, place = route(packets, seating)
    incoming = lax.all_to_all(outgoing, "rows", split_axis=0, concat_axis=0, tiled=True)
    return develop(incoming, seating, place, ker, threshold)


def solution(mesh):
    return jax.shard_map(
        local,
        mesh=mesh,
        in_specs=(
            P(("rows", "cols"), None, None),
            P(),
            P(None, "cols"),
            P(),
            P(),
            P("rows", "cols"),
            P(),
        ),
        out_specs=P("rows", "cols"),
        check_vma=False,
    )
```

```python
import functools

import jax
import jax.numpy as jnp
import ml_dtypes
import numpy as np
from jax import lax
from jax.experimental import pallas as pl
from jax.experimental.pallas import tpu as pltpu
from jax.sharding import PartitionSpec as P

REACH = 8
TILE = 384
NF = 32
NK = 16
Q = 64
SLOTS = 6
ROWS = 8
COLS = 16
CELLS = 32
LANES = 128
FORWARD = NF + 8
HALF = NF // 2
EXTRA = 3 * HALF
IDS = EXTRA + SLOTS
DOSES = IDS + 4
PACKET = EXTRA + 16
WINDOW = 4 * 6
NEAR = 6
FAR = 8
MOST = NEAR + FAR
REST = MOST * HALF // 2
OUTGOING = REST + 16
STARTS, SEATS, PLACES = 0, COLS, COLS + ROWS * NEAR
STACK = Q + 2 * REACH
SPLIT = TILE - 2 * REACH
BF16 = jnp.bfloat16
F32 = jnp.float32


def split(table):
    high = table.astype(ml_dtypes.bfloat16)
    low = (table - high.astype(np.float64)).astype(ml_dtypes.bfloat16)
    return high, low


@functools.lru_cache(maxsize=None)
def tables():
    freq = np.arange(NF) - NF // 2
    pixels = np.arange(TILE)
    points = np.arange(Q)
    turn = np.mod(freq[:, None] * pixels[None, :], TILE) * (2.0 * np.pi / TILE)
    forward = np.concatenate([np.cos(turn), np.sin(turn)]) / TILE
    high, low = split(forward)
    forward_cols = np.ascontiguousarray(np.concatenate([high, low]).T)
    turn = np.mod(freq[: HALF + 1, None] * pixels[None, :], TILE) * (2.0 * np.pi / TILE)
    forward = np.zeros((FORWARD, TILE))
    forward[:HALF] = np.cos(turn[:HALF])
    forward[HALF:NF] = -np.sin(turn[:HALF])
    forward[NF] = np.cos(turn[HALF])
    forward_rows = np.concatenate(split(forward / TILE))

    turn = np.mod(points[:, None] * freq[None, :], Q) * (2.0 * np.pi / Q)
    cos, sin = np.cos(turn), np.sin(turn)
    order = np.concatenate([np.arange(HALF + 1), np.arange(NF - 1, HALF, -1)])
    inverse_left = np.concatenate([cos[:, order], -sin[:, order]], axis=1)
    edges = np.concatenate([np.arange(TILE - REACH, TILE), np.arange(REACH)])
    turn = np.mod(edges[:, None] * freq[None, :], TILE) * (2.0 * np.pi / TILE)
    edge_left = np.concatenate([np.cos(turn)[:, order], -np.sin(turn)[:, order]], axis=1)
    right = np.zeros((LANES, 2 * LANES))
    for k in range(2):
        re = slice(2 * k * NF, (2 * k + 1) * NF)
        im = slice((2 * k + 1) * NF, (2 * k + 2) * NF)
        out_re = slice(k * LANES, k * LANES + Q)
        out_im = slice(k * LANES + Q, (k + 1) * LANES)
        right[re, out_re], right[re, out_im] = cos.T, sin.T
        right[im, out_re], right[im, out_im] = -sin.T, cos.T

    spread_up = np.zeros((LANES, 4 * LANES))
    spread_low = np.zeros((LANES, 4 * LANES))
    rest = np.zeros((LANES, 2 * LANES))
    for copy in range(4):
        for part in range(2):
            for b in range(NF):
                for tile in range(2):
                    lane = tile * Q + part * NF + b
                    base = tile * 2 * LANES + part * LANES + copy * NF
                    spread_up[lane, base + b] = 1.0
                    if b:
                        spread_low[lane, base + NF - b] = -1.0 if part else 1.0
                rest[part * NF + b, part * LANES + copy * NF + b] = 1.0
            for i in range(1, HALF):
                rest[Q + part * (HALF - 1) + i - 1, part * LANES + copy * NF] = 1.0
        rest[Q + 2 * (HALF - 1), copy * NF + HALF] = 1.0
    rest_mask = np.zeros((HALF, LANES), np.float32)
    rest_mask[0, :Q] = rest_mask[0, Q + 2 * (HALF - 1)] = 1.0
    for i in range(1, HALF):
        rest_mask[HALF - i, Q + i - 1] = rest_mask[HALF - i, Q + HALF - 1 + i - 1] = 1.0

    harmonic = np.arange(Q) - Q // 2
    fine = np.mod(pixels[:, None] * harmonic[None, :], TILE) * (2.0 * np.pi / TILE)
    grid = np.mod(points[:, None] * harmonic[None, :], Q) * (2.0 * np.pi / Q)
    interp = (np.cos(fine) @ np.cos(grid).T + np.sin(fine) @ np.sin(grid).T) / Q
    interp = interp.astype(ml_dtypes.bfloat16).astype(np.float64)

    offsets = np.arange(2 * REACH + 1) - REACH
    taps = np.exp(-offsets * offsets / 32.0)
    taps = taps / taps.sum()

    def blur(out_pixels, in_pixels):
        gap = out_pixels[:, None] - in_pixels[None, :]
        inside = np.abs(gap) <= REACH
        return np.where(inside, taps[np.clip(gap + REACH, 0, 2 * REACH)], 0.0)

    across = np.zeros((4 * Q, TILE))
    for n in range(3):
        across[n * Q : (n + 1) * Q] = (blur(pixels, pixels + (n - 1) * TILE) @ interp).T

    out_rows = np.arange(2 * TILE)
    down = np.zeros((2 * TILE, 2 * STACK))
    down[:, :Q] = blur(out_rows, pixels) @ interp
    down[:, Q : Q + REACH] = blur(out_rows, np.arange(-REACH, 0))
    down[:, STACK : STACK + Q] = blur(out_rows, pixels + TILE) @ interp
    down[:, STACK + Q : STACK + Q + REACH] = blur(out_rows, 2 * TILE + np.arange(REACH))
    assert not down[:SPLIT, STACK:].any()

    bf16 = dict(
        forward_rows=forward_rows,
        forward_cols=forward_cols,
        inverse_left=inverse_left,
        edge_left=edge_left,
        inverse_right=right,
        spread_up=spread_up,
        spread_low=spread_low,
        rest=rest,
        across=across,
        down_upper=4.0 * down[:SPLIT, :STACK],
        down_lower=4.0 * down[SPLIT:],
    )
    out = {name: value.astype(ml_dtypes.bfloat16) for name, value in bf16.items()}
    out["rest_mask"] = rest_mask
    return out


def dot(a, b):
    return jnp.dot(a, b, preferred_element_type=F32)


def halves(x):
    high = x.astype(BF16)
    return high, (x - high.astype(F32)).astype(BF16)


def lanes_of(shape):
    return lax.broadcasted_iota(jnp.int32, shape, 1)


def seats(cells, chosen, dest, row):
    count = jnp.int32(0)
    for cell in cells:
        chosen[dest * 16 + count] = cell & (CELLS - 1)
        count = count + ((cell >> 5) == row).astype(jnp.int32)
    return count


def sources(cells, place, at, taken, first):
    for n in range(ROWS + 1):
        taken[n] = jnp.int32(first)
    for n, cell in enumerate(cells):
        source = cell >> 5
        rank = taken[source + 1]
        taken[source + 1] = rank + 1
        place[at + n] = jnp.where(cell >= 0, source * 16 + rank, -1)


def rows_of(dest):
    return [i for i in range(2 * dest - 1, 2 * dest + 3) if 0 <= i < 2 * ROWS]


def window_rows(ids_s, columns):
    cells = []
    for i in range(4):
        tile_row = 2 * lax.axis_index("rows") - 1 + i
        inside = (tile_row >= 0) & (tile_row < 2 * ROWS)
        tile_row = jnp.clip(tile_row, 0, 2 * ROWS - 1)
        cells += [jnp.where(inside, ids_s[j, tile_row], -1) for j in columns]
    return cells


def near_table(ids_s, counts_s, table, chosen, taken):
    row = lax.axis_index("rows")
    start = jnp.int32(0)
    for c in range(COLS):
        table[STARTS + c] = start
        start = start + counts_s[row, c]
    for dest in range(ROWS):
        cells = [ids_s[j, i] for i in rows_of(dest) for j in range(4)]
        count = seats(cells, chosen, dest, row)
        for n in range(NEAR):
            cell = jnp.where(n < count, chosen[dest * 16 + n], CELLS)
            table[SEATS + dest * NEAR + n] = cell
    sources(window_rows(ids_s, range(4)), table, PLACES, taken, 0)


def spectra_kernel(
    mask, ids, dose, fwd_cols, fwd_rows, kernels, weights, counts, threshold,
    out, ker, table, threshold_s,
    mask_v, ids_v, dose_v, cols_v, rows_v, kernels_v, weights_s, counts_s,
    ids_s, chosen, taken, extra, sems,
):
    moves = [(ids, ids_s), (counts, counts_s), (fwd_rows, rows_v)]
    moves += [(mask.at[s], mask_v.at[s]) for s in range(SLOTS)]
    moves += [(kernels, kernels_v), (weights, weights_s), (fwd_cols, cols_v)]
    moves += [(ids, ids_v), (dose, dose_v)]
    copies = [
        pltpu.make_async_copy(src, dst, sems.at[i]) for i, (src, dst) in enumerate(moves)
    ]
    for copy in copies:
        copy.start()
    threshold_s[0] = threshold[0]
    for copy in copies[:2]:
        copy.wait()
    near_table(ids_s, counts_s, table, chosen, taken)
    for copy in copies[2:6]:
        copy.wait()

    pairs = []
    for slot in range(SLOTS):
        if slot == 3:
            for copy in copies[6:]:
                copy.wait()
            for two in range(NK // 2):
                re, im = [], []
                for k in (2 * two, 2 * two + 1):
                    scale = jnp.sqrt(jnp.full((NF, NF), weights_s[k], F32))
                    re.append(kernels_v[0, k] * scale)
                    im.append(kernels_v[1, k] * scale)
                for part, four in enumerate(
                    ([re[0], im[0], re[1], im[1]], [-im[0], re[0], -im[1], re[1]])
                ):
                    block = jnp.concatenate(four, axis=1)
                    turned = [block[n : n + 1] for n in range(NF - 1, HALF, -1)]
                    ker[part, two] = jnp.concatenate([block[: HALF + 1], *turned], axis=0)
        cols = dot(rows_v[...], mask_v[slot])
        cols = cols[:FORWARD] + cols[FORWARD:]
        high = cols.astype(BF16).astype(F32)
        pairs.append(jnp.concatenate([high, cols - high], axis=0).astype(BF16))

    lane = lanes_of((HALF, LANES))
    line = lax.broadcasted_iota(jnp.int32, (HALF, LANES), 0)
    even = (lane // NF) % 2 == 0
    in_re = (lane == Q + HALF - 1 - line) & (line > 0)
    in_im = (lane == Q + 2 * (HALF - 1) - line) & (line > 0)
    lane1 = lanes_of((1, LANES))
    blocks, rows = [], []
    for slot in range(SLOTS):
        both = dot(pairs[slot], cols_v[...])
        both = both[:FORWARD] + both[FORWARD:]
        both = both + pltpu.roll(both, Q, 1)
        cos, sin, zero = both[:HALF], both[HALF:NF], both[NF : NF + 1]
        cos_sin, sin_sin = pltpu.roll(cos, NF, 1), pltpu.roll(sin, NF, 1)
        real = cos + sin_sin
        imag = sin - cos_sin
        blocks.append(jnp.where(even, real, pltpu.roll(imag, NF, 1)))
        first = jnp.broadcast_to((cos - sin_sin)[:, 0:1], (HALF, LANES))
        second = jnp.broadcast_to(-(sin + cos_sin)[:, 0:1], (HALF, LANES))
        turned = jnp.where(in_re, first, 0.0) + jnp.where(in_im, second, 0.0)
        turned = jnp.sum(turned, axis=0, keepdims=True)
        mean = zero[:, HALF : HALF + 1]
        mean = jnp.broadcast_to(mean - mean.astype(BF16).astype(F32), (1, LANES))
        turned = jnp.where(lane1 == Q + 2 * (HALF - 1), mean, turned)
        rows.append(jnp.where(lane1 < NF, zero, jnp.where(lane1 < Q, -zero, turned)))
    half = lanes_of((HALF, LANES)) < Q
    packed = [
        jnp.where(half, blocks[2 * i], blocks[2 * i + 1]).astype(BF16)
        for i in range(SLOTS // 2)
    ]
    extra[...] = jnp.zeros_like(extra)
    for slot in range(SLOTS):
        extra[slot : slot + 1, :] = rows[slot]
    extra[IDS - EXTRA : IDS - EXTRA + 4, 0:16] = ids_v[...].astype(F32)
    at = slice(DOSES - EXTRA, DOSES - EXTRA + 2)
    high = dose_v[...].astype(BF16).astype(F32)
    middle = (dose_v[...] - high).astype(BF16).astype(F32)
    extra[at, 4:8] = high
    extra[at, 8:12] = middle
    extra[at, 12:16] = dose_v[...] - high - middle
    packed.append(extra[...].astype(BF16))
    for c in range(COLS):
        for i in range(4):
            out[c, i * HALF : (i + 1) * HALF, :] = packed[i]


def routing_kernel(
    packets, table,
    out, place,
    held, rests, buffer, chosen, taken,
):
    row, col = lax.axis_index("rows"), lax.axis_index("cols")
    def rest_of(c):
        return packets[c, EXTRA : EXTRA + 16, :].astype(F32)

    before = rest_of(jnp.maximum(col - 1, 0))
    after = rest_of(jnp.minimum(col + 1, COLS - 1))
    line = lax.broadcasted_iota(jnp.int32, (16, LANES), 0)
    first = IDS - EXTRA
    window = jnp.where(
        line == 0, pltpu.roll(before, 16 - first - 3, 0), pltpu.roll(after, 16 - first + 1, 0)
    ).astype(jnp.int32)
    exists = ((line == 0) & (col > 0)) | ((line == 1) & (col < COLS - 1))
    outer = jnp.where(exists, window, -1)
    shift = jnp.where(row > 0, LANES + 1 - 2 * row, 1)
    mine = pltpu.roll(outer, shift, 1)
    ids = [[outer[j, i] for i in range(2 * ROWS)] for j in range(2)]
    own = [[mine[j, i] for i in range(4)] for j in range(2)]

    here = rest_of(col)
    for c in range(COLS):
        rests[c * 16 : (c + 1) * 16, :] = rest_of(c)
    left = lanes_of((HALF, LANES)) < Q
    for c in range(COLS):
        start = table[STARTS + c]
        for s in range(SLOTS):
            pair = packets[c, (s // 2) * HALF : (s // 2 + 1) * HALF, :].astype(F32)
            moved = pltpu.roll(pair, Q, 1)
            both = jnp.where(left, moved, pair) if s % 2 else jnp.where(left, pair, moved)
            held[start + s] = both
            buffer[pl.ds(start + s, 1), :] = rests[c * 16 + s : c * 16 + s + 1, :]
    held[CELLS] = jnp.zeros((HALF, LANES), F32)
    buffer[CELLS : CELLS + 1, :] = jnp.zeros((1, LANES), F32)

    lane = lanes_of((2, LANES))
    at = slice(DOSES - EXTRA, DOSES - EXTRA + 2)
    doses = jnp.where(
        lane < 16,
        before[at],
        jnp.where(lane < 32, pltpu.roll(here[at], 16, 1), pltpu.roll(after[at], 32, 1)),
    )

    def send(dest, cells, at):
        for n in range(0, len(cells), 2):
            one, two = held[cells[n]], held[cells[n + 1]]
            rows = slice(at + n // 2 * HALF, at + (n // 2 + 1) * HALF)
            out[dest, rows, :] = jnp.where(left, one, two).astype(BF16)

    near = [
        [table[SEATS + dest * NEAR + n] for n in range(NEAR)] for dest in range(ROWS)
    ]
    for dest in range(ROWS):
        send(dest, near[dest], 0)
    cells = []
    for i in range(4):
        inside = (2 * row - 1 + i >= 0) & (2 * row - 1 + i < 2 * ROWS)
        cells += [jnp.where(inside, own[j][i], -1) for j in range(2)]
    sources(cells, place, 0, taken, NEAR)
    for dest in range(ROWS):
        cells = [ids[j][i] for i in rows_of(dest) for j in range(2)]
        count = seats(cells, chosen, dest, row)
        cells = [jnp.where(n < count, chosen[dest * 16 + n], CELLS) for n in range(FAR)]
        send(dest, cells, NEAR // 2 * HALF)
        rows = [buffer[pl.ds(cell, 1), :] for cell in near[dest] + cells]
        out[dest, REST : REST + 16, :] = jnp.concatenate(rows + [doses], axis=0).astype(BF16)


def develop_kernel(
    tiles, table, place, ker, threshold, spread_up, spread_low, rest, rest_mask,
    inv_left, edge_left, inv_right, across, down_upper, down_lower,
    out,
    after_rows, stage, sems,
):
    row = lax.axis_index("rows")
    for source in range(ROWS):
        at = slice(source * 16, (source + 1) * 16)
        after_rows[at, :] = tiles[source, REST : REST + 16, :].astype(F32)
    left = lanes_of((HALF, LANES)) < Q
    first = lax.broadcasted_iota(jnp.int32, (HALF, LANES), 0) == 0
    held, paired, rests = [], [], []
    for t in range(0, WINDOW, 2):
        both = []
        for n in (t, t + 1):
            i, j = n // 6, n % 6
            found = table[PLACES + 4 * i + j - 1] if 1 <= j < 5 else place[2 * i + j // 5]
            here = jnp.maximum(found, 0)
            rank = here & 15
            at = pl.multiple_of((rank >> 1) * HALF, HALF)
            pair = tiles[here >> 4, pl.ds(at, HALF), :].astype(F32)
            tile = jnp.where((rank & 1) == (n & 1), pair, pltpu.roll(pair, Q, 1))
            both.append(jnp.where(found >= 0, tile, 0.0))
            line = jnp.where(found >= 0, after_rows[pl.ds(here, 1), :], 0.0)
            rests.append(jnp.broadcast_to(line, (HALF, LANES)) * rest_mask[...])
        pair = jnp.where(left, both[0], both[1])
        held.append(pair.astype(BF16))
        paired.append(jnp.where(first, 0.0, pair).astype(BF16))
    held = jnp.concatenate(held, axis=0)
    paired = jnp.concatenate(paired, axis=0)
    upper = dot(held, spread_up[...])
    lower = dot(paired, spread_low[...])
    rests = dot(jnp.concatenate(rests, axis=0).astype(BF16), rest[...])

    def doses(source):
        info = after_rows[pl.ds(pl.multiple_of(source * 16, 16), 16), :][MOST:]
        return info + pltpu.roll(info, LANES - 4, 1) + pltpu.roll(info, LANES - 8, 1)

    own = doses(row)
    above = doses(jnp.maximum(row - 1, 0))
    below = doses(jnp.minimum(row + 1, ROWS - 1))

    def picture(i, j):
        whole_tile = i in (1, 2)
        m, t = 3 * i + j // 2, 6 * i + j
        a, r = slice(m * HALF, (m + 1) * HALF), slice(t * HALF, (t + 1) * HALF)
        re = slice((j % 2) * 2 * LANES, (j % 2) * 2 * LANES + LANES)
        im = slice(re.stop, re.stop + LANES)
        real = jnp.concatenate([upper[a, re], lower[a, re] + rests[r, :LANES]], axis=0)
        imag = jnp.concatenate([upper[a, im], lower[a, im] + rests[r, LANES:]], axis=0)
        prods = []
        for two in range(NK // 2):
            ka, kb = ker[0, two], ker[1, two]
            prod = jnp.concatenate([ka * real + kb * imag, ka * imag - kb * real], axis=0)
            prods.append(prod.astype(BF16))
        prod = jnp.concatenate(prods, axis=1)
        half = dot(inv_left[...] if whole_tile else edge_left[...], prod)
        if not whole_tile:
            half = half[:REACH] if i == 0 else half[REACH:]
        return jnp.concatenate(
            [half[:, n * LANES : (n + 1) * LANES] for n in range(NK // 2)], axis=0
        ).astype(BF16)

    def intensity(halfway):
        field = dot(halfway, inv_right[...])
        power = field * field
        power = power[:, :LANES] + power[:, LANES:]
        height = power.shape[0] // (NK // 2)
        total = power[:height]
        for n in range(1, NK // 2):
            total = total + power[n * height : (n + 1) * height]
        return total + pltpu.roll(total, Q, 1)

    lane_of = [7] + [20 + j for j in range(4)] + [36]
    dose_rows = [above[1:2], own[0:1], own[1:2], below[0:1]]
    left = lanes_of((STACK, LANES)) < Q

    images, halfway = {}, {}
    for group in ((0, 3, 1), (2,)):
        halfway.update({(i, j): picture(i, j) for i in group for j in range(6)})
        for i in group:
            for j in range(6):
                scale = dose_rows[i][:, lane_of[j] : lane_of[j] + 1]
                images[i, j] = intensity(halfway[i, j]) * scale

    def columns(strip, tile):
        none = jnp.zeros((REACH, LANES), F32)
        stack = [
            jnp.concatenate([images[tile, j], images[strip, j], none], axis=0) for j in range(6)
        ]
        wide = []
        for j in range(1, 5):
            two = jnp.where(left, stack[j - 1], stack[j])
            three = jnp.concatenate([two, stack[j + 1]], axis=1).astype(BF16)
            wide.append(dot(three, across[...]).astype(BF16))
        return jnp.concatenate(wide, axis=1)

    shift = 4.0 * threshold[0]
    copies = []

    def finish(start, stop, level):
        rows = slice(start, stop)
        stage[rows, :] = (0.5 * jnp.tanh(level - shift) + 0.5).astype(BF16)
        copy = pltpu.make_async_copy(stage.at[rows, :], out.at[rows, :], sems.at[len(copies)])
        copy.start()
        copies.append(copy)

    upper_rows = columns(0, 1)
    finish(0, SPLIT, dot(down_upper[...], upper_rows))
    both_rows = jnp.concatenate([upper_rows, columns(3, 2)], axis=0)
    middle = SPLIT + 192
    finish(SPLIT, middle, dot(down_lower[: middle - SPLIT, :], both_rows))
    finish(middle, 2 * TILE, dot(down_lower[middle - SPLIT :, :], both_rows))
    for copy in copies:
        copy.wait()


PARAMS = pltpu.CompilerParams(vmem_limit_bytes=48 * 1024 * 1024)
IN_HBM = pl.BlockSpec(memory_space=pltpu.HBM)
IN_VMEM = pl.BlockSpec(memory_space=pltpu.VMEM)
IN_SMEM = pl.BlockSpec(memory_space=pltpu.SMEM)


def spectra(masks, cell_ids, dose, kernels, kernel_weights, owned_counts, threshold):
    table = tables()
    operands = [masks, cell_ids.T, dose]
    operands += [jnp.asarray(table[n]) for n in ("forward_cols", "forward_rows")]
    operands += [kernels, kernel_weights, owned_counts, threshold]
    in_hbm = [pltpu.with_memory_space_constraint(op, pltpu.HBM) for op in operands[:-1]]
    in_hbm.append(operands[-1])
    return pl.pallas_call(
        spectra_kernel,
        out_shape=(
            jax.ShapeDtypeStruct((COLS, PACKET, LANES), BF16),
            jax.ShapeDtypeStruct((2, NK // 2, NF, LANES), F32),
            pltpu.SMEM((PLACES + 16,), jnp.int32),
            pltpu.SMEM((1,), F32),
        ),
        in_specs=[IN_HBM] * (len(operands) - 1) + [IN_SMEM],
        out_specs=(IN_VMEM, IN_VMEM, IN_SMEM, IN_SMEM),
        scratch_shapes=[
            *[pltpu.VMEM(op.shape, op.dtype) for op in operands[:-3]],
            *[pltpu.SMEM(op.shape, op.dtype) for op in operands[-3:-1]],
            pltpu.SMEM((4, 2 * ROWS), jnp.int32),
            pltpu.SMEM((ROWS * 16 + 16,), jnp.int32),
            pltpu.SMEM((16,), jnp.int32),
            pltpu.VMEM((16, LANES), F32),
            pltpu.SemaphoreType.DMA((len(operands) + SLOTS - 1,)),
        ],
        compiler_params=PARAMS,
    )(*in_hbm)


def route(packets, seating):
    return pl.pallas_call(
        routing_kernel,
        out_shape=(
            jax.ShapeDtypeStruct((ROWS, OUTGOING, LANES), BF16),
            pltpu.SMEM((8,), jnp.int32),
        ),
        in_specs=[IN_VMEM, IN_SMEM],
        out_specs=(IN_VMEM, IN_SMEM),
        scratch_shapes=[
            pltpu.VMEM((CELLS + SLOTS, HALF, LANES), F32),
            pltpu.VMEM((COLS * 16, LANES), F32),
            pltpu.VMEM((CELLS + 8, LANES), F32),
            pltpu.SMEM((ROWS * 16 + 16,), jnp.int32),
            pltpu.SMEM((16,), jnp.int32),
        ],
        compiler_params=PARAMS,
    )(packets, seating)


def develop(incoming, seating, place, ker, threshold):
    table = tables()
    names = ("spread_up", "spread_low", "rest", "rest_mask")
    names += ("inverse_left", "edge_left", "inverse_right", "across", "down_upper", "down_lower")
    constants = [jnp.asarray(table[n]) for n in names]
    return pl.pallas_call(
        develop_kernel,
        out_shape=jax.ShapeDtypeStruct((2 * TILE, 4 * TILE), BF16),
        in_specs=[IN_VMEM, IN_SMEM, IN_SMEM, IN_VMEM, IN_SMEM, *[IN_VMEM] * len(constants)],
        out_specs=IN_HBM,
        scratch_shapes=[
            pltpu.VMEM((ROWS * 16, LANES), F32),
            pltpu.VMEM((2 * TILE, 4 * TILE), BF16),
            pltpu.SemaphoreType.DMA((3,)),
        ],
        compiler_params=PARAMS,
    )(incoming, seating, place, ker, threshold, *constants)


def local(masks, owned_counts, cell_ids, kernels, kernel_weights, dose, threshold):
    packet, ker, seating, threshold = spectra(
        masks, cell_ids, dose, kernels, kernel_weights, owned_counts, threshold
    )
    packets = lax.all_to_all(packet, "cols", split_axis=0, concat_axis=0, tiled=True)
    outgoing, place = route(packets, seating)
    incoming = lax.all_to_all(outgoing, "rows", split_axis=0, concat_axis=0, tiled=True)
    return develop(incoming, seating, place, ker, threshold)


def solution(mesh):
    return jax.shard_map(
        local,
        mesh=mesh,
        in_specs=(
            P(("rows", "cols"), None, None),
            P(),
            P(None, "cols"),
            P(),
            P(),
            P("rows", "cols"),
            P(),
        ),
        out_specs=P("rows", "cols"),
        check_vma=False,
    )
```
